32 devices in a mesh: gx: 4 (over y, x), gy: 8 (over z, core).
Axes of the slice: x: 2, y: 2, z: 4, core: 2. Of those that a mesh axis runs over, the one named last changes fastest.
Arguments:
- tokens: bfloat16 [65536, 768], P(('gx', 'gy')), may hold values from -6 to 6
- segment_ids: int32 [128, 512], P(('gx', 'gy')), may hold values from 0 to 7, never falling along the last dimension, each value on 1 to 128 neighbouring positions
- pad_counts: int32 [128], P(('gx', 'gy')), may hold values from 0 to 64
- out_cotangent: bfloat16 [65536, 768], P(('gx', 'gy')), may hold values from -6 to 6
- qkv_master: float32 [768, 2304], P(('gx', 'gy')), may hold values from -0.21875 to 0.21875
- proj_master: float32 [768, 768], P(('gx', 'gy')), may hold values from -0.875 to 0.875
- up_master: float32 [768, 3072], P(('gx', 'gy')), may hold values from -0.21875 to 0.21875
- down_master: float32 [3072, 768], P(('gx', 'gy')), may hold values from -0.109375 to 0.109375
- gain_master: float32 [1536], P(('gx', 'gy')), may hold values from 0.5 to 1.5
- bias_master: float32 [7680], P(('gx', 'gy')), may hold values from -1.8 to 1.8
- qkv_moment: float32 [768, 2304], P(('gx', 'gy')), may hold values from -0.0234375 to 0.0234375
- proj_moment: float32 [768, 768], P(('gx', 'gy')), may hold values from -0.0234375 to 0.0234375
- up_moment: float32 [768, 3072], P(('gx', 'gy')), may hold values from -0.0234375 to 0.0234375
- down_moment: float32 [3072, 768], P(('gx', 'gy')), may hold values from -0.0234375 to 0.0234375
- gain_moment: float32 [1536], P(('gx', 'gy')), may hold values from -0.0234375 to 0.0234375
- bias_moment: float32 [7680], P(('gx', 'gy')), may hold values from -0.0234375 to 0.0234375
- qkv_average: float32 [768, 2304], P(('gx', 'gy')), may hold values from -0.21875 to 0.21875
- proj_average: float32 [768, 768], P(('gx', 'gy')), may hold values from -0.875 to 0.875
- up_average: float32 [768, 3072], P(('gx', 'gy')), may hold values from -0.21875 to 0.21875
- down_average: float32 [3072, 768], P(('gx', 'gy')), may hold values from -0.109375 to 0.109375
- gain_average: float32 [1536], P(('gx', 'gy')), may hold values from 0.5 to 1.5
- bias_average: float32 [7680], P(('gx', 'gy')), may hold values from -1.8 to 1.8
Outputs:
- layer_output: bfloat16 [65536, 768], P(('gx', 'gy'))
- input_grad: float32 [65536, 768], P(('gx', 'gy'))
- qkv_grad: float32 [768, 2304], P(('gx', 'gy'))
- proj_grad: float32 [768, 768], P(('gx', 'gy'))
- up_grad: float32 [768, 3072], P(('gx', 'gy'))
- down_grad: float32 [3072, 768], P(('gx', 'gy'))
- gain_grad: float32 [1536], P(('gx', 'gy'))
- bias_grad: float32 [7680], P(('gx', 'gy'))
- qkv_master_new: float32 [768, 2304], P(('gx', 'gy'))
- proj_master_new: float32 [768, 768], P(('gx', 'gy'))
- up_master_new: float32 [768, 3072], P(('gx', 'gy'))
- down_master_new: float32 [3072, 768], P(('gx', 'gy'))
- gain_master_step: float32 [1536], P(('gx', 'gy'))
- bias_master_new: float32 [7680], P(('gx', 'gy'))
- qkv_moment_new: float32 [768, 2304], P(('gx', 'gy'))
- proj_moment_new: float32 [768, 768], P(('gx', 'gy'))
- up_moment_new: float32 [768, 3072], P(('gx', 'gy'))
- down_moment_new: float32 [3072, 768], P(('gx', 'gy'))
- gain_moment_new: float32 [1536], P(('gx', 'gy'))
- bias_moment_new: float32 [7680], P(('gx', 'gy'))
- qkv_average_new: float32 [768, 2304], P(('gx', 'gy'))
- proj_average_new: float32 [768, 768], P(('gx', 'gy'))
- up_average_new: float32 [768, 3072], P(('gx', 'gy'))
- down_average_new: float32 [3072, 768], P(('gx', 'gy'))
- gain_average_step: float32 [1536], P(('gx', 'gy'))
- bias_average_new: float32 [7680], P(('gx', 'gy'))
The draws below stay inside these ranges and needn't reach their ends.
Inputs may be any that keep to these rules, and one draw needn't show every extreme that they name: `segment_ids`: within each row of 512 tokens the pair numbers never fall, and each pair has 1 to 128 tokens. The last pad_counts[r] tokens of row r are padding.
All inputs are finite; a program needn't handle non-finite values.
Results may differ from the reference program's by a relative error of at most 0.013.
The reference program's roundings to bfloat16 on the way count: a program that leaves them out, or rounds other values in their place, can miss the bound.
Values may be sent and summed in bfloat16 or wider, within the bound.
A program may use at most 320 MiB of HBM per device.

```python
import math
import jax
import jax.numpy as jnp
import numpy as np
from jax import lax

D = 768
HEADS = 12
HEAD_DIM = 64
FF = 3072
SEQ = 512
DOCS = 8
DOC_MOST = 128
PAD_MOST = 64
ROWS = 128
TOKENS = 65536
GAIN_LEN = 1536
BIAS_LEN = 7680


def touch_ends(entries, own_key, least, largest):
    index_at = [jax.random.randint(jax.random.fold_in(own_key, axis), (), 0, length) for axis, length in enumerate(entries.shape)]
    main_axis = entries.shape.index(max(entries.shape))
    beside = index_at[:main_axis] + [(index_at[main_axis] + 1) % entries.shape[main_axis]] + index_at[main_axis + 1:]
    return entries.at[tuple(index_at)].set(least).at[tuple(beside)].set(largest)


def levels(key, dims, cuts, smallest, largest):
    def one(dim, blocks):
        steps = jax.random.uniform(jax.random.fold_in(jax.random.fold_in(key, 6), dim), (blocks,), jnp.float32, smallest / len(cuts), largest / len(cuts))
        return jnp.repeat(jnp.exp(steps), dims[dim] // blocks).reshape((-1,) + (1,) * (len(dims) - dim - 1))

    level = one(*cuts[0])
    for cut in cuts[1:]:
        level = level * one(*cut)
    return level


def length_profile(amount, total, most, lean):
    portions = [(1 << 20) // math.isqrt(grade ** lean) + 1 for grade in range(2, amount + 1)]
    surplus, holding = total - most - (amount - 1), [1] * (amount - 1)
    while surplus > 0:
        free = [i for i in range(amount - 1) if holding[i] < most]
        pool, remaining = sum([portions[i] for i in free]), surplus
        for i in free:
            extra = min(most - holding[i], max(1, remaining * portions[i] // pool), surplus)
            holding[i] = holding[i] + extra
            surplus = surplus - extra
    return np.array([most] + holding)


def uneven(rng, amount, total, most, slope):
    if amount == 2:
        one = jax.random.randint(rng, (), max(1, total - most), min(most, total - 1) + 1)
        return jnp.stack([one, total - one])
    tallies = jnp.asarray(length_profile(amount, total, most, slope), jnp.int32)
    couples = (amount - 1) // 2
    donor, sink = tallies[1:1 + 2 * couples:2], tallies[2:2 + 2 * couples:2]
    room = jnp.minimum(donor - 1, most - sink)
    passed = jax.random.randint(jax.random.fold_in(rng, 1), (couples,), 0, 1 << 20) % (room + 1)
    tallies = tallies.at[1:1 + 2 * couples:2].set(donor - passed).at[2:2 + 2 * couples:2].set(sink + passed)
    return tallies[jax.random.permutation(jax.random.fold_in(rng, 2), amount)]


def scatter_about(rng, shape, width, most, cuts=(), kind=jnp.bfloat16):
    drawn = jax.random.normal(rng, shape, jnp.float32) * width
    if len(cuts) > 0:
        drawn = levels(rng, shape, cuts, -0.22, 0.18) * drawn
    return jnp.clip(drawn, min=-most, max=most).astype(kind)


def setup_inputs(seed: int = 0) -> dict:
    key_of = jax.random.split(jax.random.key(seed), 23)
    tokens = scatter_about(key_of[0], (TOKENS, D), 1.0, 6.0, ((0, 32),))
    segment_ids = jax.vmap(lambda own: jnp.searchsorted(jnp.cumsum(uneven(own, DOCS, SEQ, DOC_MOST, 1)), jnp.arange(SEQ), side="right"))(jax.random.split(key_of[1], ROWS)).reshape((ROWS, SEQ)).astype(jnp.int32)
    pad_counts = touch_ends(jax.random.randint(key_of[2], (ROWS,), 0, PAD_MOST + 1), jax.random.fold_in(key_of[2], 1), 0, PAD_MOST).astype(jnp.int32)
    out_cotangent = scatter_about(key_of[3], (TOKENS, D), 1.0, 6.0, ((0, 32),))
    qkv_master = scatter_about(key_of[4], (D, 3 * D), D ** -0.5, 0.21875, ((0, 32),), jnp.float32)
    proj_master = scatter_about(key_of[5], (D, D), (D // 16) ** -0.5, 0.875, ((0, 32),), jnp.float32)
    up_master = scatter_about(key_of[6], (D, FF), D ** -0.5, 0.21875, ((0, 32),), jnp.float32)
    down_master = scatter_about(key_of[7], (FF, D), FF ** -0.5, 0.109375, ((0, 32),), jnp.float32)
    gain_master = jnp.clip(1.0 + 0.1 * jax.random.normal(key_of[8], (GAIN_LEN,), jnp.float32), 0.5, 1.5)
    bias_master = scatter_about(key_of[9], (BIAS_LEN,), 0.3, 1.8, ((0, 32),), jnp.float32)
    qkv_moment = scatter_about(key_of[10], (D, 3 * D), (TOKENS ** -0.5), 0.0234375, ((0, 32),), jnp.float32)
    proj_moment = scatter_about(key_of[11], (D, D), (TOKENS ** -0.5), 0.0234375, ((0, 32),), jnp.float32)
    up_moment = scatter_about(key_of[12], (D, FF), (TOKENS ** -0.5), 0.0234375, ((0, 32),), jnp.float32)
    down_moment = scatter_about(key_of[13], (FF, D), (TOKENS ** -0.5), 0.0234375, ((0, 32),), jnp.float32)
    gain_moment = scatter_about(key_of[14], (GAIN_LEN,), (TOKENS ** -0.5), 0.0234375, ((0, 32),), jnp.float32)
    bias_moment = scatter_about(key_of[15], (BIAS_LEN,), (TOKENS ** -0.5), 0.0234375, ((0, 32),), jnp.float32)
    qkv_average = scatter_about(key_of[16], (D, 3 * D), D ** -0.5, 0.21875, ((0, 32),), jnp.float32)
    proj_average = scatter_about(key_of[17], (D, D), (D // 16) ** -0.5, 0.875, ((0, 32),), jnp.float32)
    up_average = scatter_about(key_of[18], (D, FF), D ** -0.5, 0.21875, ((0, 32),), jnp.float32)
    down_average = scatter_about(key_of[19], (FF, D), FF ** -0.5, 0.109375, ((0, 32),), jnp.float32)
    gain_average = jnp.clip(1.0 + 0.1 * jax.random.normal(key_of[20], (GAIN_LEN,), jnp.float32), 0.5, 1.5)
    bias_average = scatter_about(key_of[21], (BIAS_LEN,), 0.3, 1.8, ((0, 32),), jnp.float32)
    return dict(tokens=tokens, segment_ids=segment_ids, pad_counts=pad_counts, out_cotangent=out_cotangent, qkv_master=qkv_master, proj_master=proj_master, up_master=up_master, down_master=down_master, gain_master=gain_master, bias_master=bias_master, qkv_moment=qkv_moment, proj_moment=proj_moment, up_moment=up_moment, down_moment=down_moment, gain_moment=gain_moment, bias_moment=bias_moment, qkv_average=qkv_average, proj_average=proj_average, up_average=up_average, down_average=down_average, gain_average=gain_average, bias_average=bias_average)


@jax.custom_vjp
def low(v):
    return lax.optimization_barrier(v.astype(jnp.bfloat16)).astype(jnp.float32)

@jax.custom_vjp
def low_back(v):
    return v

def low_keep(v):
    return (low(v), None)

def low_pass(kept, grad):
    return (grad,)

def back_keep(v):
    return (v, None)

def back_low(kept, grad):
    return (low(grad),)
low.defvjp(low_keep, low_pass)
low_back.defvjp(back_keep, back_low)
norm_eps = 1e-06
momentum_coef = 0.9
learn_rate = 4.0
average_keep = 0.9
highest = lax.Precision.HIGHEST

def matmul_high(left, right):
    return jnp.dot(left, right, precision=highest, preferred_element_type=jnp.float32)

def layer_norm(values, gain, shift):
    centre = lax.optimization_barrier(jnp.mean(values, axis=-1, keepdims=True))
    centred = values - centre
    spread = lax.optimization_barrier(jnp.mean(centred * centred, axis=-1, keepdims=True))
    return centred * lax.rsqrt(spread + norm_eps) * gain + shift

def group_forward(params, inputs, segments, padding):
    w_qkv, w_out, w_up, w_down, gain_all, bias_all = params
    row_count = segments.shape[0]
    bias_q = bias_all[0:D]
    bias_v = bias_all[D:2 * D]
    bias_o = bias_all[2 * D:3 * D]
    shift_one = bias_all[3 * D:4 * D]
    bias_up = bias_all[4 * D:4 * D + FF]
    bias_down = bias_all[4 * D + FF:5 * D + FF]
    shift_two = bias_all[5 * D + FF:6 * D + FF]
    gain_one = gain_all[0:D]
    gain_two = gain_all[D:2 * D]
    key_zeros = jnp.zeros((D,), jnp.float32)
    projected = matmul_high(inputs, w_qkv) + jnp.concatenate([bias_q, key_zeros, bias_v])
    projected = low(low_back(projected))
    queries = projected[:, 0:D].reshape(row_count, SEQ, HEADS, HEAD_DIM)
    key_heads = projected[:, D:2 * D].reshape(row_count, SEQ, HEADS, HEAD_DIM)
    value_heads = projected[:, 2 * D:3 * D].reshape(row_count, SEQ, HEADS, HEAD_DIM)
    score_scale = HEAD_DIM ** (-0.5)
    scores = low_back(score_scale * jnp.einsum('rqhd,rkhd->rhqk', queries, key_heads, precision=highest))
    position = jnp.arange(SEQ, dtype=jnp.int32)
    is_pad = position[None, :] >= (SEQ - padding.astype(jnp.int32))[:, None]
    allowed = (segments[:, :, None] == segments[:, None, :]) & (is_pad[:, :, None] == is_pad[:, None, :])
    masked = jnp.where(allowed[:, None, :, :], scores, -1e+30)
    probs = low(jax.nn.softmax(masked, axis=-1))
    context = jnp.einsum('rhqk,rkhd->rqhd', probs, value_heads, precision=highest).reshape(row_count * SEQ, D)
    context = low(low_back(context))
    branch = low_back(matmul_high(context, w_out) + bias_o)
    normed = layer_norm(inputs + branch, gain_one, shift_one)
    hidden = low_back(matmul_high(low(normed), w_up) + bias_up)
    activated = low(jax.nn.gelu(hidden, approximate=False))
    mixed = low_back(matmul_high(activated, w_down) + bias_down)
    return layer_norm(normed + mixed, gain_two, shift_two)

def forward(params, inputs, segment_ids, pad_counts):
    group_rows = math.gcd(ROWS, 8)
    batches = ROWS // group_rows
    stacked = (inputs.reshape(batches, group_rows * SEQ, D), segment_ids.reshape(batches, group_rows, SEQ), pad_counts.reshape(batches, group_rows))

    def one_group(element):
        return group_forward(params, element[0], element[1], element[2])
    outputs = lax.map(jax.checkpoint(one_group), stacked)
    return outputs.reshape(ROWS * SEQ, D)

def update(grad, master, moment, average):
    mean_grad = grad / TOKENS
    moment_new = momentum_coef * moment + mean_grad
    step_size = -learn_rate * (mean_grad + momentum_coef * moment_new)
    master_new = master + step_size
    average_new = average_keep * average + (1.0 - average_keep) * master_new
    return (master_new, moment_new, average_new)

def update_steps(grad, master, moment, average):
    mean_grad = grad / TOKENS
    moment_new = momentum_coef * moment + mean_grad
    step_size = -learn_rate * (mean_grad + momentum_coef * moment_new)
    average_step = (1.0 - average_keep) * (master + step_size - average)
    return (step_size, moment_new, average_step)

def reference(tokens, segment_ids, pad_counts, out_cotangent, qkv_master, proj_master, up_master, down_master, gain_master, bias_master, qkv_moment, proj_moment, up_moment, down_moment, gain_moment, bias_moment, qkv_average, proj_average, up_average, down_average, gain_average, bias_average):
    params = (low(qkv_master), low(proj_master), low(up_master), low(down_master), low(gain_master), low(bias_master))
    inputs = tokens.astype(jnp.float32)

    def whole(weights, values):
        return forward(weights, values, segment_ids, pad_counts)
    output, pullback = jax.vjp(whole, params, inputs)
    grads, input_grad = pullback(out_cotangent.astype(jnp.float32))
    qkv_grad, proj_grad, up_grad, down_grad, gain_grad, bias_grad = grads
    qkv_new = update(qkv_grad, qkv_master, qkv_moment, qkv_average)
    proj_new = update(proj_grad, proj_master, proj_moment, proj_average)
    up_new = update(up_grad, up_master, up_moment, up_average)
    down_new = update(down_grad, down_master, down_moment, down_average)
    gain_new = update_steps(gain_grad, gain_master, gain_moment, gain_average)
    bias_new = update(bias_grad, bias_master, bias_moment, bias_average)
    return (output.astype(jnp.bfloat16), input_grad, qkv_grad, proj_grad, up_grad, down_grad, gain_grad, bias_grad, qkv_new[0], proj_new[0], up_new[0], down_new[0], gain_new[0], bias_new[0], qkv_new[1], proj_new[1], up_new[1], down_new[1], gain_new[1], bias_new[1], qkv_new[2], proj_new[2], up_new[2], down_new[2], gain_new[2], bias_new[2])
```

```python
from functools import partial

import jax
import jax.numpy as jnp
from jax import lax
from jax.experimental import pallas as pl
from jax.experimental.pallas import tpu as pltpu
from jax.sharding import PartitionSpec as P

D = 768
HEADS = 12
HEAD_DIM = 64
FF = 3072
SEQ = 512
BAND = 128
PACK = 4
GROUPS = HEADS // PACK
WIDE = PACK * HEAD_DIM
VMEM = 60 * 1024 * 1024

norm_eps = 1e-06
momentum_coef = 0.9
learn_rate = 4.0
average_keep = 0.9

G1, G2, BQ, BV, BO, C1, B1, B2, C2 = (
    0, 768, 1536, 2304, 3072, 3840, 4608, 7680, 8448,
)
VEC = 9216

f32 = jnp.float32
bf16 = jnp.bfloat16

LOG2E = 1.4426950408889634
SCORE = HEAD_DIM ** (-0.5) * LOG2E


def nn(a, b):
    return lax.dot_general(a, b, (((1,), (0,)), ((), ())), preferred_element_type=f32)


def nt(a, b):
    return lax.dot_general(a, b, (((1,), (1,)), ((), ())), preferred_element_type=f32)


def tn(a, b):
    return lax.dot_general(a, b, (((0,), (0,)), ((), ())), preferred_element_type=f32)


def normal_cdf(u):
    t = 1.0 / (1.0 + 0.28 * jnp.abs(u))
    gauss = jnp.exp2(u * u * (-0.5 * LOG2E))
    q = -0.10568755
    for k in (0.38938334, -0.23620046, 0.26827342, 0.0677507, 0.11648054):
        q = q * t + k
    tail = q * t * gauss
    return jnp.where(u >= 0, 1.0 - tail, tail), gauss


def windows():
    for b in range(SEQ // BAND):
        first = max(0, (b - 1) * BAND)
        last = min(SEQ, (b + 2) * BAND)
        yield b, first, last - first


def head_masks():
    lane = lax.broadcasted_iota(jnp.int32, (BAND, WIDE), 1) // HEAD_DIM
    return [jnp.where(lane == h, 1.0, 0.0).astype(bf16) for h in range(PACK)]


def spread_heads(block, masks):
    return jnp.concatenate([block * m for m in masks], axis=0)


def pick_heads(wide):
    return jnp.concatenate(
        [
            wide[h * HEAD_DIM : (h + 1) * HEAD_DIM, h * BAND : (h + 1) * BAND]
            for h in range(PACK)
        ],
        axis=0,
    )


def mask_bias(col, row, b, first, width):
    keys = col[first : first + width, :]
    queries = row[0:1, b * BAND : (b + 1) * BAND]
    bias = jnp.where(keys == queries, 0.0, -1e30)
    return jnp.concatenate([bias] * PACK, axis=1)


def norm_stats(y):
    centre = jnp.mean(y, axis=-1, keepdims=True)
    centred = y - centre
    spread = jnp.mean(centred * centred, axis=-1, keepdims=True)
    r = lax.rsqrt(spread + norm_eps)
    return centred * r, r


def norm_back(dz, z, r):
    return r * (
        dz
        - jnp.mean(dz, axis=-1, keepdims=True)
        - z * jnp.mean(dz * z, axis=-1, keepdims=True)
    )


def fold_rows(v):
    n = v.shape[0]
    return jnp.sum(v.reshape(n // 8, 8, v.shape[1]), axis=0)


def front_kernel(
    x_ref, row_ref, col_ref, vec_ref, wqkv_ref, wo_ref, w1_ref,
    q_ref, k_ref, v_ref, lse_ref, c_ref, y1_ref, n1_ref, g_ref, gp_ref,
    c_all,
):
    s = pl.program_id(0)

    @pl.when(s < GROUPS * 4)
    def _():
        hg = s // 4
        r = s % 4
        rows = pl.multiple_of(r * SEQ, SEQ)
        lanes = pl.multiple_of(hg * WIDE, WIDE)
        xr = x_ref[pl.ds(rows, SEQ), :]
        q = nn(xr, wqkv_ref[hg, :, 0:WIDE]) + vec_ref[0:1, pl.ds(BQ + lanes, WIDE)]
        q = q.astype(bf16)
        k = nn(xr, wqkv_ref[hg, :, WIDE : 2 * WIDE]).astype(bf16)
        v = nn(xr, wqkv_ref[hg, :, 2 * WIDE :]) + vec_ref[0:1, pl.ds(BV + lanes, WIDE)]
        v = v.astype(bf16)
        q_ref[...] = q
        k_ref[...] = k
        v_ref[...] = v
        vt = v.T
        masks = head_masks()
        for b, first, width in windows():
            qc = spread_heads(q[b * BAND : (b + 1) * BAND, :], masks)
            t = nt(k[first : first + width, :], qc) * SCORE
            t = t + mask_bias(col_ref.at[0], row_ref.at[0], b, first, width)
            m = jnp.max(t, axis=0, keepdims=True)
            e = jnp.exp2(t - m)
            l = jnp.sum(e, axis=0, keepdims=True)
            p = (e * (1.0 / l)).astype(bf16)
            lse_ref[0, b : b + 1, :] = m + jnp.log2(l)
            ot = nn(vt[:, first : first + width], p)
            c = pick_heads(ot).T.astype(bf16)
            c_all[pl.ds(rows + b * BAND, BAND), pl.ds(lanes, WIDE)] = c

    @pl.when(s >= GROUPS * 4)
    def _():
        r = s - GROUPS * 4
        rows = pl.multiple_of(r * SEQ, SEQ)
        c = c_all[pl.ds(rows, SEQ), :]
        c_ref[...] = c
        y1 = x_ref[pl.ds(rows, SEQ), :].astype(f32) + (
            nn(c, wo_ref[...]) + vec_ref[0:1, BO : BO + D]
        )
        y1_ref[...] = y1
        z1, _ = norm_stats(y1)
        n1 = (z1 * vec_ref[0:1, G1 : G1 + D] + vec_ref[0:1, C1 : C1 + D]).astype(bf16)
        n1_ref[...] = n1
        step = 768
        for f in range(0, FF, step):
            u = nn(n1, w1_ref[:, f : f + step]) + vec_ref[0:1, B1 + f : B1 + f + step]
            cdf, gauss = normal_cdf(u)
            g_ref[:, f : f + step] = (u * cdf).astype(bf16)
            gp_ref[:, f : f + step] = (cdf + u * (gauss * 0.3989422804014327)).astype(bf16)


def front(x, row_codes, col_codes, vec, wqkv, wo, w1):
    tokens = x.shape[0]
    rows = tokens // SEQ
    steps = GROUPS * rows + rows
    assert rows == 4
    att = GROUPS * rows

    def one(shape):
        return pl.BlockSpec(shape, lambda s: (0,) * len(shape), pipeline_mode=pl.Buffered(1))

    def code_at(s):
        return (jnp.where(s < att, s % rows, rows - 1), 0, 0)

    def head_at(s):
        return (jnp.where(s < att, s % rows, rows - 1), jnp.minimum(s // rows, GROUPS - 1))

    def lse_at(s):
        return (jnp.minimum(s, att - 1), 0, 0)

    def tile_at(s):
        return (jnp.maximum(s - att, 0), 0)

    return pl.pallas_call(
        front_kernel,
        grid=(steps,),
        in_specs=[
            one((tokens, D)),
            pl.BlockSpec((1, 8, SEQ), code_at),
            pl.BlockSpec((1, SEQ, BAND), code_at),
            one((1, VEC)),
            one((GROUPS, D, 3 * WIDE)),
            one((D, D)),
            one((D, FF)),
        ],
        out_specs=[
            pl.BlockSpec((SEQ, WIDE), head_at),
            pl.BlockSpec((SEQ, WIDE), head_at),
            pl.BlockSpec((SEQ, WIDE), head_at),
            pl.BlockSpec((1, 8, PACK * BAND), lse_at),
            pl.BlockSpec((SEQ, D), tile_at),
            pl.BlockSpec((SEQ, D), tile_at),
            pl.BlockSpec((SEQ, D), tile_at),
            pl.BlockSpec((SEQ, FF), tile_at),
            pl.BlockSpec((SEQ, FF), tile_at),
        ],
        out_shape=[
            jax.ShapeDtypeStruct((tokens, D), bf16),
            jax.ShapeDtypeStruct((tokens, D), bf16),
            jax.ShapeDtypeStruct((tokens, D), bf16),
            jax.ShapeDtypeStruct((att, 8, PACK * BAND), f32),
            jax.ShapeDtypeStruct((tokens, D), bf16),
            jax.ShapeDtypeStruct((tokens, D), f32),
            jax.ShapeDtypeStruct((tokens, D), bf16),
            jax.ShapeDtypeStruct((tokens, FF), bf16),
            jax.ShapeDtypeStruct((tokens, FF), bf16),
        ],
        scratch_shapes=[pltpu.VMEM((tokens, D), bf16)],
        compiler_params=pltpu.CompilerParams(vmem_limit_bytes=VMEM),
        name="front",
    )(x, row_codes, col_codes, vec, wqkv, wo, w1)


def middle_kernel(
    y1_ref, g_ref, gp_ref, cot_ref, vec_ref, wo_ref, w1_ref, w2_ref,
    out_ref, df_ref, du_ref, dy1_ref, da_ref, dc_ref, sums_ref, ups_ref,
):
    s = pl.program_id(0)

    @pl.when(s == 0)
    def _():
        sums_ref[...] = jnp.zeros_like(sums_ref)
        ups_ref[...] = jnp.zeros_like(ups_ref)

    z1, r1 = norm_stats(y1_ref[...])
    gain1 = vec_ref[0:1, G1 : G1 + D]
    gain2 = vec_ref[0:1, G2 : G2 + D]
    n1 = z1 * gain1 + vec_ref[0:1, C1 : C1 + D]
    y2 = n1 + (nn(g_ref[...], w2_ref[...]) + vec_ref[0:1, B2 : B2 + D])
    z2, r2 = norm_stats(y2)
    out_ref[...] = (z2 * gain2 + vec_ref[0:1, C2 : C2 + D]).astype(bf16)
    e = cot_ref[...].astype(f32)
    sums_ref[0] += fold_rows(e * z2)
    sums_ref[1] += fold_rows(e)
    dy2 = norm_back(e * gain2, z2, r2)
    df = dy2.astype(bf16)
    df_ref[...] = df
    sums_ref[2] += fold_rows(df.astype(f32))
    step = 768
    for f in range(0, FF, step):
        dg = nt(df, w2_ref[f : f + step, :])
        du = (dg * gp_ref[:, f : f + step].astype(f32)).astype(bf16)
        du_ref[:, f : f + step] = du
        ups_ref[:, f : f + step] += fold_rows(du.astype(f32))
    dn1 = nt(du_ref[...], w1_ref[...]) + dy2
    sums_ref[3] += fold_rows(dn1 * z1)
    sums_ref[4] += fold_rows(dn1)
    dy1 = norm_back(dn1 * gain1, z1, r1)
    dy1_ref[...] = dy1
    da = dy1.astype(bf16)
    da_ref[...] = da
    sums_ref[5] += fold_rows(da.astype(f32))
    dc_ref[...] = nt(da, wo_ref[...]).astype(bf16)


def middle(y1, g, gp, cot, vec, wo, w1, w2):
    tokens = y1.shape[0]
    tile = SEQ

    def one(shape):
        return pl.BlockSpec(shape, lambda s: (0,) * len(shape), pipeline_mode=pl.Buffered(1))

    narrow = pl.BlockSpec((tile, D), lambda s: (s, 0))
    wide = pl.BlockSpec((tile, FF), lambda s: (s, 0))
    wide_out = pl.BlockSpec((tile, FF), lambda s: (s, 0))
    return pl.pallas_call(
        middle_kernel,
        grid=(tokens // tile,),
        in_specs=[
            narrow, wide, wide, narrow, one((1, VEC)), one((D, D)), one((D, FF)), one((FF, D)),
        ],
        out_specs=[
            narrow, narrow, wide_out, narrow, narrow, narrow,
            pl.BlockSpec((6, 8, D), lambda s: (0, 0, 0)),
            pl.BlockSpec((8, FF), lambda s: (0, 0)),
        ],
        out_shape=[
            jax.ShapeDtypeStruct((tokens, D), bf16),
            jax.ShapeDtypeStruct((tokens, D), bf16),
            jax.ShapeDtypeStruct((tokens, FF), bf16),
            jax.ShapeDtypeStruct((tokens, D), f32),
            jax.ShapeDtypeStruct((tokens, D), bf16),
            jax.ShapeDtypeStruct((tokens, D), bf16),
            jax.ShapeDtypeStruct((6, 8, D), f32),
            jax.ShapeDtypeStruct((8, FF), f32),
        ],
        compiler_params=pltpu.CompilerParams(vmem_limit_bytes=VMEM),
        name="middle",
    )(y1, g, gp, cot, vec, wo, w1, w2)


def outer_kernel(a_ref, b_ref, o_ref):
    o_ref[...] = tn(a_ref[...], b_ref[...]).astype(o_ref.dtype)


def outer(a, b, dtype, side):
    tokens, m = a.shape
    n = b.shape[1]
    step = 768
    if side == 0:
        grid, a_at, b_at, o_at = m // step, (lambda i: (0, i)), (lambda i: (0, 0)), (lambda i: (i, 0))
    else:
        grid, a_at, b_at, o_at = n // step, (lambda i: (0, 0)), (lambda i: (0, i)), (lambda i: (0, i))
    return pl.pallas_call(
        outer_kernel,
        grid=(grid,),
        in_specs=[pl.BlockSpec((tokens, step), a_at), pl.BlockSpec((tokens, step), b_at)],
        out_specs=pl.BlockSpec((step, step), o_at),
        out_shape=jax.ShapeDtypeStruct((m, n), dtype),
        compiler_params=pltpu.CompilerParams(vmem_limit_bytes=VMEM),
        name="outer",
    )(a, b)


def back_kernel(
    x_ref, row_ref, col_ref, wqkv_ref, q_ref, k_ref, v_ref, dc_ref, lse_ref, dy1_ref,
    dw_ref, dx_ref, sums_ref,
    dqkv, dk_sum, dv_sum,
):
    s = pl.program_id(0)
    att = GROUPS * 4

    @pl.when(s < att)
    def _():
        hg = s // 4
        r = s % 4
        rows = pl.multiple_of(r * SEQ, SEQ)
        kt = k_ref[...].T
        dk_sum[...] = jnp.zeros_like(dk_sum)
        dv_sum[...] = jnp.zeros_like(dv_sum)
        masks = head_masks()

        @pl.when(r == 0)
        def _():
            sums_ref[...] = jnp.zeros_like(sums_ref)

        for b, first, width in windows():
            block = slice(b * BAND, (b + 1) * BAND)
            span = slice(first, first + width)
            qc = spread_heads(q_ref[block, :], masks)
            dcc = spread_heads(dc_ref[block, :], masks)
            t = nt(k_ref[span, :], qc) * SCORE
            t = t + mask_bias(col_ref.at[0], row_ref.at[0], b, first, width)
            p = jnp.exp2(t - lse_ref[0, b : b + 1, :])
            dp = nt(v_ref[span, :], dcc)
            dv_sum[span, :] += nn(p.astype(bf16), dcc)
            pdp = p * dp
            weighted = jnp.sum(pdp, axis=0, keepdims=True)
            ds = (pdp - p * weighted).astype(bf16)
            dk_sum[span, :] += nn(ds, qc)
            dqt = nn(kt[:, span], ds)
            dq = (pick_heads(dqt).T * HEAD_DIM ** (-0.5)).astype(bf16)
            dqkv[hg, pl.ds(rows + b * BAND, BAND), 0:WIDE] = dq
            sums_ref[0, 0] += fold_rows(dq.astype(f32))
        dk = (dk_sum[...] * HEAD_DIM ** (-0.5)).astype(bf16)
        dv = dv_sum[...].astype(bf16)
        dqkv[hg, pl.ds(rows, SEQ), WIDE : 2 * WIDE] = dk
        dqkv[hg, pl.ds(rows, SEQ), 2 * WIDE :] = dv
        sums_ref[0, 1] += fold_rows(dv.astype(f32))

        @pl.when(r == 3)
        def _():
            dw_ref[0] = tn(x_ref[...], dqkv[hg]).astype(dw_ref.dtype)

    @pl.when(s >= att)
    def _():
        rows = pl.multiple_of((s - att) * SEQ, SEQ)
        total = dy1_ref[...]
        for hg in range(GROUPS):
            total = total + nt(dqkv[hg, pl.ds(rows, SEQ), :], wqkv_ref[hg])
        dx_ref[...] = total


def back(x, row_codes, col_codes, wqkv, q, k, v, dc, lse, dy1, dtype):
    tokens = x.shape[0]
    rows = tokens // SEQ
    att = GROUPS * rows
    assert rows == 4

    def one(shape):
        return pl.BlockSpec(shape, lambda s: (0,) * len(shape), pipeline_mode=pl.Buffered(1))

    def code_at(s):
        return (jnp.where(s < att, s % rows, rows - 1), 0, 0)

    def head_at(s):
        return (jnp.where(s < att, s % rows, rows - 1), jnp.minimum(s // rows, GROUPS - 1))

    def group_at(s):
        return (jnp.minimum(s // rows, GROUPS - 1), 0, 0)

    def tile_at(s):
        return (jnp.maximum(s - att, 0), 0)

    head = pl.BlockSpec((SEQ, WIDE), head_at)
    return pl.pallas_call(
        back_kernel,
        grid=(att + rows,),
        in_specs=[
            one((tokens, D)),
            pl.BlockSpec((1, 8, SEQ), code_at),
            pl.BlockSpec((1, SEQ, BAND), code_at),
            one((GROUPS, D, 3 * WIDE)),
            head, head, head, head,
            pl.BlockSpec((1, 8, PACK * BAND), lambda s: (jnp.minimum(s, att - 1), 0, 0)),
            pl.BlockSpec((SEQ, D), tile_at),
        ],
        out_specs=[
            pl.BlockSpec((1, D, 3 * WIDE), group_at),
            pl.BlockSpec((SEQ, D), tile_at),
            pl.BlockSpec((1, 2, 8, WIDE), lambda s: (jnp.minimum(s // rows, GROUPS - 1), 0, 0, 0)),
        ],
        out_shape=[
            jax.ShapeDtypeStruct((GROUPS, D, 3 * WIDE), dtype),
            jax.ShapeDtypeStruct((tokens, D), f32),
            jax.ShapeDtypeStruct((GROUPS, 2, 8, WIDE), f32),
        ],
        scratch_shapes=[
            pltpu.VMEM((GROUPS, tokens, 3 * WIDE), bf16),
            pltpu.VMEM((SEQ, WIDE), f32),
            pltpu.VMEM((SEQ, WIDE), f32),
        ],
        compiler_params=pltpu.CompilerParams(vmem_limit_bytes=VMEM),
        name="back",
    )(x, row_codes, col_codes, wqkv, q, k, v, dc, lse, dy1)


def group_columns(w):
    n = w.shape[0]
    return w.reshape(n, 3, GROUPS, WIDE).transpose(2, 0, 1, 3).reshape(GROUPS, n, 3 * WIDE)


def ungroup_columns(w):
    n = w.shape[1]
    return w.reshape(GROUPS, n, 3, WIDE).transpose(1, 2, 0, 3).reshape(n, 3 * D)


def update(grad, master, moment, average, tokens_all):
    mean_grad = grad / tokens_all
    moment_new = momentum_coef * moment + mean_grad
    step_size = -learn_rate * (mean_grad + momentum_coef * moment_new)
    master_new = master + step_size
    average_new = average_keep * average + (1.0 - average_keep) * master_new
    return (master_new, moment_new, average_new)


def update_steps(grad, master, moment, average, tokens_all):
    mean_grad = grad / tokens_all
    moment_new = momentum_coef * moment + mean_grad
    step_size = -learn_rate * (mean_grad + momentum_coef * moment_new)
    average_step = (1.0 - average_keep) * (master + step_size - average)
    return (step_size, moment_new, average_step)


def on_device(
    tokens, segment_ids, pad_counts, out_cotangent,
    qkv_master, proj_master, up_master, down_master, gain_master, bias_master,
    qkv_moment, proj_moment, up_moment, down_moment, gain_moment, bias_moment,
    qkv_average, proj_average, up_average, down_average, gain_average, bias_average,
):
    axes = ("gx", "gy")
    seq_len = segment_ids.shape[1]
    tokens_all = tokens.shape[0] * lax.axis_size(axes)
    position = jnp.arange(seq_len, dtype=jnp.int32)
    is_pad = position[None, :] >= (seq_len - pad_counts)[:, None]
    codes = segment_ids * 2 + is_pad.astype(jnp.int32)
    row_codes = jnp.broadcast_to(codes[:, None, :], (codes.shape[0], 8, seq_len))
    col_codes = jnp.broadcast_to(codes[:, :, None], (codes.shape[0], seq_len, BAND))

    gather = partial(lax.all_gather, axis_name=axes, tiled=True)
    wqkv = group_columns(gather(qkv_master.astype(bf16), axis=0))
    wo = gather(proj_master.astype(bf16), axis=0)
    w1 = gather(up_master.astype(bf16), axis=0)
    w2 = gather(down_master.astype(bf16), axis=0)
    vec = jnp.concatenate(
        [gather(gain_master.astype(bf16), axis=0), gather(bias_master.astype(bf16), axis=0)]
    ).astype(f32)[None, :]

    q, k, v, lse, c, y1, n1, g, gp = front(tokens, row_codes, col_codes, vec, wqkv, wo, w1)
    layer_output, df, du, dy1, da, dc, sums, ups = middle(
        y1, g, gp, out_cotangent, vec, wo, w1, w2
    )
    dw2 = outer(g, df, f32, 0)
    dw1 = outer(n1, du, f32, 1)
    dwo = outer(c, da, f32, 0)
    dwqkv, input_grad, qv_sums = back(
        tokens, row_codes, col_codes, wqkv, q, k, v, dc, lse, dy1, f32
    )
    sums = jnp.sum(sums, axis=1)
    ups = jnp.sum(ups, axis=0)
    qv_sums = jnp.sum(qv_sums, axis=2)
    gain_terms = jnp.concatenate([sums[3], sums[0]])
    bias_terms = jnp.concatenate(
        [
            qv_sums[:, 0].reshape(D), qv_sums[:, 1].reshape(D),
            sums[5], sums[4], ups, sums[2], sums[1],
        ]
    )
    scatter = partial(lax.psum_scatter, axis_name=axes, scatter_dimension=0, tiled=True)
    qkv_share = scatter(ungroup_columns(dwqkv))
    proj_share = scatter(dwo)
    up_share = scatter(dw1)
    down_share = scatter(dw2)
    gain_share = scatter(gain_terms)
    bias_share = scatter(bias_terms)
    qkv_new = update(qkv_share, qkv_master, qkv_moment, qkv_average, tokens_all)
    proj_new = update(proj_share, proj_master, proj_moment, proj_average, tokens_all)
    up_new = update(up_share, up_master, up_moment, up_average, tokens_all)
    down_new = update(down_share, down_master, down_moment, down_average, tokens_all)
    gain_new = update_steps(gain_share, gain_master, gain_moment, gain_average, tokens_all)
    bias_new = update(bias_share, bias_master, bias_moment, bias_average, tokens_all)
    news = (qkv_new, proj_new, up_new, down_new, gain_new, bias_new)
    return (
        layer_output, input_grad,
        qkv_share, proj_share, up_share, down_share, gain_share, bias_share,
        *(n[0] for n in news), *(n[1] for n in news), *(n[2] for n in news),
    )


def solution(mesh):
    both = ("gx", "gy")
    two, one = P(both, None), P(both)
    weights = (two, two, two, two, one, one)
    in_specs = (two, two, one, two) + weights * 3
    out_specs = (two, two) + weights * 4
    return jax.shard_map(
        on_device, mesh=mesh, in_specs=in_specs, out_specs=out_specs, check_vma=False
    )
```

```python
from functools import partial

import jax
import jax.numpy as jnp
from jax import lax
from jax.experimental import pallas as pl
from jax.experimental.pallas import tpu as pltpu
from jax.sharding import PartitionSpec as P

D = 768
HEADS = 12
HEAD_DIM = 64
FF = 3072
SEQ = 512
BAND = 128
PACK = 4
GROUPS = HEADS // PACK
WIDE = PACK * HEAD_DIM
VMEM = 60 * 1024 * 1024

norm_eps = 1e-06
momentum_coef = 0.9
learn_rate = 4.0
average_keep = 0.9

G1, G2, BQ, BV, BO, C1, B1, B2, C2 = (0, 1, 2, 3, 4, 5, 6, 10, 11)
TABLE = 16
CHUNK = 768
CHUNKS = 12
HALF = CHUNK // 2
MESH = pl.DeviceIdType.MESH

f32 = jnp.float32
bf16 = jnp.bfloat16

LOG2E = 1.4426950408889634
SCORE = HEAD_DIM ** (-0.5) * LOG2E


def nn(a, b):
    return lax.dot_general(a, b, (((1,), (0,)), ((), ())), preferred_element_type=f32)


def nt(a, b):
    return lax.dot_general(a, b, (((1,), (1,)), ((), ())), preferred_element_type=f32)


def tn(a, b):
    return lax.dot_general(a, b, (((0,), (0,)), ((), ())), preferred_element_type=f32)


def normal_cdf(u):
    t = 1.0 / (1.0 + 0.28 * jnp.abs(u))
    gauss = jnp.exp2(u * u * (-0.5 * LOG2E))
    q = -0.10568755
    for k in (0.38938334, -0.23620046, 0.26827342, 0.0677507, 0.11648054):
        q = q * t + k
    tail = q * t * gauss
    return jnp.where(u >= 0, 1.0 - tail, tail), gauss


def windows():
    for b in range(SEQ // BAND):
        first = max(0, (b - 1) * BAND)
        last = min(SEQ, (b + 2) * BAND)
        yield b, first, last - first


def head_masks():
    lane = lax.broadcasted_iota(jnp.int32, (BAND, WIDE), 1) // HEAD_DIM
    return [jnp.where(lane == h, 1.0, 0.0).astype(bf16) for h in range(PACK)]


def spread_heads(block, masks):
    return jnp.concatenate([block * m for m in masks], axis=0)


def pick_heads(wide):
    return jnp.concatenate(
        [
            wide[h * HEAD_DIM : (h + 1) * HEAD_DIM, h * BAND : (h + 1) * BAND]
            for h in range(PACK)
        ],
        axis=0,
    )


def mask_bias(col, row, b, first, width):
    keys = col[first : first + width, :]
    queries = row[0:1, b * BAND : (b + 1) * BAND]
    bias = jnp.where(keys == queries, 0.0, -1e30)
    return jnp.concatenate([bias] * PACK, axis=1)


def norm_stats(y):
    centre = jnp.mean(y, axis=-1, keepdims=True)
    centred = y - centre
    spread = jnp.mean(centred * centred, axis=-1, keepdims=True)
    r = lax.rsqrt(spread + norm_eps)
    return centred * r, r


def norm_back(dz, z, r):
    return r * (
        dz
        - jnp.mean(dz, axis=-1, keepdims=True)
        - z * jnp.mean(dz * z, axis=-1, keepdims=True)
    )


def remote(src, dst, send, recv, device):
    return pltpu.make_async_remote_copy(
        src_ref=src, dst_ref=dst, send_sem=send, recv_sem=recv, device_id=device,
        device_id_type=MESH,
    )


class Place:
    def __init__(self, nz):
        gx = lax.axis_index("gx")
        gy = lax.axis_index("gy")
        self.nz = nz
        self.x, self.y = gx % 2, gx // 2
        self.z, self.c = gy // 2, gy % 2
        x, y, z, c = self.x, self.y, self.z, self.c
        self.other = (gx, z * 2 + 1 - c)
        ax, ay = x + (1 - c) * (1 - 2 * x), y + c * (1 - 2 * y)
        bx, by = x + c * (1 - 2 * x), y + (1 - c) * (1 - 2 * y)
        self.first = (ay * 2 + ax, gy)
        self.second = (by * 2 + bx, gy)
        self.quarter = gx
        self.quarter_first = ay * 2 + ax
        self.quarter_second = by * 2 + bx
        self.quarter_far = (1 - y) * 2 + 1 - x

    def along_z(self, j):
        return (self.quarter, (self.z + j) % self.nz * 2 + self.c)

    def barrier(self):
        sem = pltpu.get_barrier_semaphore()
        partners = [self.other, self.first, self.second]
        partners += [self.along_z(j) for j in range(1, self.nz)]
        for p in partners:
            pl.semaphore_signal(sem, inc=1, device_id=p, device_id_type=MESH)
        pl.semaphore_wait(sem, len(partners))


def fold_rows(v):
    n = v.shape[0]
    return jnp.sum(v.reshape(n // 8, 8, v.shape[1]), axis=0)


class Gather:
    def __init__(self, nz, wa, wb, held, stage, z_sem, s_sem, own_sem, load_sem):
        self.at = Place(nz)
        self.nz, self.wa, self.wb, self.held, self.stage = nz, wa, wb, held, stage
        self.z_sem, self.s_sem, self.own_sem, self.load_sem = z_sem, s_sem, own_sem, load_sem

    def step(self, j, k):
        if isinstance(k, int):
            self.act(j, k, k < 8)
            return
        pl.when((k >= 2) & (k < 8))(lambda: self.act(j, k, True))
        if j < 5:
            pl.when((k >= 8) & (k < CHUNKS))(lambda: self.act(j, k, False))

    def act(self, j, k, first):
        at, nz = self.at, self.nz
        mine = pl.ds(pl.multiple_of(at.c * HALF, HALF), HALF)
        others = pl.ds(pl.multiple_of((1 - at.c) * HALF, HALF), HALF)

        def spot(chip, lanes=mine):
            if first:
                return self.wa.at[k, chip, :, lanes]
            return self.wb.at[chip, k - 8, :, lanes]

        def quarter(q):
            return spot(pl.ds(q * nz, nz))

        def z_copy(i, chip):
            return remote(
                self.stage.at[k], spot(chip), self.z_sem.at[0, k, i - 1],
                self.z_sem.at[1, k, i - 1], at.along_z(i),
            )

        def s_copy(i, q, device):
            return remote(quarter(q), quarter(q), self.s_sem.at[0, k, i], self.s_sem.at[1, k, i], device)

        def c_copy(lanes):
            whole = spot(slice(None), lanes)
            return remote(whole, whole, self.s_sem.at[0, k, 3], self.s_sem.at[1, k, 3], at.other)

        chip = at.quarter * nz + at.z

        def own():
            return pltpu.make_async_copy(self.stage.at[k], spot(chip), self.own_sem.at[k])

        if j == 0:
            for i in range(1, nz):
                z_copy(i, chip).start()
            own().start()
        elif j == 1:
            for i in range(1, nz):
                z_copy(i, at.quarter * nz + (at.z - i + nz) % nz).wait_recv()
            own().wait()
            s_copy(0, at.quarter, at.first).start()
            s_copy(1, at.quarter, at.second).start()
        elif j == 2:
            s_copy(0, at.quarter_first, at.first).wait_recv()
            s_copy(2, at.quarter_first, at.second).start()
        elif j == 3:
            s_copy(1, at.quarter_second, at.second).wait_recv()
            s_copy(2, at.quarter_far, at.second).wait_recv()
            c_copy(mine).start()
        elif j == 4:
            c_copy(others).wait_recv()
            for i in range(1, nz):
                z_copy(i, chip).wait_send()
            s_copy(0, at.quarter, at.first).wait_send()
            s_copy(1, at.quarter, at.second).wait_send()
            s_copy(2, at.quarter_first, at.second).wait_send()
            c_copy(mine).wait_send()
            if first:
                self.load(k).start()
        elif first:
            self.load(k).wait()

    def load(self, k):
        return pltpu.make_async_copy(self.wa.at[k], self.held.at[k], self.load_sem.at[k])


def share_start(nz, part_ref, masters, sibs, stage, table_ref, sums, got, x_sem, v_sem, gather):
    at = gather.at
    at.barrier()
    swaps = [
        remote(m, o, x_sem.at[0, i], x_sem.at[1, i], at.other)
        for i, (m, o) in enumerate(zip(masters, sibs))
    ]
    swaps.insert(1, remote(part_ref, got.at[0], x_sem.at[0, 4], x_sem.at[1, 4], at.other))
    for swap in swaps:
        swap.start()
    mq, mo, m1, m2 = masters
    sq, so, s1, s2 = sibs
    even = at.c == 0

    def halves(own, sib):
        own = jnp.where(even, own[:, :HALF], own[:, HALF:])
        sib = jnp.where(even, sib[:, :HALF], sib[:, HALF:])
        top, low = jnp.where(even, own, sib), jnp.where(even, sib, own)
        return jnp.concatenate([top, low], axis=0).astype(bf16)

    def group(ref, hg):
        cols = [ref[:, i * D + hg * WIDE : i * D + (hg + 1) * WIDE] for i in range(3)]
        return jnp.concatenate(cols, axis=1)

    def vec_copy(i, src, device):
        return remote(src, got.at[i], v_sem.at[0, i], v_sem.at[1, i], device)

    swaps[0].wait()
    for hg in range(GROUPS):
        stage[hg] = halves(group(mq, hg), group(sq, hg))
        if hg < 2:
            gather.step(0, hg)
    swaps[1].wait()
    sums[0] = part_ref[...] + got[0]
    z_copies = [vec_copy(i, sums.at[0], at.along_z(i)) for i in range(1, nz)]
    for copy in z_copies:
        copy.start()
    for swap in swaps[2:]:
        swap.wait()
    stage[3] = halves(mo[...], so[...])
    for f in range(4):
        cols = slice(f * CHUNK, (f + 1) * CHUNK)
        stage[4 + f] = halves(m1[:, cols], s1[:, cols])
    step = stage.shape[1]
    for i in range(4):
        rows = slice(i % 2 * step, (i % 2 + 1) * step)
        block = jnp.where(at.c == i // 2, m2[rows, :], s2[rows, :])
        stage[8 + i] = jnp.where(even, block[:, :HALF], block[:, HALF:]).astype(bf16)
    gather.step(1, 0)
    gather.step(1, 1)
    for copy in z_copies:
        copy.wait()
    total = sums[0]
    for i in range(1, nz):
        total = total + got[i]
    sums[1] = total
    a_copy = vec_copy(nz, sums.at[1], at.first)
    a_copy.start()
    gather.step(2, 0)
    a_copy.wait()
    sums[2] = sums[1] + got[nz]
    b_copy = vec_copy(nz + 1, sums.at[2], at.second)
    b_copy.start()
    gather.step(2, 1)
    gather.step(3, 0)
    b_copy.wait()
    table_ref[...] = (sums[2] + got[nz + 1]).astype(f32)
    gather.step(4, 0)
    gather.step(3, 1)
    gather.step(5, 0)


def front_kernel(nz, *refs):
    refs = list(refs)
    x_ref, row_ref, col_ref, vec_ref = refs[:4]
    s = pl.program_id(0)
    att = GROUPS * 4
    if nz:
        masters, refs = refs[4:8], refs[8:]
    else:
        wa_ref, refs = refs[4], refs[5:]
    q_ref, k_ref, v_ref, lse_ref, c_ref, y1_ref, n1_ref, g_ref, gp_ref = refs[:9]
    refs = refs[9:]
    if nz:
        wa_ref, wb_ref, table_ref = refs[:3]
        c_all, held, stage, sq, so, s1, s2, sums, got = refs[3:12]
        z_sem, s_sem, own_sem, load_sem, x_sem, v_sem = refs[12:]
        gather = Gather(nz, wa_ref, wb_ref, held, stage, z_sem, s_sem, own_sem, load_sem)

        @pl.when(s == 0)
        def _():
            share_start(
                nz, vec_ref, masters, (sq, so, s1, s2), stage, table_ref, sums, got,
                x_sem, v_sem, gather,
            )

        for j in (5, 4, 3, 2, 1, 0):
            if j >= 4:
                pl.when(s == j - 4)(lambda: gather.step(j, 1))
            gather.step(j, s + 2 - j)
    else:
        c_all, held, load_sem = refs
        table_ref = vec_ref

        @pl.when(s == 0)
        def _():
            copy = pltpu.make_async_copy(wa_ref, held, load_sem)
            copy.start()
            copy.wait()

    def weight(k):
        return held[k].reshape(CHUNK, CHUNK)

    @pl.when(s < att)
    def _():
        hg = s // 4
        r = s % 4
        rows = pl.multiple_of(r * SEQ, SEQ)
        lanes = pl.multiple_of(hg * WIDE, WIDE)
        xr = x_ref[pl.ds(rows, SEQ), :]
        wqkv = weight(hg)
        q = nn(xr, wqkv[:, 0:WIDE]) + table_ref[BQ : BQ + 1, pl.ds(lanes, WIDE)]
        q = q.astype(bf16)
        k = nn(xr, wqkv[:, WIDE : 2 * WIDE]).astype(bf16)
        v = nn(xr, wqkv[:, 2 * WIDE :]) + table_ref[BV : BV + 1, pl.ds(lanes, WIDE)]
        v = v.astype(bf16)
        q_ref[...] = q
        k_ref[...] = k
        v_ref[...] = v
        vt = v.T
        masks = head_masks()
        for b, first, width in windows():
            qc = spread_heads(q[b * BAND : (b + 1) * BAND, :], masks)
            t = nt(k[first : first + width, :], qc) * SCORE
            t = t + mask_bias(col_ref.at[0], row_ref.at[0], b, first, width)
            m = jnp.max(t, axis=0, keepdims=True)
            e = jnp.exp2(t - m)
            l = jnp.sum(e, axis=0, keepdims=True)
            p = (e * (1.0 / l)).astype(bf16)
            lse_ref[0, b : b + 1, :] = m + jnp.log2(l)
            ot = nn(vt[:, first : first + width], p)
            c = pick_heads(ot).T.astype(bf16)
            c_all[pl.ds(rows + b * BAND, BAND), pl.ds(lanes, WIDE)] = c

    @pl.when(s >= att)
    def _():
        r = s - att
        rows = pl.multiple_of(r * SEQ, SEQ)
        c = c_all[pl.ds(rows, SEQ), :]
        c_ref[...] = c
        y1 = x_ref[pl.ds(rows, SEQ), :].astype(f32) + (
            nn(c, weight(3)) + table_ref[BO : BO + 1, :]
        )
        y1_ref[...] = y1
        z1, _ = norm_stats(y1)
        n1 = (z1 * table_ref[G1 : G1 + 1, :] + table_ref[C1 : C1 + 1, :]).astype(bf16)
        n1_ref[...] = n1
        for f in range(4):
            cols = slice(f * CHUNK, (f + 1) * CHUNK)
            u = nn(n1, weight(4 + f)) + table_ref[B1 + f : B1 + f + 1, :]
            cdf, gauss = normal_cdf(u)
            g_ref[:, cols] = (u * cdf).astype(bf16)
            gp_ref[:, cols] = (cdf + u * (gauss * 0.3989422804014327)).astype(bf16)


def constant(shape):
    return pl.BlockSpec(shape, lambda s: (0,) * len(shape), pipeline_mode=pl.Buffered(1))


def front(x, row_codes, col_codes, table, weights, chips=0):
    tokens = x.shape[0]
    rows = tokens // SEQ
    assert rows == 4
    att = GROUPS * rows
    nz = chips // 4

    def code_at(s):
        return (jnp.where(s < att, s % rows, rows - 1), 0, 0)

    def head_at(s):
        return (jnp.where(s < att, s % rows, rows - 1), jnp.minimum(s // rows, GROUPS - 1))

    def tile_at(s):
        return (jnp.maximum(s - att, 0), 0)

    anywhere = pl.BlockSpec(memory_space=pl.ANY)
    narrow = pl.BlockSpec((SEQ, D), tile_at)
    head = pl.BlockSpec((SEQ, WIDE), head_at)
    wide = pl.BlockSpec((SEQ, FF), tile_at)
    in_specs = [
        constant((tokens, D)),
        pl.BlockSpec((1, 8, SEQ), code_at),
        pl.BlockSpec((1, SEQ, BAND), code_at),
        constant((TABLE, CHUNK)),
    ]
    out_specs = [
        head, head, head,
        pl.BlockSpec((1, 8, PACK * BAND), lambda s: (jnp.minimum(s, att - 1), 0, 0)),
        narrow, narrow, narrow, wide, wide,
    ]
    low = jax.ShapeDtypeStruct((tokens, D), bf16)
    out_shape = [
        low, low, low,
        jax.ShapeDtypeStruct((att, 8, PACK * BAND), f32),
        low,
        jax.ShapeDtypeStruct((tokens, D), f32),
        low,
        jax.ShapeDtypeStruct((tokens, FF), bf16),
        jax.ShapeDtypeStruct((tokens, FF), bf16),
    ]
    if nz:
        step = CHUNK // chips
        in_specs += [constant(w.shape) for w in weights]
        out_specs += [anywhere, anywhere, pl.BlockSpec((TABLE, CHUNK), lambda s: (0, 0))]
        out_shape += [
            jax.ShapeDtypeStruct((8, chips, step, CHUNK), bf16),
            jax.ShapeDtypeStruct((chips, 4, step, CHUNK), bf16),
            jax.ShapeDtypeStruct((TABLE, CHUNK), f32),
        ]
        dma = pltpu.SemaphoreType.DMA
        scratch = [
            pltpu.VMEM((tokens, D), bf16),
            pltpu.VMEM((8, chips, step, CHUNK), bf16),
            pltpu.VMEM((CHUNKS, step, HALF), bf16),
            *(pltpu.VMEM(w.shape, f32) for w in weights),
            pltpu.VMEM((3, TABLE, CHUNK), bf16),
            pltpu.VMEM((nz + 2, TABLE, CHUNK), bf16),
            dma((2, CHUNKS, nz - 1)), dma((2, CHUNKS, 4)), dma((CHUNKS,)), dma((8,)),
            dma((2, 5)), dma((2, nz + 2)),
        ]
        params = pltpu.CompilerParams(
            vmem_limit_bytes=VMEM, collective_id=0, has_side_effects=True
        )
    else:
        in_specs.append(anywhere)
        scratch = [
            pltpu.VMEM((tokens, D), bf16),
            pltpu.VMEM(weights[0].shape, bf16),
            pltpu.SemaphoreType.DMA,
        ]
        params = pltpu.CompilerParams(vmem_limit_bytes=VMEM)
    return pl.pallas_call(
        partial(front_kernel, nz),
        grid=(att + rows,),
        in_specs=in_specs,
        out_specs=out_specs,
        out_shape=out_shape,
        scratch_shapes=scratch,
        compiler_params=params,
        name="front",
    )(x, row_codes, col_codes, table, *weights)


def middle_kernel(
    y1_ref, g_ref, gp_ref, cot_ref, vec_ref, wo_ref, w1_ref, w2_ref,
    out_ref, df_ref, du_ref, dy1_ref, da_ref, dc_ref, grads_ref, sums_ref, ups_ref,
):
    s = pl.program_id(0)

    @pl.when(s == 0)
    def _():
        sums_ref[...] = jnp.zeros_like(sums_ref)
        ups_ref[...] = jnp.zeros_like(ups_ref)

    z1, r1 = norm_stats(y1_ref[...])
    gain1 = vec_ref[G1 : G1 + 1, :]
    gain2 = vec_ref[G2 : G2 + 1, :]
    n1 = z1 * gain1 + vec_ref[C1 : C1 + 1, :]
    y2 = n1 + (nn(g_ref[...], w2_ref[...]) + vec_ref[B2 : B2 + 1, :])
    z2, r2 = norm_stats(y2)
    out_ref[...] = (z2 * gain2 + vec_ref[C2 : C2 + 1, :]).astype(bf16)
    e = cot_ref[...].astype(f32)
    sums_ref[0] += fold_rows(e * z2)
    sums_ref[1] += fold_rows(e)
    dy2 = norm_back(e * gain2, z2, r2)
    df = dy2.astype(bf16)
    df_ref[...] = df
    sums_ref[2] += fold_rows(df.astype(f32))
    step = 768
    for f in range(0, FF, step):
        dg = nt(df, w2_ref[f : f + step, :])
        du = (dg * gp_ref[:, f : f + step].astype(f32)).astype(bf16)
        du_ref[:, f : f + step] = du
        ups_ref[:, f : f + step] += fold_rows(du.astype(f32))
    dn1 = dy2
    for f in range(4):
        dn1 = dn1 + nt(du_ref[:, f * CHUNK : (f + 1) * CHUNK], w1_ref[f])
    sums_ref[3] += fold_rows(dn1 * z1)
    sums_ref[4] += fold_rows(dn1)
    dy1 = norm_back(dn1 * gain1, z1, r1)
    dy1_ref[...] = dy1
    da = dy1.astype(bf16)
    da_ref[...] = da
    sums_ref[5] += fold_rows(da.astype(f32))
    dc_ref[...] = nt(da, wo_ref[0]).astype(bf16)

    @pl.when(s == pl.num_programs(0) - 1)
    def _():
        grads_ref[...] = jnp.zeros_like(grads_ref)
        for i, row in enumerate((G2, C2, B2, G1, C1, BO)):
            grads_ref[row : row + 1, :] = jnp.sum(sums_ref[i], axis=0, keepdims=True)
        for f in range(4):
            cols = slice(f * CHUNK, (f + 1) * CHUNK)
            grads_ref[B1 + f : B1 + f + 1, :] = jnp.sum(ups_ref[:, cols], axis=0, keepdims=True)


def chunks_at(count, index):
    return pl.BlockSpec(
        (count, CHUNK, CHUNK), lambda s: (index, 0, 0), pipeline_mode=pl.Buffered(1)
    )


def middle(y1, g, gp, cot, table, wa, w2):
    tokens = y1.shape[0]
    tile = SEQ

    narrow = pl.BlockSpec((tile, D), lambda s: (s, 0))
    wide = pl.BlockSpec((tile, FF), lambda s: (s, 0))
    wide_out = pl.BlockSpec((tile, FF), lambda s: (s, 0))
    return pl.pallas_call(
        middle_kernel,
        grid=(tokens // tile,),
        in_specs=[
            narrow, wide, wide, narrow, constant((TABLE, CHUNK)),
            chunks_at(1, 3), chunks_at(4, 1), constant((FF, D)),
        ],
        out_specs=[
            narrow, narrow, wide_out, narrow, narrow, narrow,
            pl.BlockSpec((TABLE, CHUNK), lambda s: (0, 0)),
        ],
        out_shape=[
            jax.ShapeDtypeStruct((tokens, D), bf16),
            jax.ShapeDtypeStruct((tokens, D), bf16),
            jax.ShapeDtypeStruct((tokens, FF), bf16),
            jax.ShapeDtypeStruct((tokens, D), f32),
            jax.ShapeDtypeStruct((tokens, D), bf16),
            jax.ShapeDtypeStruct((tokens, D), bf16),
            jax.ShapeDtypeStruct((TABLE, CHUNK), f32),
        ],
        scratch_shapes=[pltpu.VMEM((6, 8, D), f32), pltpu.VMEM((8, FF), f32)],
        compiler_params=pltpu.CompilerParams(vmem_limit_bytes=VMEM),
        name="middle",
    )(y1, g, gp, cot, table, wa, wa, w2)


def outer_kernel(a_ref, b_ref, o_ref):
    o_ref[...] = tn(a_ref[...], b_ref[...]).astype(o_ref.dtype).reshape(o_ref.shape)


def outer(a, b, dtype, side):
    tokens, m = a.shape
    n = b.shape[1]
    if side == 0:
        grid, a_at, b_at = m // CHUNK, (lambda i: (0, i)), (lambda i: (0, 0))
    else:
        grid, a_at, b_at = n // CHUNK, (lambda i: (0, 0)), (lambda i: (0, i))
    return pl.pallas_call(
        outer_kernel,
        grid=(grid,),
        in_specs=[pl.BlockSpec((tokens, CHUNK), a_at), pl.BlockSpec((tokens, CHUNK), b_at)],
        out_specs=pl.BlockSpec((1, CHUNK, CHUNK), lambda i: (i, 0, 0)),
        out_shape=jax.ShapeDtypeStruct((grid, CHUNK, CHUNK), dtype),
        compiler_params=pltpu.CompilerParams(vmem_limit_bytes=VMEM),
        name="outer",
    )(a, b)


DOWN, UP, PROJ, QKV = 0, 4, 8, 9


class Reduce:
    def __init__(self, nz, grads, made, local, bufs, fin, outs, sems):
        self.at = Place(nz)
        self.nz, self.grads, self.made, self.local = nz, grads, made, local
        self.bufs, self.fin, self.outs = bufs, fin, outs
        self.c_sem, self.l_sem, self.q_sem, self.z_sem, self.f_sem = sems

    def step(self, j, r):
        if isinstance(r, int):
            self.act(j, r)
        else:
            pl.when((r >= 0) & (r < QKV))(lambda: self.act(j, r))

    def source(self, r, lanes, fn):
        g2, g1, go = self.grads
        if isinstance(r, int):
            assert r >= QKV
            fn(self.made.at[r - QKV, :, :, lanes])
            return
        pl.when(r < UP)(lambda: fn(g2.at[:, r, :, lanes]))
        pl.when((r >= UP) & (r < PROJ))(lambda: fn(g1.at[r - UP, :, :, lanes]))
        pl.when(r == PROJ)(lambda: fn(go.at[0, :, :, lanes]))

    def act(self, j, r):
        at, nz = self.at, self.nz
        r0, r1, r2, r3 = self.bufs
        fin, got = self.fin
        c, x, y, z = at.c, at.x, at.y, at.z
        half = [pl.ds(pl.multiple_of(i * HALF, HALF), HALF) for i in (c, 1 - c)]

        def c_copy(src):
            return remote(src, r0.at[r], self.c_sem.at[0, r], self.c_sem.at[1, r], at.other)

        def l_copy(src):
            return pltpu.make_async_copy(src, self.local.at[r % 2], self.l_sem.at[r % 2])

        def a_copy(i):
            q = (1 - c) * (2 * i + 1 - x) + c * (2 * (1 - y) + i)
            return remote(
                r0.at[r, pl.ds(q * nz, nz)], r1.at[r, i],
                self.q_sem.at[0, r, i], self.q_sem.at[1, r, i], at.first,
            )

        keep = (1 - c) * y + c * x

        def b_copy():
            return remote(
                r1.at[r, 1 - keep], r2.at[r],
                self.q_sem.at[0, r, 2], self.q_sem.at[1, r, 2], at.second,
            )

        def z_copy(i):
            return remote(
                r2.at[r, (z + i) % nz], r3.at[r, i - 1],
                self.z_sem.at[0, r, i - 1], self.z_sem.at[1, r, i - 1], at.along_z(i),
            )

        def f_copy():
            return remote(fin.at[r], got.at[r], self.f_sem.at[0, r], self.f_sem.at[1, r], at.other)

        rows = fin.shape[1] // 2
        if j == 0:
            self.source(r, half[1], lambda src: c_copy(src).start())
            if not isinstance(r, int):
                self.source(r, half[0], lambda src: l_copy(src).start())
        elif j == 1:
            if isinstance(r, int):
                c_copy(self.made.at[r - QKV, :, :, half[1]]).wait()
                mine = jnp.where(
                    c == 0, self.made[r - QKV, :, :, :HALF], self.made[r - QKV, :, :, HALF:]
                )
            else:
                self.source(r, half[1], lambda src: c_copy(src).wait())
                self.source(r, half[0], lambda src: l_copy(src).wait())
                mine = self.local[r % 2]
            r0[r] = r0[r] + mine
            a_copy(0).start()
            a_copy(1).start()
        elif j == 2:
            for i in (0, 1):
                a_copy(i).wait()
                q = (1 - c) * (2 * i + x) + c * (2 * y + i)
                r1[r, i] = r1[r, i] + r0[r, pl.ds(q * nz, nz)]
            b_copy().start()
        elif j == 3:
            b_copy().wait()
            r2[r] = r2[r] + r1[r, keep]
            for i in range(1, nz):
                z_copy(i).start()
        elif j == 4:
            total = r2[r, z].astype(f32)
            for i in range(1, nz):
                z_copy(i).wait()
                total = total + r3[r, i - 1].astype(f32)
            fin[r] = total
            f_copy().start()
        else:
            f_copy().wait()
            self.finish(r, rows)

    def finish(self, r, rows):
        c = self.at.c
        fin, got = self.fin
        out, out_down = self.outs
        even = c == 0

        def sides(own, other):
            return jnp.concatenate(
                [jnp.where(even, own, other), jnp.where(even, other, own)], axis=1
            )

        def down():
            @pl.when(c == r // 2)
            def _():
                out_down[r % 2] = sides(fin[r], got[r])

        def rest():
            own = jnp.where(even, fin[r, :rows, :], fin[r, rows:, :])
            other = jnp.where(even, got[r, :rows, :], got[r, rows:, :])
            out[r - UP] = sides(own, other)

        if isinstance(r, int):
            rest()
        else:
            pl.when(r < UP)(down)
            pl.when(r >= UP)(rest)


def back_kernel(nz, *refs):
    x_ref, row_ref, col_ref, wqkv_ref, q_ref, k_ref, v_ref, dc_ref, lse_ref, dy1_ref = refs[:10]
    refs = refs[10:]
    s = pl.program_id(0)
    att = GROUPS * 4
    if nz:
        table_ref, g2, g1, go, out, out_down, total_ref, dx_ref = refs[:8]
        dqkv, dk_sum, dv_sum, qv_sum, made, local, r0, r1, r2, r3, fin, got = refs[8:20]
        mine, came = refs[20:22]
        sems, v_sem = refs[22:27], refs[27]
        reduce = Reduce(
            nz, (g2, g1, go), made, local, (r0, r1, r2, r3), (fin, got), (out, out_down), sems
        )
        at = reduce.at

        @pl.when(s == 0)
        def _():
            at.barrier()

        for j in (5, 4, 3, 2, 1, 0):
            reduce.step(j, s - j)
            for hg in range(GROUPS - 1):
                pl.when(s == (hg + 1) * 4 + j)(lambda: reduce.step(j, QKV + hg))
    else:
        dw_ref, dx_ref, total_ref, dqkv, dk_sum, dv_sum, qv_sum = refs

    @pl.when(s == 0)
    def _():
        qv_sum[...] = jnp.zeros_like(qv_sum)

    @pl.when(s < att)
    def _():
        hg = s // 4
        r = s % 4
        rows = pl.multiple_of(r * SEQ, SEQ)
        lanes = pl.ds(pl.multiple_of(hg * WIDE, WIDE), WIDE)
        kt = k_ref[...].T
        dk_sum[...] = jnp.zeros_like(dk_sum)
        dv_sum[...] = jnp.zeros_like(dv_sum)
        masks = head_masks()
        for b, first, width in windows():
            block = slice(b * BAND, (b + 1) * BAND)
            span = slice(first, first + width)
            qc = spread_heads(q_ref[block, :], masks)
            dcc = spread_heads(dc_ref[block, :], masks)
            t = nt(k_ref[span, :], qc) * SCORE
            t = t + mask_bias(col_ref.at[0], row_ref.at[0], b, first, width)
            p = jnp.exp2(t - lse_ref[0, b : b + 1, :])
            dp = nt(v_ref[span, :], dcc)
            dv_sum[span, :] += nn(p.astype(bf16), dcc)
            pdp = p * dp
            weighted = jnp.sum(pdp, axis=0, keepdims=True)
            ds = (pdp - p * weighted).astype(bf16)
            dk_sum[span, :] += nn(ds, qc)
            dqt = nn(kt[:, span], ds)
            dq = (pick_heads(dqt).T * HEAD_DIM ** (-0.5)).astype(bf16)
            dqkv[hg, pl.ds(rows + b * BAND, BAND), 0:WIDE] = dq
            qv_sum[0, :, lanes] += fold_rows(dq.astype(f32))
        dk = (dk_sum[...] * HEAD_DIM ** (-0.5)).astype(bf16)
        dv = dv_sum[...].astype(bf16)
        dqkv[hg, pl.ds(rows, SEQ), WIDE : 2 * WIDE] = dk
        dqkv[hg, pl.ds(rows, SEQ), 2 * WIDE :] = dv
        qv_sum[1, :, lanes] += fold_rows(dv.astype(f32))

        @pl.when(r == 3)
        def _():
            dw = tn(x_ref[...], dqkv[hg])
            if nz:
                made[hg] = dw.astype(bf16).reshape(made.shape[1:])
            else:
                dw_ref[0] = dw

    if nz:
        def vec_copy(i, src, device):
            return remote(src, came.at[i], v_sem.at[0, i], v_sem.at[1, i], device)

        c_copy = vec_copy(0, mine.at[0], at.other)
        z_copies = [vec_copy(i, mine.at[1], at.along_z(i)) for i in range(1, nz)]
        a_copy = vec_copy(nz, mine.at[2], at.first)
        b_copy = vec_copy(nz + 1, mine.at[3], at.second)

        @pl.when(s == att - 1)
        def _():
            reduce.step(0, QKV + GROUPS - 1)
            mine[0] = table_ref[...]
            mine[0, BQ : BQ + 1, :] = jnp.sum(qv_sum[0], axis=0, keepdims=True)
            mine[0, BV : BV + 1, :] = jnp.sum(qv_sum[1], axis=0, keepdims=True)
            c_copy.start()

        @pl.when(s == att)
        def _():
            reduce.step(1, QKV + GROUPS - 1)
            c_copy.wait()
            mine[1] = mine[0] + came[0]
            for copy in z_copies:
                copy.start()

        @pl.when(s == att + 1)
        def _():
            reduce.step(2, QKV + GROUPS - 1)
            total = mine[1]
            for i in range(1, nz):
                z_copies[i - 1].wait()
                total = total + came[i]
            mine[2] = total
            a_copy.start()

        @pl.when(s == att + 2)
        def _():
            reduce.step(3, QKV + GROUPS - 1)
            a_copy.wait()
            mine[3] = mine[2] + came[nz]
            b_copy.start()

        @pl.when(s == att + 3)
        def _():
            reduce.step(4, QKV + GROUPS - 1)

    @pl.when(s >= att)
    def _():
        rows = pl.multiple_of((s - att) * SEQ, SEQ)
        total = dy1_ref[...]
        for hg in range(GROUPS):
            total = total + nt(dqkv[hg, pl.ds(rows, SEQ), :], wqkv_ref[hg])
        dx_ref[...] = total

    @pl.when(s == att + 3)
    def _():
        if nz:
            b_copy.wait()
            total_ref[...] = mine[3] + came[nz + 1]
            reduce.step(5, QKV + GROUPS - 1)
        else:
            total_ref[...] = jnp.zeros_like(total_ref)
            total_ref[BQ : BQ + 1, :] = jnp.sum(qv_sum[0], axis=0, keepdims=True)
            total_ref[BV : BV + 1, :] = jnp.sum(qv_sum[1], axis=0, keepdims=True)


def back(x, row_codes, col_codes, wa, q, k, v, dc, lse, dy1, table=None, grads=None, chips=0):
    tokens = x.shape[0]
    rows = tokens // SEQ
    att = GROUPS * rows
    assert rows == 4
    nz = chips // 4

    def code_at(s):
        return (jnp.where(s < att, s % rows, rows - 1), 0, 0)

    def head_at(s):
        return (jnp.where(s < att, s % rows, rows - 1), jnp.minimum(s // rows, GROUPS - 1))

    def tile_at(s):
        return (jnp.maximum(s - att, 0), 0)

    anywhere = pl.BlockSpec(memory_space=pl.ANY)
    whole_table = pl.BlockSpec((TABLE, CHUNK), lambda s: (0, 0))
    head = pl.BlockSpec((SEQ, WIDE), head_at)
    tile = pl.BlockSpec((SEQ, D), tile_at)
    dx = jax.ShapeDtypeStruct((tokens, D), f32)
    total = jax.ShapeDtypeStruct((TABLE, CHUNK), f32)
    in_specs = [
        constant((tokens, D)),
        pl.BlockSpec((1, 8, SEQ), code_at),
        pl.BlockSpec((1, SEQ, BAND), code_at),
        chunks_at(3, 0),
        head, head, head, head,
        pl.BlockSpec((1, 8, PACK * BAND), lambda s: (jnp.minimum(s, att - 1), 0, 0)),
        tile,
    ]
    scratch = [
        pltpu.VMEM((GROUPS, tokens, 3 * WIDE), bf16),
        pltpu.VMEM((SEQ, WIDE), f32),
        pltpu.VMEM((SEQ, WIDE), f32),
        pltpu.VMEM((2, 8, D), f32),
    ]
    args = [x, row_codes, col_codes, wa, q, k, v, dc, lse, dy1]
    if nz:
        step = CHUNK // chips
        dma = pltpu.SemaphoreType.DMA
        g2, g1, go = grads
        args += [
            table,
            g2.reshape(chips, 4, step, CHUNK),
            g1.reshape(4, chips, step, CHUNK),
            go.reshape(1, chips, step, CHUNK),
        ]
        in_specs += [whole_table, anywhere, anywhere, anywhere]
        out_specs = [
            pl.BlockSpec((8, step // 2, CHUNK), lambda s: (0, 0, 0)),
            pl.BlockSpec((2, step, CHUNK), lambda s: (0, 0, 0)),
            whole_table, tile,
        ]
        out_shape = [
            jax.ShapeDtypeStruct((8, step // 2, CHUNK), f32),
            jax.ShapeDtypeStruct((2, step, CHUNK), f32),
            total, dx,
        ]
        scratch += [
            pltpu.VMEM((GROUPS, chips, step, CHUNK), bf16),
            pltpu.VMEM((2, chips, step, HALF), bf16),
            pltpu.VMEM((CHUNKS, chips, step, HALF), bf16),
            pltpu.VMEM((CHUNKS, 2, nz, step, HALF), bf16),
            pltpu.VMEM((CHUNKS, nz, step, HALF), bf16),
            pltpu.VMEM((CHUNKS, nz - 1, step, HALF), bf16),
            pltpu.VMEM((CHUNKS, step, HALF), f32),
            pltpu.VMEM((CHUNKS, step, HALF), f32),
            pltpu.VMEM((4, TABLE, CHUNK), f32),
            pltpu.VMEM((nz + 2, TABLE, CHUNK), f32),
            dma((2, CHUNKS)), dma((2,)), dma((2, CHUNKS, 3)), dma((2, CHUNKS, nz - 1)),
            dma((2, CHUNKS)), dma((2, nz + 2)),
        ]
        params = pltpu.CompilerParams(
            vmem_limit_bytes=VMEM, collective_id=1, has_side_effects=True
        )
    else:
        out_specs = [
            pl.BlockSpec((1, D, 3 * WIDE), lambda s: (jnp.minimum(s // rows, GROUPS - 1), 0, 0)),
            tile, whole_table,
        ]
        out_shape = [jax.ShapeDtypeStruct((GROUPS, D, 3 * WIDE), f32), dx, total]
        params = pltpu.CompilerParams(vmem_limit_bytes=VMEM)
    return pl.pallas_call(
        partial(back_kernel, nz),
        grid=(att + rows,),
        in_specs=in_specs,
        out_specs=out_specs,
        out_shape=out_shape,
        scratch_shapes=scratch,
        compiler_params=params,
        name="back",
    )(*args)


def update(grad, master, moment, average, tokens_all):
    mean_grad = grad / tokens_all
    moment_new = momentum_coef * moment + mean_grad
    step_size = -learn_rate * (mean_grad + momentum_coef * moment_new)
    master_new = master + step_size
    average_new = average_keep * average + (1.0 - average_keep) * master_new
    return (master_new, moment_new, average_new)


def update_steps(grad, master, moment, average, tokens_all):
    mean_grad = grad / tokens_all
    moment_new = momentum_coef * moment + mean_grad
    step_size = -learn_rate * (mean_grad + momentum_coef * moment_new)
    average_step = (1.0 - average_keep) * (master + step_size - average)
    return (step_size, moment_new, average_step)


def update_kernel(tokens_all, *refs):
    grad_ref, down_ref = refs[:2]
    states, outs = refs[2:14], refs[14:]

    def one(i, index, grad):
        master, moment, average = (states[i + 4 * j][index] for j in range(3))
        outs[i][index] = grad
        new = update(grad, master, moment, average, tokens_all)
        for j in range(3):
            outs[i + 4 * (j + 1)][index] = new[j]

    rows = grad_ref.shape[1]
    for hg in range(GROUPS):
        for i in range(3):
            cols = slice(i * D + hg * WIDE, i * D + (hg + 1) * WIDE)
            one(0, (slice(None), cols), grad_ref[5 + hg, :, i * WIDE : (i + 1) * WIDE])
    one(1, (slice(None), slice(None)), grad_ref[4])
    for f in range(4):
        one(2, (slice(None), slice(f * CHUNK, (f + 1) * CHUNK)), grad_ref[f])
    for i in range(2):
        one(3, (slice(2 * rows * i, 2 * rows * (i + 1)), slice(None)), down_ref[i])


def update_weights(grads, grads_down, states, tokens_all):
    whole = pl.BlockSpec(memory_space=pltpu.VMEM)
    shapes = [jax.ShapeDtypeStruct(w.shape, f32) for w in states[:4]]
    return pl.pallas_call(
        partial(update_kernel, tokens_all),
        in_specs=[whole] * 14,
        out_specs=[whole] * 16,
        out_shape=shapes * 4,
        compiler_params=pltpu.CompilerParams(vmem_limit_bytes=VMEM),
        name="update",
    )(grads, grads_down, *states)


def group_columns(w):
    n = w.shape[0]
    return w.reshape(n, 3, GROUPS, WIDE).transpose(2, 0, 1, 3).reshape(GROUPS, n, 3 * WIDE)


def ungroup_columns(w):
    n = w.shape[1]
    return w.reshape(GROUPS, n, 3, WIDE).transpose(1, 2, 0, 3).reshape(n, 3 * D)


def table_of(gains, biases):
    flat = jnp.concatenate([gains, biases, jnp.zeros((TABLE * CHUNK - 9216,), gains.dtype)])
    return flat.reshape(TABLE, CHUNK)


def on_device(
    tokens, segment_ids, pad_counts, out_cotangent,
    qkv_master, proj_master, up_master, down_master, gain_master, bias_master,
    qkv_moment, proj_moment, up_moment, down_moment, gain_moment, bias_moment,
    qkv_average, proj_average, up_average, down_average, gain_average, bias_average,
):
    axes = ("gx", "gy")
    devices = lax.axis_size(axes)
    seq_len = segment_ids.shape[1]
    tokens_all = tokens.shape[0] * devices
    position = jnp.arange(seq_len, dtype=jnp.int32)
    is_pad = position[None, :] >= (seq_len - pad_counts)[:, None]
    codes = segment_ids * 2 + is_pad.astype(jnp.int32)
    row_codes = jnp.broadcast_to(codes[:, None, :], (codes.shape[0], 8, seq_len))
    col_codes = jnp.broadcast_to(codes[:, :, None], (codes.shape[0], seq_len, BAND))
    gain_len, bias_len = gain_master.shape[0], bias_master.shape[0]
    gains = gain_len * devices
    place = lax.axis_index(axes)

    fine = lax.axis_size("gx") == 4 and (2 * D // devices) % 16 == 0
    if fine:
        chips = devices // 2
        part = jnp.zeros((TABLE * CHUNK,), bf16)
        part = lax.dynamic_update_slice(part, gain_master.astype(bf16), (place * gain_len,))
        part = lax.dynamic_update_slice(
            part, bias_master.astype(bf16), (gains + place * bias_len,)
        ).reshape(TABLE, CHUNK)
        q, k, v, lse, c, y1, n1, g, gp, wa, w2, table = front(
            tokens, row_codes, col_codes, part,
            (qkv_master, proj_master, up_master, down_master), chips,
        )
        wa = wa.reshape(8, CHUNK, CHUNK)
        w2 = w2.reshape(FF, D)
    else:
        gather = partial(lax.all_gather, axis_name=axes, axis=0, tiled=True)
        w1 = gather(up_master.astype(bf16))
        wa = jnp.concatenate(
            [
                group_columns(gather(qkv_master.astype(bf16))),
                gather(proj_master.astype(bf16))[None],
                w1.reshape(D, 4, CHUNK).transpose(1, 0, 2),
            ]
        )
        w2 = gather(down_master.astype(bf16))
        table = table_of(
            gather(gain_master.astype(bf16)), gather(bias_master.astype(bf16))
        ).astype(f32)
        q, k, v, lse, c, y1, n1, g, gp = front(
            tokens, row_codes, col_codes, table, (wa.reshape(8, 16, CHUNK // 16, CHUNK),)
        )
    layer_output, df, du, dy1, da, dc, terms = middle(y1, g, gp, out_cotangent, table, wa, w2)
    kept = bf16 if fine else f32
    dw2 = outer(g, df, kept, 0)
    dw1 = outer(n1, du, kept, 1)
    dwo = outer(c, da, kept, 0)
    scatter = partial(lax.psum_scatter, axis_name=axes, scatter_dimension=0, tiled=True)
    states = (
        qkv_master, proj_master, up_master, down_master,
        qkv_moment, proj_moment, up_moment, down_moment,
        qkv_average, proj_average, up_average, down_average,
    )
    if fine:
        grads, grads_down, terms, input_grad = back(
            tokens, row_codes, col_codes, wa, q, k, v, dc, lse, dy1, terms,
            (dw2, dw1, dwo), chips,
        )
        new = update_weights(grads, grads_down, states, tokens_all)
        shares, masters, moments, averages = new[:4], new[4:8], new[8:12], new[12:]
        terms = terms.reshape(-1)
        gain_share = lax.dynamic_slice(terms, (place * gain_len,), (gain_len,))
        bias_share = lax.dynamic_slice(terms, (gains + place * bias_len,), (bias_len,))
    else:
        dwqkv, input_grad, more = back(
            tokens, row_codes, col_codes, wa, q, k, v, dc, lse, dy1
        )
        terms = (terms + more).reshape(-1)
        shares = (
            scatter(ungroup_columns(dwqkv)),
            scatter(dwo[0]),
            scatter(dw1.transpose(1, 0, 2).reshape(D, FF)),
            scatter(dw2.reshape(FF, D)),
        )
        news = [
            update(shares[i], states[i], states[4 + i], states[8 + i], tokens_all)
            for i in range(4)
        ]
        masters, moments, averages = zip(*news)
        gain_share = scatter(terms[:gains])
        bias_share = scatter(terms[gains : gains + bias_len * devices])
    gain_new = update_steps(gain_share, gain_master, gain_moment, gain_average, tokens_all)
    bias_new = update(bias_share, bias_master, bias_moment, bias_average, tokens_all)
    return (
        layer_output, input_grad, *shares, gain_share, bias_share,
        *masters, gain_new[0], bias_new[0],
        *moments, gain_new[1], bias_new[1],
        *averages, gain_new[2], bias_new[2],
    )


def solution(mesh):
    both = ("gx", "gy")
    two, one = P(both, None), P(both)
    weights = (two, two, two, two, one, one)
    in_specs = (two, two, one, two) + weights * 3
    out_specs = (two, two) + weights * 4
    return jax.shard_map(
        on_device, mesh=mesh, in_specs=in_specs, out_specs=out_specs, check_vma=False
    )
```

```python
from functools import partial

import jax
import jax.numpy as jnp
from jax import lax
from jax.experimental import pallas as pl
from jax.experimental.pallas import tpu as pltpu
from jax.sharding import PartitionSpec as P

D = 768
HEADS = 12
HEAD_DIM = 64
FF = 3072
SEQ = 512
BAND = 128
PACK = 4
GROUPS = HEADS // PACK
WIDE = PACK * HEAD_DIM
VMEM = 60 * 1024 * 1024

norm_eps = 1e-06
momentum_coef = 0.9
learn_rate = 4.0
average_keep = 0.9

G1, G2, BQ, BV, BO, C1, B1, B2, C2 = (0, 1, 2, 3, 4, 5, 6, 10, 11)
TABLE = 16
CHUNK = 768
CHUNKS = 12
HALF = CHUNK // 2
MESH = pl.DeviceIdType.MESH

f32 = jnp.float32
bf16 = jnp.bfloat16

LOG2E = 1.4426950408889634
SCORE = HEAD_DIM ** (-0.5) * LOG2E


def nn(a, b):
    return lax.dot_general(a, b, (((1,), (0,)), ((), ())), preferred_element_type=f32)


def nt(a, b):
    return lax.dot_general(a, b, (((1,), (1,)), ((), ())), preferred_element_type=f32)


def tn(a, b):
    return lax.dot_general(a, b, (((0,), (0,)), ((), ())), preferred_element_type=f32)


def normal_cdf(u):
    gauss = jnp.exp2(u * u * (-0.5 * LOG2E))
    return 0.5 + 0.5 * lax.erf(u * 0.7071067811865476), gauss


def windows():
    for b in range(SEQ // BAND):
        first = max(0, (b - 1) * BAND)
        last = min(SEQ, (b + 2) * BAND)
        yield b, first, last - first


def head_masks():
    lane = lax.broadcasted_iota(jnp.int32, (BAND, WIDE), 1) // HEAD_DIM
    return [jnp.where(lane == h, 1.0, 0.0).astype(bf16) for h in range(PACK)]


def spread_heads(block, masks):
    return jnp.concatenate([block * m for m in masks], axis=0)


def pick_heads(wide):
    return jnp.concatenate(
        [
            wide[h * HEAD_DIM : (h + 1) * HEAD_DIM, h * BAND : (h + 1) * BAND]
            for h in range(PACK)
        ],
        axis=0,
    )


def mask_bias(col, row, b, first, width):
    keys = col[first : first + width, :]
    queries = row[0:1, b * BAND : (b + 1) * BAND]
    bias = jnp.where(keys == queries, 0.0, -1e30)
    return jnp.concatenate([bias] * PACK, axis=1)


def norm_stats(y):
    centre = jnp.mean(y, axis=-1, keepdims=True)
    centred = y - centre
    spread = jnp.mean(centred * centred, axis=-1, keepdims=True)
    r = lax.rsqrt(spread + norm_eps)
    return centred * r, r


def norm_back(dz, z, r):
    return r * (
        dz
        - jnp.mean(dz, axis=-1, keepdims=True)
        - z * jnp.mean(dz * z, axis=-1, keepdims=True)
    )


def remote(src, dst, send, recv, device):
    return pltpu.make_async_remote_copy(
        src_ref=src, dst_ref=dst, send_sem=send, recv_sem=recv, device_id=device,
        device_id_type=MESH,
    )


class Place:
    def __init__(self, nz):
        gx = lax.axis_index("gx")
        gy = lax.axis_index("gy")
        self.nz = nz
        self.x, self.y = gx % 2, gx // 2
        self.z, self.c = gy // 2, gy % 2
        x, y, z, c = self.x, self.y, self.z, self.c
        self.other = (gx, z * 2 + 1 - c)
        ax, ay = x + (1 - c) * (1 - 2 * x), y + c * (1 - 2 * y)
        bx, by = x + c * (1 - 2 * x), y + (1 - c) * (1 - 2 * y)
        self.first = (ay * 2 + ax, gy)
        self.second = (by * 2 + bx, gy)
        self.far = ((1 - y) * 2 + 1 - x, gy)
        self.quarter = gx
        self.quarter_first = ay * 2 + ax
        self.quarter_second = by * 2 + bx
        self.quarter_far = (1 - y) * 2 + 1 - x

    def along_z(self, j):
        return (self.quarter, (self.z + j) % self.nz * 2 + self.c)

    def greet(self):
        sem = pltpu.get_barrier_semaphore()
        partners = [self.other, self.first, self.second, self.far]
        partners += [self.along_z(j) for j in range(1, self.nz)]
        for p in partners:
            pl.semaphore_signal(sem, inc=1, device_id=p, device_id_type=MESH)

    def meet(self):
        pl.semaphore_wait(pltpu.get_barrier_semaphore(), 4 + self.nz - 1)


def fold_rows(v):
    n = v.shape[0]
    return jnp.sum(v.reshape(n // 8, 8, v.shape[1]), axis=0)


class Gather:
    TURNS = (0, 4, 7, 10, 12, 13)

    def __init__(self, nz, wa, wb, held, stage, z_sem, s_sem, own_sem, out_sem):
        self.at = Place(nz)
        self.nz, self.wa, self.wb, self.held, self.stage = nz, wa, wb, held, stage
        self.z_sem, self.s_sem, self.own_sem, self.out_sem = z_sem, s_sem, own_sem, out_sem

    def pump(self, s, half):
        for j in (5, 4, 3, 2, 1, 0):
            if self.TURNS[j] % 2 == half:
                k = s + 2 + (half - self.TURNS[j]) // 2
                pl.when((k >= 2) & (k < CHUNKS))(partial(self.act, j, k))

    def act(self, j, k):
        at, nz = self.at, self.nz
        direct = isinstance(k, int) and k == 0
        mine = pl.ds(pl.multiple_of(at.c * HALF, HALF), HALF)
        others = pl.ds(pl.multiple_of((1 - at.c) * HALF, HALF), HALF)

        def spot(chip, lanes=mine):
            return self.held.at[k, chip, :, lanes]

        def quarter(q):
            return spot(pl.ds(q * nz, nz))

        def z_copy(i, chip):
            return remote(
                self.stage.at[k], spot(chip), self.z_sem.at[0, k, i - 1],
                self.z_sem.at[1, k, i - 1], at.along_z(i),
            )

        def s_copy(i, q, device):
            return remote(
                quarter(q), quarter(q), self.s_sem.at[0, k, i], self.s_sem.at[1, k, i], device
            )

        def far_copy(q):
            if direct:
                return s_copy(2, at.quarter if q is None else q, at.far)
            return s_copy(2, at.quarter_first if q is None else q, at.second)

        def c_copy(lanes):
            whole = spot(slice(None), lanes)
            return remote(
                whole, whole, self.s_sem.at[0, k, 3], self.s_sem.at[1, k, 3], at.other
            )

        def own():
            return pltpu.make_async_copy(self.stage.at[k], spot(chip), self.own_sem.at[k])

        chip = at.quarter * nz + at.z
        if j == 0:
            for i in range(1, nz):
                z_copy(i, chip).start()
            own().start()
        elif j == 1:
            for i in range(1, nz):
                z_copy(i, at.quarter * nz + (at.z - i + nz) % nz).wait_recv()
            own().wait()
            s_copy(0, at.quarter, at.first).start()
            s_copy(1, at.quarter, at.second).start()
            if direct:
                far_copy(None).start()
        elif j == 2:
            s_copy(0, at.quarter_first, at.first).wait_recv()
            if not direct:
                far_copy(None).start()
        elif j == 3:
            s_copy(1, at.quarter_second, at.second).wait_recv()
            far_copy(at.quarter_far).wait_recv()
            c_copy(mine).start()
        elif j == 4:
            c_copy(others).wait_recv()
            for i in range(1, nz):
                z_copy(i, chip).wait_send()
            s_copy(0, at.quarter, at.first).wait_send()
            s_copy(1, at.quarter, at.second).wait_send()
            far_copy(None).wait_send()
            c_copy(mine).wait_send()
            self.keep(k, lambda copy: copy.start())
        else:
            self.keep(k, lambda copy: copy.wait())

    def keep(self, k, fn):
        def early():
            fn(pltpu.make_async_copy(self.held.at[k], self.wa.at[k], self.out_sem.at[k]))

        def late():
            fn(pltpu.make_async_copy(self.held.at[k], self.wb.at[:, k - 8], self.out_sem.at[k]))

        if isinstance(k, int):
            early()
        else:
            pl.when(k < 8)(early)
            pl.when(k >= 8)(late)


def share_start(nz, part_ref, masters, sibs, stage, table_ref, sums, got, x_sem, v_sem, gather):
    at = gather.at
    at.greet()
    at.meet()
    swaps = [
        remote(m, o, x_sem.at[0, i], x_sem.at[1, i], at.other)
        for i, (m, o) in enumerate(zip(masters, sibs))
    ]
    swaps.insert(1, remote(part_ref, got.at[0], x_sem.at[0, 4], x_sem.at[1, 4], at.other))
    for swap in swaps:
        swap.start()
    mq, mo, m1, m2 = masters
    sq, so, s1, s2 = sibs
    even = at.c == 0

    def halves(own, sib):
        own = jnp.where(even, own[:, :HALF], own[:, HALF:])
        sib = jnp.where(even, sib[:, :HALF], sib[:, HALF:])
        top, low = jnp.where(even, own, sib), jnp.where(even, sib, own)
        return jnp.concatenate([top, low], axis=0).astype(bf16)

    def group(ref, hg):
        cols = [ref[:, i * D + hg * WIDE : i * D + (hg + 1) * WIDE] for i in range(3)]
        return jnp.concatenate(cols, axis=1)

    def vec_copy(i, src, device):
        return remote(src, got.at[i], v_sem.at[0, i], v_sem.at[1, i], device)

    swaps[0].wait()
    for hg in range(GROUPS):
        stage[hg] = halves(group(mq, hg), group(sq, hg))
        if hg < 2:
            gather.act(0, hg)
    swaps[1].wait()
    sums[0] = part_ref[...] + got[0]
    z_copies = [vec_copy(i, sums.at[0], at.along_z(i)) for i in range(1, nz)]
    for copy in z_copies:
        copy.start()
    for swap in swaps[2:]:
        swap.wait()
    stage[3] = halves(mo[...], so[...])
    for f in range(4):
        cols = slice(f * CHUNK, (f + 1) * CHUNK)
        stage[4 + f] = halves(m1[:, cols], s1[:, cols])
    step = stage.shape[1]
    for i in range(4):
        rows = slice(i % 2 * step, (i % 2 + 1) * step)
        block = jnp.where(at.c == i // 2, m2[rows, :], s2[rows, :])
        stage[8 + i] = jnp.where(even, block[:, :HALF], block[:, HALF:]).astype(bf16)
    for copy in z_copies:
        copy.wait()
    total = sums[0]
    for i in range(1, nz):
        total = total + got[i]
    sums[1] = total
    near = [
        vec_copy(nz + i, sums.at[1], device)
        for i, device in enumerate((at.first, at.second, at.far))
    ]
    gather.act(1, 0)
    for copy in near:
        copy.start()
    gather.act(2, 0)
    gather.act(3, 0)
    for copy in near:
        copy.wait()
    table_ref[...] = (sums[1] + got[nz] + got[nz + 1] + got[nz + 2]).astype(f32)
    gather.act(4, 0)


def front_kernel(nz, *refs):
    refs = list(refs)
    x_ref, row_ref, col_ref, vec_ref = refs[:4]
    s = pl.program_id(0)
    att = GROUPS * 4
    if nz:
        masters, refs = refs[4:8], refs[8:]
    else:
        wa_ref, refs = refs[4], refs[5:]
    q_ref, k_ref, v_ref, lse_ref, c_ref, y1_ref, n1_ref, g_ref, gp_ref = refs[:9]
    refs = refs[9:]
    if nz:
        wa_ref, wb_ref, table_ref = refs[:3]
        c_all, held, stage, sq, so, s1, s2, sums, got = refs[3:12]
        z_sem, s_sem, own_sem, out_sem, x_sem, v_sem = refs[12:]
        gather = Gather(nz, wa_ref, wb_ref, held, stage, z_sem, s_sem, own_sem, out_sem)

        @pl.when(s == 0)
        def _():
            share_start(
                nz, vec_ref, masters, (sq, so, s1, s2), stage, table_ref, sums, got,
                x_sem, v_sem, gather,
            )

        for j in (1, 2, 3, 4, 5):
            pl.when(s == j - 1)(partial(gather.act, j, 1))
        pl.when(s == 2)(partial(gather.act, 5, 0))
        gather.pump(s, 0)
    else:
        c_all, held, load_sem = refs
        table_ref = vec_ref

        @pl.when(s == 0)
        def _():
            copy = pltpu.make_async_copy(wa_ref, held, load_sem)
            copy.start()
            copy.wait()

    def weight(k):
        return held[k].reshape(CHUNK, CHUNK)

    @pl.when(s < att)
    def _():
        hg = s // 4
        r = s % 4
        rows = pl.multiple_of(r * SEQ, SEQ)
        lanes = pl.multiple_of(hg * WIDE, WIDE)
        xr = x_ref[pl.ds(rows, SEQ), :]
        wqkv = weight(hg)
        q = nn(xr, wqkv[:, 0:WIDE]) + table_ref[BQ : BQ + 1, pl.ds(lanes, WIDE)]
        q = q.astype(bf16)
        k = nn(xr, wqkv[:, WIDE : 2 * WIDE]).astype(bf16)
        v = nn(xr, wqkv[:, 2 * WIDE :]) + table_ref[BV : BV + 1, pl.ds(lanes, WIDE)]
        v = v.astype(bf16)
        q_ref[...] = q
        k_ref[...] = k
        v_ref[...] = v
        vt = v.T
        masks = head_masks()
        for b, first, width in windows():
            if nz and b == 2:
                gather.pump(s, 1)
            qc = spread_heads(q[b * BAND : (b + 1) * BAND, :], masks)
            t = nt(k[first : first + width, :], qc) * SCORE
            t = t + mask_bias(col_ref.at[0], row_ref.at[0], b, first, width)
            m = jnp.max(t, axis=0, keepdims=True)
            e = jnp.exp2(t - m)
            l = jnp.sum(e, axis=0, keepdims=True)
            p = (e * (1.0 / l)).astype(bf16)
            lse_ref[0, b : b + 1, :] = m + jnp.log2(l)
            ot = nn(vt[:, first : first + width], p)
            c = pick_heads(ot).T.astype(bf16)
            c_all[pl.ds(rows + b * BAND, BAND), pl.ds(lanes, WIDE)] = c

    @pl.when(s >= att)
    def _():
        r = s - att
        rows = pl.multiple_of(r * SEQ, SEQ)
        c = c_all[pl.ds(rows, SEQ), :]
        c_ref[...] = c
        y1 = x_ref[pl.ds(rows, SEQ), :].astype(f32) + (
            nn(c, weight(3)) + table_ref[BO : BO + 1, :]
        )
        y1_ref[...] = y1
        z1, _ = norm_stats(y1)
        n1 = (z1 * table_ref[G1 : G1 + 1, :] + table_ref[C1 : C1 + 1, :]).astype(bf16)
        n1_ref[...] = n1
        for f in range(4):
            if nz and f == 2:
                gather.pump(s, 1)
            cols = slice(f * CHUNK, (f + 1) * CHUNK)
            u = nn(n1, weight(4 + f)) + table_ref[B1 + f : B1 + f + 1, :]
            cdf, gauss = normal_cdf(u)
            g_ref[:, cols] = (u * cdf).astype(bf16)
            gp_ref[:, cols] = (cdf + u * (gauss * 0.3989422804014327)).astype(bf16)


def constant(shape):
    return pl.BlockSpec(shape, lambda s: (0,) * len(shape), pipeline_mode=pl.Buffered(1))


def front(x, row_codes, col_codes, table, weights, chips=0):
    tokens = x.shape[0]
    rows = tokens // SEQ
    assert rows == 4
    att = GROUPS * rows
    nz = chips // 4

    def code_at(s):
        return (jnp.where(s < att, s % rows, rows - 1), 0, 0)

    def head_at(s):
        return (jnp.where(s < att, s % rows, rows - 1), jnp.minimum(s // rows, GROUPS - 1))

    def tile_at(s):
        return (jnp.maximum(s - att, 0), 0)

    anywhere = pl.BlockSpec(memory_space=pl.ANY)
    narrow = pl.BlockSpec((SEQ, D), tile_at)
    head = pl.BlockSpec((SEQ, WIDE), head_at)
    wide = pl.BlockSpec((SEQ, FF), tile_at)
    in_specs = [
        constant((tokens, D)),
        pl.BlockSpec((1, 8, SEQ), code_at),
        pl.BlockSpec((1, SEQ, BAND), code_at),
        constant((TABLE, CHUNK)),
    ]
    out_specs = [
        head, head, head,
        pl.BlockSpec((1, 8, PACK * BAND), lambda s: (jnp.minimum(s, att - 1), 0, 0)),
        narrow, narrow, narrow, wide, wide,
    ]
    low = jax.ShapeDtypeStruct((tokens, D), bf16)
    out_shape = [
        low, low, low,
        jax.ShapeDtypeStruct((att, 8, PACK * BAND), f32),
        low,
        jax.ShapeDtypeStruct((tokens, D), f32),
        low,
        jax.ShapeDtypeStruct((tokens, FF), bf16),
        jax.ShapeDtypeStruct((tokens, FF), bf16),
    ]
    if nz:
        step = CHUNK // chips
        in_specs += [constant(w.shape) for w in weights]
        out_specs += [anywhere, anywhere, pl.BlockSpec((TABLE, CHUNK), lambda s: (0, 0))]
        out_shape += [
            jax.ShapeDtypeStruct((8, chips, step, CHUNK), bf16),
            jax.ShapeDtypeStruct((chips, 4, step, CHUNK), bf16),
            jax.ShapeDtypeStruct((TABLE, CHUNK), f32),
        ]
        dma = pltpu.SemaphoreType.DMA
        scratch = [
            pltpu.VMEM((tokens, D), bf16),
            pltpu.VMEM((CHUNKS, chips, step, CHUNK), bf16),
            pltpu.VMEM((CHUNKS, step, HALF), bf16),
            *(pltpu.VMEM(w.shape, f32) for w in weights),
            pltpu.VMEM((2, TABLE, CHUNK), bf16),
            pltpu.VMEM((nz + 3, TABLE, CHUNK), bf16),
            dma((2, CHUNKS, nz - 1)), dma((2, CHUNKS, 4)), dma((CHUNKS,)), dma((CHUNKS,)),
            dma((2, 5)), dma((2, nz + 3)),
        ]
        params = pltpu.CompilerParams(
            vmem_limit_bytes=VMEM, collective_id=0, has_side_effects=True
        )
    else:
        in_specs.append(anywhere)
        scratch = [
            pltpu.VMEM((tokens, D), bf16),
            pltpu.VMEM(weights[0].shape, bf16),
            pltpu.SemaphoreType.DMA,
        ]
        params = pltpu.CompilerParams(vmem_limit_bytes=VMEM)
    return pl.pallas_call(
        partial(front_kernel, nz),
        grid=(att + rows,),
        in_specs=in_specs,
        out_specs=out_specs,
        out_shape=out_shape,
        scratch_shapes=scratch,
        compiler_params=params,
        name="front",
    )(x, row_codes, col_codes, table, *weights)


def middle_kernel(
    y1_ref, g_ref, gp_ref, cot_ref, vec_ref, wo_ref, w1_ref, w2_ref,
    out_ref, df_ref, du_ref, dy1_ref, da_ref, dc_ref, grads_ref, sums_ref, ups_ref,
):
    s = pl.program_id(0)

    @pl.when(s == 0)
    def _():
        sums_ref[...] = jnp.zeros_like(sums_ref)
        ups_ref[...] = jnp.zeros_like(ups_ref)

    z1, r1 = norm_stats(y1_ref[...])
    gain1 = vec_ref[G1 : G1 + 1, :]
    gain2 = vec_ref[G2 : G2 + 1, :]
    n1 = z1 * gain1 + vec_ref[C1 : C1 + 1, :]
    y2 = n1 + (nn(g_ref[...], w2_ref[...]) + vec_ref[B2 : B2 + 1, :])
    z2, r2 = norm_stats(y2)
    out_ref[...] = (z2 * gain2 + vec_ref[C2 : C2 + 1, :]).astype(bf16)
    e = cot_ref[...].astype(f32)
    sums_ref[0] += fold_rows(e * z2)
    sums_ref[1] += fold_rows(e)
    dy2 = norm_back(e * gain2, z2, r2)
    df = dy2.astype(bf16)
    df_ref[...] = df
    sums_ref[2] += fold_rows(df.astype(f32))
    step = 768
    for f in range(0, FF, step):
        dg = nt(df, w2_ref[f : f + step, :])
        du = (dg * gp_ref[:, f : f + step].astype(f32)).astype(bf16)
        du_ref[:, f : f + step] = du
        ups_ref[:, f : f + step] += fold_rows(du.astype(f32))
    dn1 = dy2
    for f in range(4):
        dn1 = dn1 + nt(du_ref[:, f * CHUNK : (f + 1) * CHUNK], w1_ref[f])
    sums_ref[3] += fold_rows(dn1 * z1)
    sums_ref[4] += fold_rows(dn1)
    dy1 = norm_back(dn1 * gain1, z1, r1)
    dy1_ref[...] = dy1
    da = dy1.astype(bf16)
    da_ref[...] = da
    sums_ref[5] += fold_rows(da.astype(f32))
    dc_ref[...] = nt(da, wo_ref[0]).astype(bf16)

    @pl.when(s == pl.num_programs(0) - 1)
    def _():
        grads_ref[...] = jnp.zeros_like(grads_ref)
        for i, row in enumerate((G2, C2, B2, G1, C1, BO)):
            grads_ref[row : row + 1, :] = jnp.sum(sums_ref[i], axis=0, keepdims=True)
        for f in range(4):
            cols = slice(f * CHUNK, (f + 1) * CHUNK)
            grads_ref[B1 + f : B1 + f + 1, :] = jnp.sum(ups_ref[:, cols], axis=0, keepdims=True)


def chunks_at(count, index):
    return pl.BlockSpec(
        (count, CHUNK, CHUNK), lambda s: (index, 0, 0), pipeline_mode=pl.Buffered(1)
    )


def middle(y1, g, gp, cot, table, wa, w2):
    tokens = y1.shape[0]
    tile = SEQ

    narrow = pl.BlockSpec((tile, D), lambda s: (s, 0))
    wide = pl.BlockSpec((tile, FF), lambda s: (s, 0))
    wide_out = pl.BlockSpec((tile, FF), lambda s: (s, 0))
    return pl.pallas_call(
        middle_kernel,
        grid=(tokens // tile,),
        in_specs=[
            narrow, wide, wide, narrow, constant((TABLE, CHUNK)),
            chunks_at(1, 3), chunks_at(4, 1), constant((FF, D)),
        ],
        out_specs=[
            narrow, narrow, wide_out, narrow, narrow, narrow,
            pl.BlockSpec((TABLE, CHUNK), lambda s: (0, 0)),
        ],
        out_shape=[
            jax.ShapeDtypeStruct((tokens, D), bf16),
            jax.ShapeDtypeStruct((tokens, D), bf16),
            jax.ShapeDtypeStruct((tokens, FF), bf16),
            jax.ShapeDtypeStruct((tokens, D), f32),
            jax.ShapeDtypeStruct((tokens, D), bf16),
            jax.ShapeDtypeStruct((tokens, D), bf16),
            jax.ShapeDtypeStruct((TABLE, CHUNK), f32),
        ],
        scratch_shapes=[pltpu.VMEM((6, 8, D), f32), pltpu.VMEM((8, FF), f32)],
        compiler_params=pltpu.CompilerParams(vmem_limit_bytes=VMEM),
        name="middle",
    )(y1, g, gp, cot, table, wa, wa, w2)


DOWN, UP, PROJ, QKV = 0, 4, 8, 9
OUTERS = 9


class Reduce:
    def __init__(self, nz, grads, made, local, bufs, fin, outs, sems):
        self.at = Place(nz)
        self.nz, self.grads, self.made, self.local = nz, grads, made, local
        self.bufs, self.fin, self.outs = bufs, fin, outs
        self.c_sem, self.l_sem, self.q_sem, self.z_sem, self.f_sem = sems

    TURNS = (0, 2, 6, 10, 15, 17)
    LATE_TURNS = (0, 2, 5, 8, 12, 14)

    def pump(self, s, half):
        for j in (5, 4, 3, 2, 1, 0):
            if self.TURNS[j] % 2 != half:
                r = s + (half - 9 - self.TURNS[j]) // 2
                pl.when((r >= 0) & (r < QKV))(partial(self.act, j, r))

        @pl.when(s >= 13)
        def _():
            for hg, start, turns in ((0, 27, self.TURNS), (1, 35, self.LATE_TURNS)):
                for j in range(6):
                    turn = start + turns[j]
                    if turn % 2 == half:
                        pl.when(s == turn // 2)(partial(self.act, j, QKV + hg))

    def source(self, r, lanes, fn):
        g2, g19 = self.grads
        if isinstance(r, int):
            fn(self.made.at[r - QKV, :, :, :, lanes])
            return
        pl.when(r < UP)(lambda: fn(g2.at[:, :, r, :, lanes]))
        pl.when(r >= UP)(lambda: fn(g19.at[r - UP, :, :, :, lanes]))

    def act(self, j, r):
        at, nz = self.at, self.nz
        r0, r1, r2, r3 = self.bufs
        fin, got = self.fin
        c, x, y, z = at.c, at.x, at.y, at.z
        half = [pl.ds(pl.multiple_of(i * HALF, HALF), HALF) for i in (c, 1 - c)]

        def c_copy(src):
            return remote(src, r0.at[r], self.c_sem.at[0, r], self.c_sem.at[1, r], at.other)

        def l_copy(src):
            return pltpu.make_async_copy(src, self.local.at[r % 2], self.l_sem.at[r % 2])

        def a_copy(i):
            q = (1 - c) * (2 * i + 1 - x) + c * (2 * (1 - y) + i)
            return remote(
                r0.at[r, q], r1.at[r, i],
                self.q_sem.at[0, r, i], self.q_sem.at[1, r, i], at.first,
            )

        keep = (1 - c) * y + c * x

        def b_copy():
            return remote(
                r1.at[r, 1 - keep], r2.at[r],
                self.q_sem.at[0, r, 2], self.q_sem.at[1, r, 2], at.second,
            )

        def z_copy(i):
            return remote(
                r2.at[r, (z + i) % nz], r3.at[r, i - 1],
                self.z_sem.at[0, r, i - 1], self.z_sem.at[1, r, i - 1], at.along_z(i),
            )

        def f_copy():
            return remote(fin.at[r], got.at[r], self.f_sem.at[0, r], self.f_sem.at[1, r], at.other)

        rows = fin.shape[1] // 2
        if j == 0:
            self.source(r, half[1], lambda src: c_copy(src).start())
            if not isinstance(r, int):
                self.source(r, half[0], lambda src: l_copy(src).start())
        elif j == 1:
            if isinstance(r, int):
                c_copy(self.made.at[r - QKV, :, :, :, half[1]]).wait()
                own = self.made.at[r - QKV]
                mine = jnp.where(c == 0, own[:, :, :, :HALF], own[:, :, :, HALF:])
            else:
                self.source(r, half[1], lambda src: c_copy(src).wait())
                self.source(r, half[0], lambda src: l_copy(src).wait())
                mine = self.local[r % 2]
            r0[r] = r0[r] + mine
            a_copy(0).start()
            a_copy(1).start()
        elif j == 2:
            for i in (0, 1):
                a_copy(i).wait()
                q = (1 - c) * (2 * i + x) + c * (2 * y + i)
                r1[r, i] = r1[r, i] + r0[r, q]
            b_copy().start()
        elif j == 3:
            b_copy().wait()
            r2[r] = r2[r] + r1[r, keep]
            for i in range(1, nz):
                z_copy(i).start()
        elif j == 4:
            total = r2[r, z].astype(f32)
            for i in range(1, nz):
                z_copy(i).wait()
                total = total + r3[r, i - 1].astype(f32)
            fin[r] = total
            f_copy().start()
        else:
            f_copy().wait()
            self.finish(r, rows)

    def finish(self, r, rows):
        c = self.at.c
        fin, got = self.fin
        out, out_down = self.outs
        even = c == 0

        def sides(own, other):
            return jnp.concatenate(
                [jnp.where(even, own, other), jnp.where(even, other, own)], axis=1
            )

        def down():
            @pl.when(c == r // 2)
            def _():
                out_down[r % 2] = sides(fin[r], got[r])

        def rest():
            own = jnp.where(even, fin[r, :rows, :], fin[r, rows:, :])
            other = jnp.where(even, got[r, :rows, :], got[r, rows:, :])
            out[r - UP] = sides(own, other)

        if isinstance(r, int):
            rest()
        else:
            pl.when(r < UP)(down)
            pl.when(r >= UP)(rest)


def back_kernel(comm, nz, *refs):
    (
        x_hbm, row_ref, col_ref, wa_hbm, q_ref, k_ref, v_ref, dc_ref, lse_ref, dy1_ref, table_ref,
        g_hbm, df_hbm, n1_hbm, du_hbm, c_hbm, da_hbm,
        g2_hbm, g19_hbm, out, out_down, total_ref, dx_ref,
        x_ref, wqkv_ref, work, res, made, dk_sum, dv_sum, qv_sum, in_sem, res_sem,
    ) = refs[:33]
    s = pl.program_id(0)
    att = GROUPS * 4
    end = OUTERS + att
    if comm:
        local, r0, r1, r2, r3, fin, got, mine, came = refs[33:42]
        sems, v_sem = refs[42:47], refs[47]
        reduce = Reduce(
            nz, (g2_hbm, g19_hbm), made, local, (r0, r1, r2, r3), (fin, got), (out, out_down), sems
        )
        at = reduce.at

        pl.when(s == 0)(at.greet)
        pl.when(s == 4)(at.meet)

    def pump(half):
        if half == 1:
            pl.when((s >= 1) & (s <= OUTERS))(lambda: store(s - 1, lambda copy: copy.wait()))
        if comm:
            reduce.pump(s, half)

    def bring(src, dst, i):
        return pltpu.make_async_copy(src, dst, in_sem.at[i])

    def stream(i, fn):
        cols = pl.ds(pl.multiple_of(i % 4 * CHUNK, CHUNK), CHUNK)
        slot = i % 2
        pl.when(i < 4)(lambda: fn(bring(g_hbm.at[:, cols], work.at[slot], slot)))
        pl.when((i >= 4) & (i < 8))(lambda: fn(bring(du_hbm.at[:, cols], work.at[slot], slot)))
        pl.when(i == 8)(lambda: fn(bring(c_hbm, work.at[slot], slot)))

    def store(i, fn):
        slot = i % 2
        pl.when(i < 4)(
            lambda: fn(pltpu.make_async_copy(res.at[slot], g2_hbm.at[i], res_sem.at[slot]))
        )
        pl.when(i >= 4)(
            lambda: fn(pltpu.make_async_copy(res.at[slot], g19_hbm.at[i - 4], res_sem.at[slot]))
        )

    whole_df, whole_da = bring(df_hbm, work.at[2], 2), bring(da_hbm, work.at[2], 2)
    whole_n1 = bring(n1_hbm, work.at[3], 3)
    whole_x = bring(x_hbm, x_ref, 4)
    whole_w = bring(wa_hbm.at[0:GROUPS], wqkv_ref, 5)

    @pl.when(s == 0)
    def _():
        stream(s, lambda copy: copy.start())
        whole_df.start()
        stream(s + 1, lambda copy: copy.start())
        whole_n1.start()
        whole_df.wait()
        qv_sum[...] = jnp.zeros_like(qv_sum)

    pump(0)

    @pl.when(s < OUTERS)
    def _():
        stream(s, lambda copy: copy.wait())
        pl.when(s == 4)(lambda: whole_n1.wait())
        pl.when(s == 8)(lambda: whole_da.wait())
        part = CHUNK // 2

        def piece(h):
            @pl.when((s < 4) | (s == 8))
            def _():
                left = work[s % 2, :, h * part : (h + 1) * part]
                put(h, tn(left, work[2]))

            @pl.when((s >= 4) & (s < 8))
            def _():
                put(h, tn(work[3, :, h * part : (h + 1) * part], work[s % 2]))

        def put(h, product):
            shape = (2, *res.shape[2:])
            res[s % 2, 2 * h : 2 * h + 2] = product.astype(bf16).reshape(shape)

        piece(0)
        pump(1)
        piece(1)
        store(s, lambda copy: copy.start())
        pl.when(s < OUTERS - 2)(lambda: stream(s + 2, lambda copy: copy.start()))
        pl.when(s == 3)(lambda: whole_da.start())

        @pl.when(s == 2)
        def _():
            whole_x.start()
            whole_w.start()

        @pl.when(s == OUTERS - 1)
        def _():
            whole_x.wait()
            whole_w.wait()

    @pl.when((s >= OUTERS) & (s < end))
    def _():
        hg = (s - OUTERS) // 4
        r = (s - OUTERS) % 4
        rows = pl.multiple_of(r * SEQ, SEQ)
        lanes = pl.ds(pl.multiple_of(hg * WIDE, WIDE), WIDE)
        kt = k_ref[...].T
        dk_sum[...] = jnp.zeros_like(dk_sum)
        dv_sum[...] = jnp.zeros_like(dv_sum)
        masks = head_masks()
        for b, first, width in windows():
            if b == 2:
                pump(1)
            block = slice(b * BAND, (b + 1) * BAND)
            span = slice(first, first + width)
            qc = spread_heads(q_ref[block, :], masks)
            dcc = spread_heads(dc_ref[block, :], masks)
            t = nt(k_ref[span, :], qc) * SCORE
            t = t + mask_bias(col_ref.at[0], row_ref.at[0], b, first, width)
            p = jnp.exp2(t - lse_ref[0, b : b + 1, :])
            dp = nt(v_ref[span, :], dcc)
            dv_sum[span, :] += nn(p.astype(bf16), dcc)
            pdp = p * dp
            weighted = jnp.sum(pdp, axis=0, keepdims=True)
            ds = (pdp - p * weighted).astype(bf16)
            dk_sum[span, :] += nn(ds, qc)
            dqt = nn(kt[:, span], ds)
            dq = (pick_heads(dqt).T * HEAD_DIM ** (-0.5)).astype(bf16)
            work[hg, pl.ds(rows + b * BAND, BAND), 0:WIDE] = dq
            qv_sum[0, :, lanes] += fold_rows(dq.astype(f32))
        dk = (dk_sum[...] * HEAD_DIM ** (-0.5)).astype(bf16)
        dv = dv_sum[...].astype(bf16)
        work[hg, pl.ds(rows, SEQ), WIDE : 2 * WIDE] = dk
        work[hg, pl.ds(rows, SEQ), 2 * WIDE :] = dv
        qv_sum[1, :, lanes] += fold_rows(dv.astype(f32))

        @pl.when(r == 3)
        def _():
            made[hg] = tn(x_ref[...], work[hg]).astype(bf16).reshape(made.shape[1:])

    last = QKV + GROUPS - 1
    if comm:
        def vec_copy(i, src, device):
            return remote(src, came.at[i], v_sem.at[0, i], v_sem.at[1, i], device)

        c_copy = vec_copy(0, mine.at[0], at.other)
        z_copies = [vec_copy(i, mine.at[1], at.along_z(i)) for i in range(1, nz)]
        near = [
            vec_copy(nz + i, mine.at[2], device)
            for i, device in enumerate((at.first, at.second, at.far))
        ]

        @pl.when(s == end - 1)
        def _():
            reduce.act(0, last)
            mine[0] = table_ref[...]
            mine[0, BQ : BQ + 1, :] = jnp.sum(qv_sum[0], axis=0, keepdims=True)
            mine[0, BV : BV + 1, :] = jnp.sum(qv_sum[1], axis=0, keepdims=True)
            c_copy.start()

        @pl.when(s == end)
        def _():
            reduce.act(1, last)
            c_copy.wait()
            mine[1] = mine[0] + came[0]
            for copy in z_copies:
                copy.start()

        @pl.when(s == end + 1)
        def _():
            reduce.act(3, last)
            total = mine[1]
            for i in range(1, nz):
                z_copies[i - 1].wait()
                total = total + came[i]
            mine[2] = total
            for copy in near:
                copy.start()

    @pl.when(s >= end)
    def _():
        half = SEQ // 2
        for h in range(2):
            if h == 1:
                pump(1)
                if comm:
                    pl.when(s == end)(lambda: reduce.act(2, last))
                    pl.when(s == end + 1)(lambda: reduce.act(4, last))
            rows = pl.ds(pl.multiple_of((s - end) * SEQ + h * half, half), half)
            total = dy1_ref[h * half : (h + 1) * half, :]
            for hg in range(GROUPS):
                total = total + nt(work[hg, rows, :], wqkv_ref[hg].reshape(CHUNK, CHUNK))
            dx_ref[h * half : (h + 1) * half, :] = total

    @pl.when(s == end + 3)
    def _():
        if comm:
            for copy in near:
                copy.wait()
            total_ref[...] = mine[2] + came[nz] + came[nz + 1] + came[nz + 2]
            reduce.act(5, last)
        else:
            total_ref[...] = table_ref[...]
            total_ref[BQ : BQ + 1, :] = jnp.sum(qv_sum[0], axis=0, keepdims=True)
            total_ref[BV : BV + 1, :] = jnp.sum(qv_sum[1], axis=0, keepdims=True)
            out[...] = jnp.zeros_like(out)
            out_down[...] = jnp.zeros_like(out_down)


def back(x, row_codes, col_codes, wa, q, k, v, dc, lse, dy1, table, pairs, chips, comm):
    tokens = x.shape[0]
    rows = tokens // SEQ
    att = GROUPS * rows
    end = OUTERS + att
    assert rows == 4
    nz = chips // 4
    step = CHUNK // chips

    def turn(s):
        return jnp.clip(s - OUTERS, 0, att - 1)

    def code_at(s):
        return (turn(s) % rows, 0, 0)

    def head_at(s):
        return (turn(s) % rows, turn(s) // rows)

    def tile_at(s):
        return (jnp.maximum(s - end, 0), 0)

    anywhere = pl.BlockSpec(memory_space=pl.ANY)
    whole_table = pl.BlockSpec((TABLE, CHUNK), lambda s: (0, 0))
    head = pl.BlockSpec((SEQ, WIDE), head_at)
    tile = pl.BlockSpec((SEQ, D), tile_at)
    made_shape = (GROUPS, 4, nz, step, CHUNK)
    dma = pltpu.SemaphoreType.DMA
    scratch = [
        pltpu.VMEM((tokens, D), bf16),
        pltpu.VMEM((GROUPS, *wa.shape[1:]), bf16),
        pltpu.VMEM((4, tokens, CHUNK), bf16),
        pltpu.VMEM((2, 4, nz, step, CHUNK), bf16),
    ]
    if comm:
        scratch.append(pltpu.VMEM(made_shape, bf16))
    scratch += [
        pltpu.VMEM((SEQ, WIDE), f32),
        pltpu.VMEM((SEQ, WIDE), f32),
        pltpu.VMEM((2, 8, D), f32),
        dma((6,)), dma((2,)),
    ]
    out_specs = [
        anywhere, anywhere,
        pl.BlockSpec((8, step // 2, CHUNK), lambda s: (0, 0, 0)),
        pl.BlockSpec((2, step, CHUNK), lambda s: (0, 0, 0)),
        whole_table, tile,
    ]
    out_shape = [
        jax.ShapeDtypeStruct((4, nz, 4, step, CHUNK), bf16),
        jax.ShapeDtypeStruct((5, 4, nz, step, CHUNK), bf16),
        jax.ShapeDtypeStruct((8, step // 2, CHUNK), f32),
        jax.ShapeDtypeStruct((2, step, CHUNK), f32),
        jax.ShapeDtypeStruct((TABLE, CHUNK), f32),
        jax.ShapeDtypeStruct((tokens, D), f32),
    ]
    kernel = partial(back_kernel, comm, nz)
    if comm:
        scratch += [
            pltpu.VMEM((2, 4, nz, step, HALF), bf16),
            pltpu.VMEM((CHUNKS, 4, nz, step, HALF), bf16),
            pltpu.VMEM((CHUNKS, 2, nz, step, HALF), bf16),
            pltpu.VMEM((CHUNKS, nz, step, HALF), bf16),
            pltpu.VMEM((CHUNKS, nz - 1, step, HALF), bf16),
            pltpu.VMEM((CHUNKS, step, HALF), f32),
            pltpu.VMEM((CHUNKS, step, HALF), f32),
            pltpu.VMEM((3, TABLE, CHUNK), f32),
            pltpu.VMEM((nz + 3, TABLE, CHUNK), f32),
            dma((2, CHUNKS)), dma((2,)), dma((2, CHUNKS, 3)), dma((2, CHUNKS, nz - 1)),
            dma((2, CHUNKS)), dma((2, nz + 3)),
        ]
        params = pltpu.CompilerParams(
            vmem_limit_bytes=VMEM, collective_id=1, has_side_effects=True
        )
    else:
        def kernel(*refs):
            refs = list(refs)
            made = refs.pop(23)
            refs.insert(27, made)
            back_kernel(comm, nz, *refs)

        out_specs.append(pl.BlockSpec(made_shape, lambda s: (0,) * 5, pipeline_mode=pl.Buffered(1)))
        out_shape.append(jax.ShapeDtypeStruct(made_shape, bf16))
        params = pltpu.CompilerParams(vmem_limit_bytes=VMEM)
    return pl.pallas_call(
        kernel,
        grid=(end + rows,),
        in_specs=[
            anywhere,
            pl.BlockSpec((1, 8, SEQ), code_at),
            pl.BlockSpec((1, SEQ, BAND), code_at),
            anywhere,
            head, head, head, head,
            pl.BlockSpec((1, 8, PACK * BAND), lambda s: (turn(s), 0, 0)),
            tile, whole_table,
            *(anywhere for _ in pairs),
        ],
        out_specs=out_specs,
        out_shape=out_shape,
        scratch_shapes=scratch,
        compiler_params=params,
        name="back",
    )(x, row_codes, col_codes, wa, q, k, v, dc, lse, dy1, table, *pairs)


def update(grad, master, moment, average, tokens_all):
    mean_grad = grad / tokens_all
    moment_new = momentum_coef * moment + mean_grad
    step_size = -learn_rate * (mean_grad + momentum_coef * moment_new)
    master_new = master + step_size
    average_new = average_keep * average + (1.0 - average_keep) * master_new
    return (master_new, moment_new, average_new)


def update_steps(grad, master, moment, average, tokens_all):
    mean_grad = grad / tokens_all
    moment_new = momentum_coef * moment + mean_grad
    step_size = -learn_rate * (mean_grad + momentum_coef * moment_new)
    average_step = (1.0 - average_keep) * (master + step_size - average)
    return (step_size, moment_new, average_step)


def update_kernel(tokens_all, *refs):
    grad_ref, down_ref = refs[:2]
    states, outs = refs[2:14], refs[14:]

    def one(i, index, grad):
        master, moment, average = (states[i + 4 * j][index] for j in range(3))
        outs[i][index] = grad
        new = update(grad, master, moment, average, tokens_all)
        for j in range(3):
            outs[i + 4 * (j + 1)][index] = new[j]

    rows = grad_ref.shape[1]
    for hg in range(GROUPS):
        for i in range(3):
            cols = slice(i * D + hg * WIDE, i * D + (hg + 1) * WIDE)
            one(0, (slice(None), cols), grad_ref[5 + hg, :, i * WIDE : (i + 1) * WIDE])
    one(1, (slice(None), slice(None)), grad_ref[4])
    for f in range(4):
        one(2, (slice(None), slice(f * CHUNK, (f + 1) * CHUNK)), grad_ref[f])
    for i in range(2):
        one(3, (slice(2 * rows * i, 2 * rows * (i + 1)), slice(None)), down_ref[i])


def update_weights(grads, grads_down, states, tokens_all):
    whole = pl.BlockSpec(memory_space=pltpu.VMEM)
    shapes = [jax.ShapeDtypeStruct(w.shape, f32) for w in states[:4]]
    return pl.pallas_call(
        partial(update_kernel, tokens_all),
        in_specs=[whole] * 14,
        out_specs=[whole] * 16,
        out_shape=shapes * 4,
        compiler_params=pltpu.CompilerParams(vmem_limit_bytes=VMEM),
        name="update",
    )(grads, grads_down, *states)


def group_columns(w):
    n = w.shape[0]
    return w.reshape(n, 3, GROUPS, WIDE).transpose(2, 0, 1, 3).reshape(GROUPS, n, 3 * WIDE)


def ungroup_columns(w):
    n = w.shape[1]
    return w.reshape(GROUPS, n, 3, WIDE).transpose(1, 2, 0, 3).reshape(n, 3 * D)


def table_of(gains, biases):
    flat = jnp.concatenate([gains, biases, jnp.zeros((TABLE * CHUNK - 9216,), gains.dtype)])
    return flat.reshape(TABLE, CHUNK)


def on_device(
    tokens, segment_ids, pad_counts, out_cotangent,
    qkv_master, proj_master, up_master, down_master, gain_master, bias_master,
    qkv_moment, proj_moment, up_moment, down_moment, gain_moment, bias_moment,
    qkv_average, proj_average, up_average, down_average, gain_average, bias_average,
):
    axes = ("gx", "gy")
    devices = lax.axis_size(axes)
    seq_len = segment_ids.shape[1]
    tokens_all = tokens.shape[0] * devices
    position = jnp.arange(seq_len, dtype=jnp.int32)
    is_pad = position[None, :] >= (seq_len - pad_counts)[:, None]
    codes = segment_ids * 2 + is_pad.astype(jnp.int32)
    row_codes = jnp.broadcast_to(codes[:, None, :], (codes.shape[0], 8, seq_len))
    col_codes = jnp.broadcast_to(codes[:, :, None], (codes.shape[0], seq_len, BAND))
    gain_len, bias_len = gain_master.shape[0], bias_master.shape[0]
    gains = gain_len * devices
    place = lax.axis_index(axes)

    fine = lax.axis_size("gx") == 4 and lax.axis_size("gy") == 8
    if fine:
        chips = devices // 2
        part = jnp.zeros((TABLE * CHUNK,), bf16)
        part = lax.dynamic_update_slice(part, gain_master.astype(bf16), (place * gain_len,))
        part = lax.dynamic_update_slice(
            part, bias_master.astype(bf16), (gains + place * bias_len,)
        ).reshape(TABLE, CHUNK)
        q, k, v, lse, c, y1, n1, g, gp, wa, w2, table = front(
            tokens, row_codes, col_codes, part,
            (qkv_master, proj_master, up_master, down_master), chips,
        )
        w2 = w2.reshape(FF, D)
    else:
        gather = partial(lax.all_gather, axis_name=axes, axis=0, tiled=True)
        w1 = gather(up_master.astype(bf16))
        wa = jnp.concatenate(
            [
                group_columns(gather(qkv_master.astype(bf16))),
                gather(proj_master.astype(bf16))[None],
                w1.reshape(D, 4, CHUNK).transpose(1, 0, 2),
            ]
        ).reshape(8, 16, CHUNK // 16, CHUNK)
        w2 = gather(down_master.astype(bf16))
        table = table_of(
            gather(gain_master.astype(bf16)), gather(bias_master.astype(bf16))
        ).astype(f32)
        q, k, v, lse, c, y1, n1, g, gp = front(
            tokens, row_codes, col_codes, table, (wa,)
        )
    layer_output, df, du, dy1, da, dc, terms = middle(
        y1, g, gp, out_cotangent, table, wa.reshape(8, CHUNK, CHUNK), w2
    )
    results = back(
        tokens, row_codes, col_codes, wa, q, k, v, dc, lse, dy1, terms,
        (g, df, n1, du, c, da), chips if fine else 16, fine,
    )
    input_grad = results[5]
    scatter = partial(lax.psum_scatter, axis_name=axes, scatter_dimension=0, tiled=True)
    states = (
        qkv_master, proj_master, up_master, down_master,
        qkv_moment, proj_moment, up_moment, down_moment,
        qkv_average, proj_average, up_average, down_average,
    )
    if fine:
        grads, grads_down, terms = results[2:5]
        new = update_weights(grads, grads_down, states, tokens_all)
        shares, masters, moments, averages = new[:4], new[4:8], new[8:12], new[12:]
        terms = terms.reshape(-1)
        gain_share = lax.dynamic_slice(terms, (place * gain_len,), (gain_len,))
        bias_share = lax.dynamic_slice(terms, (gains + place * bias_len,), (bias_len,))
    else:
        down_part, rest, terms, dwqkv = (results[i].astype(f32) for i in (0, 1, 4, 6))
        rest = rest.reshape(5, CHUNK, CHUNK)
        terms = terms.reshape(-1)
        shares = (
            scatter(ungroup_columns(dwqkv.reshape(GROUPS, CHUNK, CHUNK))),
            scatter(rest[4]),
            scatter(rest[:4].transpose(1, 0, 2).reshape(D, FF)),
            scatter(down_part.reshape(FF, D)),
        )
        news = [
            update(shares[i], states[i], states[4 + i], states[8 + i], tokens_all)
            for i in range(4)
        ]
        masters, moments, averages = zip(*news)
        gain_share = scatter(terms[:gains])
        bias_share = scatter(terms[gains : gains + bias_len * devices])
    gain_new = update_steps(gain_share, gain_master, gain_moment, gain_average, tokens_all)
    bias_new = update(bias_share, bias_master, bias_moment, bias_average, tokens_all)
    return (
        layer_output, input_grad, *shares, gain_share, bias_share,
        *masters, gain_new[0], bias_new[0],
        *moments, gain_new[1], bias_new[1],
        *averages, gain_new[2], bias_new[2],
    )


def solution(mesh):
    both = ("gx", "gy")
    two, one = P(both, None), P(both)
    weights = (two, two, two, two, one, one)
    in_specs = (two, two, one, two) + weights * 3
    out_specs = (two, two) + weights * 4
    return jax.shard_map(
        on_device, mesh=mesh, in_specs=in_specs, out_specs=out_specs, check_vma=False
    )
```

```python
from functools import partial

import jax
import jax.numpy as jnp
from jax import lax
from jax.experimental import pallas as pl
from jax.experimental.pallas import tpu as pltpu
from jax.sharding import PartitionSpec as P

D = 768
HEADS = 12
HEAD_DIM = 64
FF = 3072
SEQ = 512
BAND = 128
PACK = 4
GROUPS = HEADS // PACK
WIDE = PACK * HEAD_DIM
VMEM = 60 * 1024 * 1024

norm_eps = 1e-06
momentum_coef = 0.9
learn_rate = 4.0
average_keep = 0.9

G1, G2, BQ, BV, BO, C1, B1, B2, C2 = (0, 1, 2, 3, 4, 5, 6, 10, 11)
TABLE = 16
CHUNK = 768
CHUNKS = 12
HALF = CHUNK // 2
MESH = pl.DeviceIdType.MESH

f32 = jnp.float32
bf16 = jnp.bfloat16

LOG2E = 1.4426950408889634
SCORE = HEAD_DIM ** (-0.5) * LOG2E


def nn(a, b):
    return lax.dot_general(a, b, (((1,), (0,)), ((), ())), preferred_element_type=f32)


def nt(a, b):
    return lax.dot_general(a, b, (((1,), (1,)), ((), ())), preferred_element_type=f32)


def tn(a, b):
    return lax.dot_general(a, b, (((0,), (0,)), ((), ())), preferred_element_type=f32)


def normal_cdf(u):
    gauss = jnp.exp2(u * u * (-0.5 * LOG2E))
    return 0.5 + 0.5 * lax.erf(u * 0.7071067811865476), gauss


def windows():
    for b in range(SEQ // BAND):
        first = max(0, (b - 1) * BAND)
        last = min(SEQ, (b + 2) * BAND)
        yield b, first, last - first


def head_masks():
    lane = lax.broadcasted_iota(jnp.int32, (BAND, WIDE), 1) // HEAD_DIM
    return [jnp.where(lane == h, 1.0, 0.0).astype(bf16) for h in range(PACK)]


def spread_heads(block, masks):
    return jnp.concatenate([block * m for m in masks], axis=0)


def pick_heads(wide):
    return jnp.concatenate(
        [
            wide[h * HEAD_DIM : (h + 1) * HEAD_DIM, h * BAND : (h + 1) * BAND]
            for h in range(PACK)
        ],
        axis=0,
    )


def mask_bias(col, row, b, first, width):
    keys = col[first : first + width, :]
    queries = row[0:1, b * BAND : (b + 1) * BAND]
    bias = jnp.where(keys == queries, 0.0, -1e30)
    return jnp.concatenate([bias] * PACK, axis=1)


def norm_stats(y):
    centre = jnp.mean(y, axis=-1, keepdims=True)
    centred = y - centre
    spread = jnp.mean(centred * centred, axis=-1, keepdims=True)
    r = lax.rsqrt(spread + norm_eps)
    return centred * r, r


def norm_back(dz, z, r):
    return r * (
        dz
        - jnp.mean(dz, axis=-1, keepdims=True)
        - z * jnp.mean(dz * z, axis=-1, keepdims=True)
    )


def remote(src, dst, send, recv, device):
    return pltpu.make_async_remote_copy(
        src_ref=src, dst_ref=dst, send_sem=send, recv_sem=recv, device_id=device,
        device_id_type=MESH,
    )


class Place:
    def __init__(self, nz):
        gx = lax.axis_index("gx")
        gy = lax.axis_index("gy")
        self.nz = nz
        self.x, self.y = gx % 2, gx // 2
        self.z, self.c = gy // 2, gy % 2
        x, y, z, c = self.x, self.y, self.z, self.c
        self.other = (gx, z * 2 + 1 - c)
        ax, ay = x + (1 - c) * (1 - 2 * x), y + c * (1 - 2 * y)
        bx, by = x + c * (1 - 2 * x), y + (1 - c) * (1 - 2 * y)
        self.first = (ay * 2 + ax, gy)
        self.second = (by * 2 + bx, gy)
        self.far = ((1 - y) * 2 + 1 - x, gy)
        self.quarter = gx
        self.quarter_first = ay * 2 + ax
        self.quarter_second = by * 2 + bx
        self.quarter_far = (1 - y) * 2 + 1 - x

    def along_z(self, j):
        return (self.quarter, (self.z + j) % self.nz * 2 + self.c)

    def greet(self):
        sem = pltpu.get_barrier_semaphore()
        partners = [self.other, self.first, self.second, self.far]
        partners += [self.along_z(j) for j in range(1, self.nz)]
        for p in partners:
            pl.semaphore_signal(sem, inc=1, device_id=p, device_id_type=MESH)

    def meet(self):
        pl.semaphore_wait(pltpu.get_barrier_semaphore(), 4 + self.nz - 1)


def fold_rows(v):
    n = v.shape[0]
    return jnp.sum(v.reshape(n // 8, 8, v.shape[1]), axis=0)


class Gather:
    TURNS = (0, 2, 4, 6, 7, 8)

    def __init__(self, nz, wa, wb, held, stage, z_sem, s_sem, own_sem, out_sem):
        self.at = Place(nz)
        self.nz, self.wa, self.wb, self.held, self.stage = nz, wa, wb, held, stage
        self.z_sem, self.s_sem, self.own_sem, self.out_sem = z_sem, s_sem, own_sem, out_sem

    def pump(self, s):
        for j in (5, 4, 3, 2, 1, 0):
            k = s + 3 - self.TURNS[j]
            pl.when((k >= (2 if j else 3)) & (k < CHUNKS))(partial(self.act, j, k))

    def act(self, j, k):
        at, nz = self.at, self.nz
        direct = isinstance(k, int) and k == 0
        mine = pl.ds(pl.multiple_of(at.c * HALF, HALF), HALF)
        others = pl.ds(pl.multiple_of((1 - at.c) * HALF, HALF), HALF)

        def spot(chip, lanes=mine):
            return self.held.at[k, chip, :, lanes]

        def quarter(q):
            return spot(pl.ds(q * nz, nz))

        def z_copy(i, chip):
            return remote(
                self.stage.at[k], spot(chip), self.z_sem.at[0, k, i - 1],
                self.z_sem.at[1, k, i - 1], at.along_z(i),
            )

        def s_copy(i, q, device):
            return remote(
                quarter(q), quarter(q), self.s_sem.at[0, k, i], self.s_sem.at[1, k, i], device
            )

        def far_copy(q):
            if direct:
                return s_copy(2, at.quarter if q is None else q, at.far)
            return s_copy(2, at.quarter_first if q is None else q, at.second)

        def c_copy(lanes):
            whole = spot(slice(None), lanes)
            return remote(
                whole, whole, self.s_sem.at[0, k, 3], self.s_sem.at[1, k, 3], at.other
            )

        def own():
            return pltpu.make_async_copy(self.stage.at[k], spot(chip), self.own_sem.at[k])

        chip = at.quarter * nz + at.z
        if j == 0:
            for i in range(1, nz):
                z_copy(i, chip).start()
            own().start()
        elif j == 1:
            for i in range(1, nz):
                z_copy(i, at.quarter * nz + (at.z - i + nz) % nz).wait_recv()
            own().wait()
            s_copy(0, at.quarter, at.first).start()
            s_copy(1, at.quarter, at.second).start()
            if direct:
                far_copy(None).start()
        elif j == 2:
            s_copy(0, at.quarter_first, at.first).wait_recv()
            if not direct:
                far_copy(None).start()
        elif j == 3:
            s_copy(1, at.quarter_second, at.second).wait_recv()
            far_copy(at.quarter_far).wait_recv()
            c_copy(mine).start()
        elif j == 4:
            c_copy(others).wait_recv()
            for i in range(1, nz):
                z_copy(i, chip).wait_send()
            s_copy(0, at.quarter, at.first).wait_send()
            s_copy(1, at.quarter, at.second).wait_send()
            far_copy(None).wait_send()
            c_copy(mine).wait_send()
            self.keep(k, lambda copy: copy.start())
        else:
            self.keep(k, lambda copy: copy.wait())

    def keep(self, k, fn):
        def early():
            fn(pltpu.make_async_copy(self.held.at[k], self.wa.at[k], self.out_sem.at[k]))

        def late():
            fn(pltpu.make_async_copy(self.held.at[k], self.wb.at[:, k - 8], self.out_sem.at[k]))

        if isinstance(k, int) and k < 8:
            early()
        elif isinstance(k, int):
            late()
        else:
            pl.when(k < 8)(early)
            pl.when(k >= 8)(late)


def share_start(nz, part_ref, masters, sibs, stage, table_ref, sums, got, x_sem, v_sem, gather):
    at = gather.at
    at.greet()
    at.meet()
    swaps = [
        remote(m, o, x_sem.at[0, i], x_sem.at[1, i], at.other)
        for i, (m, o) in enumerate(zip(masters, sibs))
    ]
    swaps.insert(1, remote(part_ref, got.at[0], x_sem.at[0, 4], x_sem.at[1, 4], at.other))
    for swap in swaps:
        swap.start()
    mq, mo, m1, m2 = masters
    sq, so, s1, s2 = sibs
    even = at.c == 0

    def halves(own, sib):
        own = jnp.where(even, own[:, :HALF], own[:, HALF:])
        sib = jnp.where(even, sib[:, :HALF], sib[:, HALF:])
        top, low = jnp.where(even, own, sib), jnp.where(even, sib, own)
        return jnp.concatenate([top, low], axis=0).astype(bf16)

    def group(ref, hg):
        cols = [ref[:, i * D + hg * WIDE : i * D + (hg + 1) * WIDE] for i in range(3)]
        return jnp.concatenate(cols, axis=1)

    def vec_copy(i, src, device):
        return remote(src, got.at[i], v_sem.at[0, i], v_sem.at[1, i], device)

    swaps[0].wait()
    for hg in range(GROUPS):
        stage[hg] = halves(group(mq, hg), group(sq, hg))
        if hg == 0:
            gather.act(0, hg)
    swaps[1].wait()
    sums[0] = part_ref[...] + got[0]
    z_copies = [vec_copy(i, sums.at[0], at.along_z(i)) for i in range(1, nz)]
    for copy in z_copies:
        copy.start()
    for swap in swaps[2:]:
        swap.wait()
    stage[3] = halves(mo[...], so[...])
    for f in range(4):
        cols = slice(f * CHUNK, (f + 1) * CHUNK)
        stage[4 + f] = halves(m1[:, cols], s1[:, cols])
    step = stage.shape[1]
    for i in range(4):
        rows = slice(i % 2 * step, (i % 2 + 1) * step)
        block = jnp.where(at.c == i // 2, m2[rows, :], s2[rows, :])
        stage[8 + i] = jnp.where(even, block[:, :HALF], block[:, HALF:]).astype(bf16)
    for copy in z_copies:
        copy.wait()
    total = sums[0]
    for i in range(1, nz):
        total = total + got[i]
    sums[1] = total
    near = [
        vec_copy(nz + i, sums.at[1], device)
        for i, device in enumerate((at.first, at.second, at.far))
    ]
    gather.act(1, 0)
    for copy in near:
        copy.start()
    gather.act(0, 1)
    gather.act(0, 2)
    gather.act(2, 0)
    gather.act(3, 0)
    for copy in near:
        copy.wait()
    table_ref[...] = (sums[1] + got[nz] + got[nz + 1] + got[nz + 2]).astype(f32)
    gather.act(4, 0)


def front_kernel(nz, *refs):
    refs = list(refs)
    x_ref, row_ref, col_ref, vec_ref = refs[:4]
    s = pl.program_id(0)
    att = GROUPS * 4
    if nz:
        masters, refs = refs[4:8], refs[8:]
    else:
        wa_ref, refs = refs[4], refs[5:]
    q_ref, k_ref, v_ref, lse_ref, c_ref, y1_ref, n1_ref, g_ref, gp_ref = refs[:9]
    refs = refs[9:]
    if nz:
        wa_ref, wb_ref, table_ref = refs[:3]
        c_all, held, stage, sq, so, s1, s2, sums, got = refs[3:12]
        z_sem, s_sem, own_sem, out_sem, x_sem, v_sem = refs[12:]
        gather = Gather(nz, wa_ref, wb_ref, held, stage, z_sem, s_sem, own_sem, out_sem)

        @pl.when(s == 0)
        def _():
            share_start(
                nz, vec_ref, masters, (sq, so, s1, s2), stage, table_ref, sums, got,
                x_sem, v_sem, gather,
            )

        for j in (1, 2, 3, 4, 5):
            pl.when(s == j - 1)(partial(gather.act, j, 1))
        pl.when(s == 2)(partial(gather.act, 5, 0))
        gather.pump(s)
    else:
        c_all, held, load_sem = refs
        table_ref = vec_ref

        @pl.when(s == 0)
        def _():
            copy = pltpu.make_async_copy(wa_ref, held, load_sem)
            copy.start()
            copy.wait()

    def weight(k):
        return held[k].reshape(CHUNK, CHUNK)

    @pl.when(s < att)
    def _():
        hg = s // 4
        r = s % 4
        rows = pl.multiple_of(r * SEQ, SEQ)
        lanes = pl.multiple_of(hg * WIDE, WIDE)
        xr = x_ref[pl.ds(rows, SEQ), :]
        wqkv = weight(hg)
        q = nn(xr, wqkv[:, 0:WIDE]) + table_ref[BQ : BQ + 1, pl.ds(lanes, WIDE)]
        q = q.astype(bf16)
        k = nn(xr, wqkv[:, WIDE : 2 * WIDE]).astype(bf16)
        v = nn(xr, wqkv[:, 2 * WIDE :]) + table_ref[BV : BV + 1, pl.ds(lanes, WIDE)]
        v = v.astype(bf16)
        q_ref[...] = q
        k_ref[...] = k
        v_ref[...] = v
        vt = v.T
        masks = head_masks()
        places = list(windows())

        def begin(b, first, width):
            qc = spread_heads(q[b * BAND : (b + 1) * BAND, :], masks)
            return nt(k[first : first + width, :], qc)

        ahead = begin(*places[0])
        for b, first, width in places:
            t = ahead
            if b + 1 < len(places):
                ahead = begin(*places[b + 1])
            t = t * SCORE + mask_bias(col_ref.at[0], row_ref.at[0], b, first, width)
            m = jnp.max(t, axis=0, keepdims=True)
            e = jnp.exp2(t - m)
            l = jnp.sum(e, axis=0, keepdims=True)
            p = (e * (1.0 / l)).astype(bf16)
            lse_ref[0, b : b + 1, :] = m + jnp.log2(l)
            ot = nn(vt[:, first : first + width], p)
            c = pick_heads(ot).T.astype(bf16)
            c_all[pl.ds(rows + b * BAND, BAND), pl.ds(lanes, WIDE)] = c

    @pl.when(s >= att)
    def _():
        r = s - att
        rows = pl.multiple_of(r * SEQ, SEQ)
        c = c_all[pl.ds(rows, SEQ), :]
        c_ref[...] = c
        y1 = x_ref[pl.ds(rows, SEQ), :].astype(f32) + (
            nn(c, weight(3)) + table_ref[BO : BO + 1, :]
        )
        y1_ref[...] = y1
        z1, _ = norm_stats(y1)
        n1 = (z1 * table_ref[G1 : G1 + 1, :] + table_ref[C1 : C1 + 1, :]).astype(bf16)
        n1_ref[...] = n1
        for f in range(4):
            cols = slice(f * CHUNK, (f + 1) * CHUNK)
            u = nn(n1, weight(4 + f)) + table_ref[B1 + f : B1 + f + 1, :]
            cdf, gauss = normal_cdf(u)
            g_ref[:, cols] = (u * cdf).astype(bf16)
            gp_ref[:, cols] = (cdf + u * (gauss * 0.3989422804014327)).astype(bf16)
        if nz:
            pl.when(s == att + 3)(partial(gather.act, 5, CHUNKS - 1))


def constant(shape):
    return pl.BlockSpec(shape, lambda s: (0,) * len(shape), pipeline_mode=pl.Buffered(1))


def front(x, row_codes, col_codes, table, weights, chips=0):
    tokens = x.shape[0]
    rows = tokens // SEQ
    assert rows == 4
    att = GROUPS * rows
    nz = chips // 4

    def code_at(s):
        return (jnp.where(s < att, s % rows, rows - 1), 0, 0)

    def head_at(s):
        return (jnp.where(s < att, s % rows, rows - 1), jnp.minimum(s // rows, GROUPS - 1))

    def tile_at(s):
        return (jnp.maximum(s - att, 0), 0)

    anywhere = pl.BlockSpec(memory_space=pl.ANY)
    narrow = pl.BlockSpec((SEQ, D), tile_at)
    head = pl.BlockSpec((SEQ, WIDE), head_at)
    wide = pl.BlockSpec((SEQ, FF), tile_at)
    in_specs = [
        constant((tokens, D)),
        pl.BlockSpec((1, 8, SEQ), code_at),
        pl.BlockSpec((1, SEQ, BAND), code_at),
        constant((TABLE, CHUNK)),
    ]
    out_specs = [
        head, head, head,
        pl.BlockSpec((1, 8, PACK * BAND), lambda s: (jnp.minimum(s, att - 1), 0, 0)),
        narrow, narrow, narrow, wide, wide,
    ]
    low = jax.ShapeDtypeStruct((tokens, D), bf16)
    out_shape = [
        low, low, low,
        jax.ShapeDtypeStruct((att, 8, PACK * BAND), f32),
        low,
        jax.ShapeDtypeStruct((tokens, D), f32),
        low,
        jax.ShapeDtypeStruct((tokens, FF), bf16),
        jax.ShapeDtypeStruct((tokens, FF), bf16),
    ]
    if nz:
        step = CHUNK // chips
        in_specs += [constant(w.shape) for w in weights]
        out_specs += [anywhere, anywhere, pl.BlockSpec((TABLE, CHUNK), lambda s: (0, 0))]
        out_shape += [
            jax.ShapeDtypeStruct((8, chips, step, CHUNK), bf16),
            jax.ShapeDtypeStruct((chips, 4, step, CHUNK), bf16),
            jax.ShapeDtypeStruct((TABLE, CHUNK), f32),
        ]
        dma = pltpu.SemaphoreType.DMA
        scratch = [
            pltpu.VMEM((tokens, D), bf16),
            pltpu.VMEM((CHUNKS, chips, step, CHUNK), bf16),
            pltpu.VMEM((CHUNKS, step, HALF), bf16),
            *(pltpu.VMEM(w.shape, f32) for w in weights),
            pltpu.VMEM((2, TABLE, CHUNK), bf16),
            pltpu.VMEM((nz + 3, TABLE, CHUNK), bf16),
            dma((2, CHUNKS, nz - 1)), dma((2, CHUNKS, 4)), dma((CHUNKS,)), dma((CHUNKS,)),
            dma((2, 5)), dma((2, nz + 3)),
        ]
        params = pltpu.CompilerParams(
            vmem_limit_bytes=VMEM, collective_id=0, has_side_effects=True
        )
    else:
        in_specs.append(anywhere)
        scratch = [
            pltpu.VMEM((tokens, D), bf16),
            pltpu.VMEM(weights[0].shape, bf16),
            pltpu.SemaphoreType.DMA,
        ]
        params = pltpu.CompilerParams(vmem_limit_bytes=VMEM)
    return pl.pallas_call(
        partial(front_kernel, nz),
        grid=(att + rows,),
        in_specs=in_specs,
        out_specs=out_specs,
        out_shape=out_shape,
        scratch_shapes=scratch,
        compiler_params=params,
        name="front",
    )(x, row_codes, col_codes, table, *weights)


def middle_kernel(
    y1_ref, g_ref, gp_ref, cot_ref, vec_ref, wo_ref, w1_ref, w2_ref,
    out_ref, df_ref, du_ref, dy1_ref, da_ref, dc_ref, grads_ref, sums_ref, ups_ref,
):
    s = pl.program_id(0)

    @pl.when(s == 0)
    def _():
        sums_ref[...] = jnp.zeros_like(sums_ref)
        ups_ref[...] = jnp.zeros_like(ups_ref)

    gain1 = vec_ref[G1 : G1 + 1, :]
    gain2 = vec_ref[G2 : G2 + 1, :]
    part = y1_ref.shape[0] // 2
    kept = [{}, {}]

    def down(h):
        rows = slice(h * part, (h + 1) * part)
        kept[h]["f"] = nn(g_ref[rows, :], w2_ref[...])

    def norm_two(h):
        rows = slice(h * part, (h + 1) * part)
        z1, r1 = norm_stats(y1_ref[rows, :])
        n1 = z1 * gain1 + vec_ref[C1 : C1 + 1, :]
        y2 = n1 + (kept[h]["f"] + vec_ref[B2 : B2 + 1, :])
        z2, r2 = norm_stats(y2)
        out_ref[rows, :] = (z2 * gain2 + vec_ref[C2 : C2 + 1, :]).astype(bf16)
        e = cot_ref[rows, :].astype(f32)
        sums_ref[0] += fold_rows(e * z2)
        sums_ref[1] += fold_rows(e)
        dy2 = norm_back(e * gain2, z2, r2)
        df = dy2.astype(bf16)
        df_ref[rows, :] = df
        sums_ref[2] += fold_rows(df.astype(f32))
        kept[h].update(dy2=dy2, df=df)

    def up_grad(h):
        rows = slice(h * part, (h + 1) * part)
        for f in range(4):
            cols = slice(f * CHUNK, (f + 1) * CHUNK)
            dg = nt(kept[h]["df"], w2_ref[cols, :])
            du = (dg * gp_ref[rows, cols].astype(f32)).astype(bf16)
            du_ref[rows, cols] = du
            ups_ref[:, cols] += fold_rows(du.astype(f32))

    def up_back(h):
        rows = slice(h * part, (h + 1) * part)
        dn1 = kept[h]["dy2"]
        for f in range(4):
            dn1 = dn1 + nt(du_ref[rows, f * CHUNK : (f + 1) * CHUNK], w1_ref[f])
        kept[h]["dn1"] = dn1

    def norm_one(h):
        rows = slice(h * part, (h + 1) * part)
        z1, r1 = norm_stats(y1_ref[rows, :])
        dn1 = kept[h]["dn1"]
        sums_ref[3] += fold_rows(dn1 * z1)
        sums_ref[4] += fold_rows(dn1)
        dy1 = norm_back(dn1 * gain1, z1, r1)
        dy1_ref[rows, :] = dy1
        da = dy1.astype(bf16)
        da_ref[rows, :] = da
        sums_ref[5] += fold_rows(da.astype(f32))
        dc_ref[rows, :] = nt(da, wo_ref[0]).astype(bf16)

    for stage in (down, norm_two, up_grad, up_back, norm_one):
        for h in range(2):
            stage(h)

    @pl.when(s == pl.num_programs(0) - 1)
    def _():
        grads_ref[...] = jnp.zeros_like(grads_ref)
        for i, row in enumerate((G2, C2, B2, G1, C1, BO)):
            grads_ref[row : row + 1, :] = jnp.sum(sums_ref[i], axis=0, keepdims=True)
        for f in range(4):
            cols = slice(f * CHUNK, (f + 1) * CHUNK)
            grads_ref[B1 + f : B1 + f + 1, :] = jnp.sum(ups_ref[:, cols], axis=0, keepdims=True)


def chunks_at(count, index):
    return pl.BlockSpec(
        (count, CHUNK, CHUNK), lambda s: (index, 0, 0), pipeline_mode=pl.Buffered(1)
    )


def middle(y1, g, gp, cot, table, wa, w2):
    tokens = y1.shape[0]
    tile = SEQ

    narrow = pl.BlockSpec((tile, D), lambda s: (s, 0))
    wide = pl.BlockSpec((tile, FF), lambda s: (s, 0))
    wide_out = pl.BlockSpec((tile, FF), lambda s: (s, 0))
    return pl.pallas_call(
        middle_kernel,
        grid=(tokens // tile,),
        in_specs=[
            narrow, wide, wide, narrow, constant((TABLE, CHUNK)),
            chunks_at(1, 3), chunks_at(4, 1), constant((FF, D)),
        ],
        out_specs=[
            narrow, narrow, wide_out, narrow, narrow, narrow,
            pl.BlockSpec((TABLE, CHUNK), lambda s: (0, 0)),
        ],
        out_shape=[
            jax.ShapeDtypeStruct((tokens, D), bf16),
            jax.ShapeDtypeStruct((tokens, D), bf16),
            jax.ShapeDtypeStruct((tokens, FF), bf16),
            jax.ShapeDtypeStruct((tokens, D), f32),
            jax.ShapeDtypeStruct((tokens, D), bf16),
            jax.ShapeDtypeStruct((tokens, D), bf16),
            jax.ShapeDtypeStruct((TABLE, CHUNK), f32),
        ],
        scratch_shapes=[pltpu.VMEM((6, 8, D), f32), pltpu.VMEM((8, FF), f32)],
        compiler_params=pltpu.CompilerParams(vmem_limit_bytes=VMEM),
        name="middle",
    )(y1, g, gp, cot, table, wa, wa, w2)


DOWN, UP, PROJ, QKV = 0, 4, 8, 9
OUTERS = 9


class Reduce:
    def __init__(self, nz, grads, made, local, bufs, fin, outs, sems):
        self.at = Place(nz)
        self.nz, self.grads, self.made, self.local = nz, grads, made, local
        self.bufs, self.fin, self.outs = bufs, fin, outs
        self.c_sem, self.l_sem, self.q_sem, self.z_sem, self.f_sem = sems

    TURNS = (0, 1, 3, 5, 7, 8)
    LATE_TURNS = (0, 1, 3, 4, 6, 7)

    def pump(self, s):
        for j in (5, 4, 3, 2, 1, 0):
            r = s - 5 - self.TURNS[j]
            pl.when((r >= 0) & (r < QKV))(partial(self.act, j, r))

        @pl.when(s >= 5 + QKV)
        def _():
            for hg, start, turns in ((0, 5 + QKV, self.TURNS), (1, 17, self.LATE_TURNS)):
                for j in range(6):
                    pl.when(s == start + turns[j])(partial(self.act, j, QKV + hg))

    def source(self, r, lanes, fn):
        g2, g19 = self.grads
        if isinstance(r, int):
            fn(self.made.at[r - QKV, :, :, :, lanes])
            return
        pl.when(r < UP)(lambda: fn(g2.at[:, :, r, :, lanes]))
        pl.when(r >= UP)(lambda: fn(g19.at[r - UP, :, :, :, lanes]))

    def act(self, j, r):
        at, nz = self.at, self.nz
        r0, r1, r2, r3 = self.bufs
        fin, got = self.fin
        c, x, y, z = at.c, at.x, at.y, at.z
        half = [pl.ds(pl.multiple_of(i * HALF, HALF), HALF) for i in (c, 1 - c)]

        def c_copy(src):
            return remote(src, r0.at[r], self.c_sem.at[0, r], self.c_sem.at[1, r], at.other)

        def l_copy(src):
            return pltpu.make_async_copy(src, self.local.at[r % 2], self.l_sem.at[r % 2])

        def a_copy(i):
            q = (1 - c) * (2 * i + 1 - x) + c * (2 * (1 - y) + i)
            return remote(
                r0.at[r, q], r1.at[r, i],
                self.q_sem.at[0, r, i], self.q_sem.at[1, r, i], at.first,
            )

        keep = (1 - c) * y + c * x

        def b_copy():
            return remote(
                r1.at[r, 1 - keep], r2.at[r],
                self.q_sem.at[0, r, 2], self.q_sem.at[1, r, 2], at.second,
            )

        def z_copy(i):
            return remote(
                r2.at[r, (z + i) % nz], r3.at[r, i - 1],
                self.z_sem.at[0, r, i - 1], self.z_sem.at[1, r, i - 1], at.along_z(i),
            )

        def f_copy():
            return remote(fin.at[r], got.at[r], self.f_sem.at[0, r], self.f_sem.at[1, r], at.other)

        rows = fin.shape[1] // 2
        if j == 0:
            self.source(r, half[1], lambda src: c_copy(src).start())
            if not isinstance(r, int):
                self.source(r, half[0], lambda src: l_copy(src).start())
        elif j == 1:
            if isinstance(r, int):
                c_copy(self.made.at[r - QKV, :, :, :, half[1]]).wait()
                own = self.made.at[r - QKV]
                mine = jnp.where(c == 0, own[:, :, :, :HALF], own[:, :, :, HALF:])
            else:
                self.source(r, half[1], lambda src: c_copy(src).wait())
                self.source(r, half[0], lambda src: l_copy(src).wait())
                mine = self.local[r % 2]
            r0[r] = r0[r] + mine
            a_copy(0).start()
            a_copy(1).start()
        elif j == 2:
            for i in (0, 1):
                a_copy(i).wait()
                q = (1 - c) * (2 * i + x) + c * (2 * y + i)
                r1[r, i] = r1[r, i] + r0[r, q]
            b_copy().start()
        elif j == 3:
            b_copy().wait()
            r2[r] = r2[r] + r1[r, keep]
            for i in range(1, nz):
                z_copy(i).start()
        elif j == 4:
            total = r2[r, z].astype(f32)
            for i in range(1, nz):
                z_copy(i).wait()
                total = total + r3[r, i - 1].astype(f32)
            fin[r] = total
            f_copy().start()
        else:
            f_copy().wait()
            self.finish(r, rows)

    def finish(self, r, rows):
        c = self.at.c
        fin, got = self.fin
        out, out_down = self.outs
        even = c == 0

        def sides(own, other):
            return jnp.concatenate(
                [jnp.where(even, own, other), jnp.where(even, other, own)], axis=1
            )

        def down():
            @pl.when(c == r // 2)
            def _():
                out_down[r % 2] = sides(fin[r], got[r])

        def rest():
            own = jnp.where(even, fin[r, :rows, :], fin[r, rows:, :])
            other = jnp.where(even, got[r, :rows, :], got[r, rows:, :])
            out[r - UP] = sides(own, other)

        if isinstance(r, int):
            rest()
        else:
            pl.when(r < UP)(down)
            pl.when(r >= UP)(rest)


def back_kernel(comm, nz, *refs):
    (
        x_hbm, row_ref, col_ref, wa_hbm, q_ref, k_ref, v_ref, dc_ref, lse_ref, dy1_ref, table_ref,
        g_hbm, df_hbm, n1_hbm, du_hbm, c_hbm, da_hbm,
        g2_hbm, g19_hbm, out, out_down, total_ref, dx_ref,
        x_ref, wqkv_ref, work, res, made, dk_sum, dv_sum, qv_sum, in_sem, res_sem,
    ) = refs[:33]
    s = pl.program_id(0)
    att = GROUPS * 4
    end = OUTERS + att
    if comm:
        local, r0, r1, r2, r3, fin, got, mine, came = refs[33:42]
        sems, v_sem = refs[42:47], refs[47]
        reduce = Reduce(
            nz, (g2_hbm, g19_hbm), made, local, (r0, r1, r2, r3), (fin, got), (out, out_down), sems
        )
        at = reduce.at

        pl.when(s == 0)(at.greet)
        pl.when(s == 5)(at.meet)

    def bring(src, dst, i):
        return pltpu.make_async_copy(src, dst, in_sem.at[i])

    def stream(i, fn):
        cols = pl.ds(pl.multiple_of(i % 4 * CHUNK, CHUNK), CHUNK)
        slot = i % 2
        pl.when(i < 4)(lambda: fn(bring(g_hbm.at[:, cols], work.at[slot], slot)))
        pl.when((i >= 4) & (i < 8))(lambda: fn(bring(du_hbm.at[:, cols], work.at[slot], slot)))
        pl.when(i == 8)(lambda: fn(bring(c_hbm, work.at[slot], slot)))

    def store(i, fn):
        slot = i % 2
        pl.when(i < 4)(
            lambda: fn(pltpu.make_async_copy(res.at[slot], g2_hbm.at[i], res_sem.at[slot]))
        )
        pl.when(i >= 4)(
            lambda: fn(pltpu.make_async_copy(res.at[slot], g19_hbm.at[i - 4], res_sem.at[slot]))
        )

    whole_df, whole_da = bring(df_hbm, work.at[2], 2), bring(da_hbm, work.at[2], 2)
    whole_n1 = bring(n1_hbm, work.at[3], 3)
    whole_x = bring(x_hbm, x_ref, 4)
    whole_w = bring(wa_hbm.at[0:GROUPS], wqkv_ref, 5)

    @pl.when(s == 0)
    def _():
        stream(s, lambda copy: copy.start())
        whole_df.start()
        stream(s + 1, lambda copy: copy.start())
        whole_n1.start()
        whole_df.wait()
        qv_sum[...] = jnp.zeros_like(qv_sum)

    pl.when((s >= 2) & (s < OUTERS + 2))(lambda: store(s - 2, lambda copy: copy.wait()))
    if comm:
        reduce.pump(s)

    @pl.when(s < OUTERS)
    def _():
        stream(s, lambda copy: copy.wait())
        pl.when(s == 4)(lambda: whole_n1.wait())
        pl.when(s == 8)(lambda: whole_da.wait())
        def put(product):
            res[s % 2] = product.astype(bf16).reshape(res.shape[1:])

        @pl.when((s < 4) | (s == 8))
        def _():
            put(tn(work[s % 2], work[2]))

        @pl.when((s >= 4) & (s < 8))
        def _():
            put(tn(work[3], work[s % 2]))

        store(s, lambda copy: copy.start())
        pl.when(s < OUTERS - 2)(lambda: stream(s + 2, lambda copy: copy.start()))
        pl.when(s == 3)(lambda: whole_da.start())

        @pl.when(s == 2)
        def _():
            whole_x.start()
            whole_w.start()

        @pl.when(s == OUTERS - 1)
        def _():
            whole_x.wait()
            whole_w.wait()

    @pl.when((s >= OUTERS) & (s < end))
    def _():
        hg = (s - OUTERS) // 4
        r = (s - OUTERS) % 4
        rows = pl.multiple_of(r * SEQ, SEQ)
        lanes = pl.ds(pl.multiple_of(hg * WIDE, WIDE), WIDE)
        kt = k_ref[...].T
        dk_sum[...] = jnp.zeros_like(dk_sum)
        dv_sum[...] = jnp.zeros_like(dv_sum)
        masks = head_masks()
        places = list(windows())

        def begin(b, first, width):
            block, span = slice(b * BAND, (b + 1) * BAND), slice(first, first + width)
            qc = spread_heads(q_ref[block, :], masks)
            dcc = spread_heads(dc_ref[block, :], masks)
            return qc, dcc, nt(k_ref[span, :], qc), nt(v_ref[span, :], dcc)

        ahead = begin(*places[0])
        for b, first, width in places:
            span = slice(first, first + width)
            qc, dcc, t, dp = ahead
            if b + 1 < len(places):
                ahead = begin(*places[b + 1])
            t = t * SCORE + mask_bias(col_ref.at[0], row_ref.at[0], b, first, width)
            p = jnp.exp2(t - lse_ref[0, b : b + 1, :])
            pdp = p * dp
            weighted = jnp.sum(pdp, axis=0, keepdims=True)
            ds = (pdp - p * weighted).astype(bf16)
            dv_sum[span, :] += nn(p.astype(bf16), dcc)
            dk_sum[span, :] += nn(ds, qc)
            dqt = nn(kt[:, span], ds)
            dq = (pick_heads(dqt).T * HEAD_DIM ** (-0.5)).astype(bf16)
            work[hg, pl.ds(rows + b * BAND, BAND), 0:WIDE] = dq
            qv_sum[0, :, lanes] += fold_rows(dq.astype(f32))
        dk = (dk_sum[...] * HEAD_DIM ** (-0.5)).astype(bf16)
        dv = dv_sum[...].astype(bf16)
        work[hg, pl.ds(rows, SEQ), WIDE : 2 * WIDE] = dk
        work[hg, pl.ds(rows, SEQ), 2 * WIDE :] = dv
        qv_sum[1, :, lanes] += fold_rows(dv.astype(f32))

        @pl.when(r == 3)
        def _():
            made[hg] = tn(x_ref[...], work[hg]).astype(bf16).reshape(made.shape[1:])

    last = QKV + GROUPS - 1
    if comm:
        def vec_copy(i, src, device):
            return remote(src, came.at[i], v_sem.at[0, i], v_sem.at[1, i], device)

        c_copy = vec_copy(0, mine.at[0], at.other)
        z_copies = [vec_copy(i, mine.at[1], at.along_z(i)) for i in range(1, nz)]
        near = [
            vec_copy(nz + i, mine.at[2], device)
            for i, device in enumerate((at.first, at.second, at.far))
        ]

        @pl.when(s == end - 1)
        def _():
            reduce.act(0, last)
            mine[0] = table_ref[...]
            mine[0, BQ : BQ + 1, :] = jnp.sum(qv_sum[0], axis=0, keepdims=True)
            mine[0, BV : BV + 1, :] = jnp.sum(qv_sum[1], axis=0, keepdims=True)
            c_copy.start()

        @pl.when(s == end)
        def _():
            reduce.act(1, last)
            c_copy.wait()
            mine[1] = mine[0] + came[0]
            for copy in z_copies:
                copy.start()

        @pl.when(s == end + 1)
        def _():
            reduce.act(3, last)
            total = mine[1]
            for i in range(1, nz):
                z_copies[i - 1].wait()
                total = total + came[i]
            mine[2] = total
            for copy in near:
                copy.start()

    @pl.when(s >= end)
    def _():
        half = SEQ // 2
        for h in range(2):
            if h == 1 and comm:
                pl.when(s == end)(lambda: reduce.act(2, last))
                pl.when(s == end + 1)(lambda: reduce.act(4, last))
            rows = pl.ds(pl.multiple_of((s - end) * SEQ + h * half, half), half)
            total = dy1_ref[h * half : (h + 1) * half, :]
            for hg in range(GROUPS):
                total = total + nt(work[hg, rows, :], wqkv_ref[hg].reshape(CHUNK, CHUNK))
            dx_ref[h * half : (h + 1) * half, :] = total

    @pl.when(s == end + 3)
    def _():
        if comm:
            for copy in near:
                copy.wait()
            total_ref[...] = mine[2] + came[nz] + came[nz + 1] + came[nz + 2]
            reduce.act(5, last)
        else:
            total_ref[...] = table_ref[...]
            total_ref[BQ : BQ + 1, :] = jnp.sum(qv_sum[0], axis=0, keepdims=True)
            total_ref[BV : BV + 1, :] = jnp.sum(qv_sum[1], axis=0, keepdims=True)
            out[...] = jnp.zeros_like(out)
            out_down[...] = jnp.zeros_like(out_down)


def back(x, row_codes, col_codes, wa, q, k, v, dc, lse, dy1, table, pairs, chips, comm):
    tokens = x.shape[0]
    rows = tokens // SEQ
    att = GROUPS * rows
    end = OUTERS + att
    assert rows == 4
    nz = chips // 4
    step = CHUNK // chips

    def turn(s):
        return jnp.clip(s - OUTERS, 0, att - 1)

    def code_at(s):
        return (turn(s) % rows, 0, 0)

    def head_at(s):
        return (turn(s) % rows, turn(s) // rows)

    def tile_at(s):
        return (jnp.maximum(s - end, 0), 0)

    anywhere = pl.BlockSpec(memory_space=pl.ANY)
    whole_table = pl.BlockSpec((TABLE, CHUNK), lambda s: (0, 0))
    head = pl.BlockSpec((SEQ, WIDE), head_at)
    tile = pl.BlockSpec((SEQ, D), tile_at)
    made_shape = (GROUPS, 4, nz, step, CHUNK)
    dma = pltpu.SemaphoreType.DMA
    scratch = [
        pltpu.VMEM((tokens, D), bf16),
        pltpu.VMEM((GROUPS, *wa.shape[1:]), bf16),
        pltpu.VMEM((4, tokens, CHUNK), bf16),
        pltpu.VMEM((2, 4, nz, step, CHUNK), bf16),
    ]
    if comm:
        scratch.append(pltpu.VMEM(made_shape, bf16))
    scratch += [
        pltpu.VMEM((SEQ, WIDE), f32),
        pltpu.VMEM((SEQ, WIDE), f32),
        pltpu.VMEM((2, 8, D), f32),
        dma((6,)), dma((2,)),
    ]
    out_specs = [
        anywhere, anywhere,
        pl.BlockSpec((8, step // 2, CHUNK), lambda s: (0, 0, 0)),
        pl.BlockSpec((2, step, CHUNK), lambda s: (0, 0, 0)),
        whole_table, tile,
    ]
    out_shape = [
        jax.ShapeDtypeStruct((4, nz, 4, step, CHUNK), bf16),
        jax.ShapeDtypeStruct((5, 4, nz, step, CHUNK), bf16),
        jax.ShapeDtypeStruct((8, step // 2, CHUNK), f32),
        jax.ShapeDtypeStruct((2, step, CHUNK), f32),
        jax.ShapeDtypeStruct((TABLE, CHUNK), f32),
        jax.ShapeDtypeStruct((tokens, D), f32),
    ]
    kernel = partial(back_kernel, comm, nz)
    if comm:
        scratch += [
            pltpu.VMEM((2, 4, nz, step, HALF), bf16),
            pltpu.VMEM((CHUNKS, 4, nz, step, HALF), bf16),
            pltpu.VMEM((CHUNKS, 2, nz, step, HALF), bf16),
            pltpu.VMEM((CHUNKS, nz, step, HALF), bf16),
            pltpu.VMEM((CHUNKS, nz - 1, step, HALF), bf16),
            pltpu.VMEM((CHUNKS, step, HALF), f32),
            pltpu.VMEM((CHUNKS, step, HALF), f32),
            pltpu.VMEM((3, TABLE, CHUNK), f32),
            pltpu.VMEM((nz + 3, TABLE, CHUNK), f32),
            dma((2, CHUNKS)), dma((2,)), dma((2, CHUNKS, 3)), dma((2, CHUNKS, nz - 1)),
            dma((2, CHUNKS)), dma((2, nz + 3)),
        ]
        params = pltpu.CompilerParams(
            vmem_limit_bytes=VMEM, collective_id=1, has_side_effects=True
        )
    else:
        def kernel(*refs):
            refs = list(refs)
            made = refs.pop(23)
            refs.insert(27, made)
            back_kernel(comm, nz, *refs)

        out_specs.append(pl.BlockSpec(made_shape, lambda s: (0,) * 5, pipeline_mode=pl.Buffered(1)))
        out_shape.append(jax.ShapeDtypeStruct(made_shape, bf16))
        params = pltpu.CompilerParams(vmem_limit_bytes=VMEM)
    return pl.pallas_call(
        kernel,
        grid=(end + rows,),
        in_specs=[
            anywhere,
            pl.BlockSpec((1, 8, SEQ), code_at),
            pl.BlockSpec((1, SEQ, BAND), code_at),
            anywhere,
            head, head, head, head,
            pl.BlockSpec((1, 8, PACK * BAND), lambda s: (turn(s), 0, 0)),
            tile, whole_table,
            *(anywhere for _ in pairs),
        ],
        out_specs=out_specs,
        out_shape=out_shape,
        scratch_shapes=scratch,
        compiler_params=params,
        name="back",
    )(x, row_codes, col_codes, wa, q, k, v, dc, lse, dy1, table, *pairs)


def update(grad, master, moment, average, tokens_all):
    mean_grad = grad / tokens_all
    moment_new = momentum_coef * moment + mean_grad
    step_size = -learn_rate * (mean_grad + momentum_coef * moment_new)
    master_new = master + step_size
    average_new = average_keep * average + (1.0 - average_keep) * master_new
    return (master_new, moment_new, average_new)


def update_steps(grad, master, moment, average, tokens_all):
    mean_grad = grad / tokens_all
    moment_new = momentum_coef * moment + mean_grad
    step_size = -learn_rate * (mean_grad + momentum_coef * moment_new)
    average_step = (1.0 - average_keep) * (master + step_size - average)
    return (step_size, moment_new, average_step)


def update_kernel(tokens_all, *refs):
    grad_ref, down_ref, dx_ref = refs[:3]
    states, outs, dx_out, kept, sem = refs[3:15], refs[15:31], *refs[31:34]
    parts = kept.shape[0]
    spans = [pl.ds(i * kept.shape[1], kept.shape[1]) for i in range(parts)]
    loads = [
        pltpu.make_async_copy(dx_ref.at[span], kept.at[i], sem.at[0, i])
        for i, span in enumerate(spans)
    ]
    saves = [
        pltpu.make_async_copy(kept.at[i], dx_out.at[span], sem.at[1, i])
        for i, span in enumerate(spans)
    ]
    for load in loads:
        load.start()

    def one(i, index, grad):
        master, moment, average = (states[i + 4 * j][index] for j in range(3))
        outs[i][index] = grad
        new = update(grad, master, moment, average, tokens_all)
        for j in range(3):
            outs[i + 4 * (j + 1)][index] = new[j]

    rows = grad_ref.shape[1]
    for i in range(parts):
        loads[i].wait()
        saves[i].start()
    for hg in range(GROUPS):
        for i in range(3):
            cols = slice(i * D + hg * WIDE, i * D + (hg + 1) * WIDE)
            one(0, (slice(None), cols), grad_ref[5 + hg, :, i * WIDE : (i + 1) * WIDE])
    one(1, (slice(None), slice(None)), grad_ref[4])
    for f in range(4):
        one(2, (slice(None), slice(f * CHUNK, (f + 1) * CHUNK)), grad_ref[f])
    for i in range(2):
        one(3, (slice(2 * rows * i, 2 * rows * (i + 1)), slice(None)), down_ref[i])
    for save in saves:
        save.wait()


def update_weights(grads, grads_down, dx, states, tokens_all):
    whole = pl.BlockSpec(memory_space=pltpu.VMEM)
    anywhere = pl.BlockSpec(memory_space=pl.ANY)
    shapes = [jax.ShapeDtypeStruct(w.shape, f32) for w in states[:4]]
    return pl.pallas_call(
        partial(update_kernel, tokens_all),
        in_specs=[whole] * 2 + [anywhere] + [whole] * 12,
        out_specs=[whole] * 16 + [anywhere],
        out_shape=shapes * 4 + [jax.ShapeDtypeStruct(dx.shape, f32)],
        scratch_shapes=[
            pltpu.VMEM((8, dx.shape[0] // 8, D), f32), pltpu.SemaphoreType.DMA((2, 8)),
        ],
        compiler_params=pltpu.CompilerParams(vmem_limit_bytes=VMEM),
        name="update",
    )(grads, grads_down, dx, *states)


def group_columns(w):
    n = w.shape[0]
    return w.reshape(n, 3, GROUPS, WIDE).transpose(2, 0, 1, 3).reshape(GROUPS, n, 3 * WIDE)


def ungroup_columns(w):
    n = w.shape[1]
    return w.reshape(GROUPS, n, 3, WIDE).transpose(1, 2, 0, 3).reshape(n, 3 * D)


def table_of(gains, biases):
    flat = jnp.concatenate([gains, biases, jnp.zeros((TABLE * CHUNK - 9216,), gains.dtype)])
    return flat.reshape(TABLE, CHUNK)


def on_device(
    tokens, segment_ids, pad_counts, out_cotangent,
    qkv_master, proj_master, up_master, down_master, gain_master, bias_master,
    qkv_moment, proj_moment, up_moment, down_moment, gain_moment, bias_moment,
    qkv_average, proj_average, up_average, down_average, gain_average, bias_average,
):
    axes = ("gx", "gy")
    devices = lax.axis_size(axes)
    seq_len = segment_ids.shape[1]
    tokens_all = tokens.shape[0] * devices
    position = jnp.arange(seq_len, dtype=jnp.int32)
    is_pad = position[None, :] >= (seq_len - pad_counts)[:, None]
    codes = segment_ids * 2 + is_pad.astype(jnp.int32)
    row_codes = jnp.broadcast_to(codes[:, None, :], (codes.shape[0], 8, seq_len))
    col_codes = jnp.broadcast_to(codes[:, :, None], (codes.shape[0], seq_len, BAND))
    gain_len, bias_len = gain_master.shape[0], bias_master.shape[0]
    gains = gain_len * devices
    place = lax.axis_index(axes)

    fine = lax.axis_size("gx") == 4 and lax.axis_size("gy") == 8
    if fine:
        chips = devices // 2
        part = jnp.zeros((TABLE * CHUNK,), bf16)
        part = lax.dynamic_update_slice(part, gain_master.astype(bf16), (place * gain_len,))
        part = lax.dynamic_update_slice(
            part, bias_master.astype(bf16), (gains + place * bias_len,)
        ).reshape(TABLE, CHUNK)
        q, k, v, lse, c, y1, n1, g, gp, wa, w2, table = front(
            tokens, row_codes, col_codes, part,
            (qkv_master, proj_master, up_master, down_master), chips,
        )
        w2 = w2.reshape(FF, D)
    else:
        gather = partial(lax.all_gather, axis_name=axes, axis=0, tiled=True)
        w1 = gather(up_master.astype(bf16))
        wa = jnp.concatenate(
            [
                group_columns(gather(qkv_master.astype(bf16))),
                gather(proj_master.astype(bf16))[None],
                w1.reshape(D, 4, CHUNK).transpose(1, 0, 2),
            ]
        ).reshape(8, 16, CHUNK // 16, CHUNK)
        w2 = gather(down_master.astype(bf16))
        table = table_of(
            gather(gain_master.astype(bf16)), gather(bias_master.astype(bf16))
        ).astype(f32)
        q, k, v, lse, c, y1, n1, g, gp = front(
            tokens, row_codes, col_codes, table, (wa,)
        )
    layer_output, df, du, dy1, da, dc, terms = middle(
        y1, g, gp, out_cotangent, table, wa.reshape(8, CHUNK, CHUNK), w2
    )
    results = back(
        tokens, row_codes, col_codes, wa, q, k, v, dc, lse, dy1, terms,
        (g, df, n1, du, c, da), chips if fine else 16, fine,
    )
    input_grad = results[5]
    scatter = partial(lax.psum_scatter, axis_name=axes, scatter_dimension=0, tiled=True)
    states = (
        qkv_master, proj_master, up_master, down_master,
        qkv_moment, proj_moment, up_moment, down_moment,
        qkv_average, proj_average, up_average, down_average,
    )
    if fine:
        grads, grads_down, terms = results[2:5]
        new = update_weights(grads, grads_down, input_grad, states, tokens_all)
        shares, masters, moments, averages = new[:4], new[4:8], new[8:12], new[12:16]
        input_grad = new[16]
        terms = terms.reshape(-1)
        gain_share = lax.dynamic_slice(terms, (place * gain_len,), (gain_len,))
        bias_share = lax.dynamic_slice(terms, (gains + place * bias_len,), (bias_len,))
    else:
        down_part, rest, terms, dwqkv = (results[i].astype(f32) for i in (0, 1, 4, 6))
        rest = rest.reshape(5, CHUNK, CHUNK)
        terms = terms.reshape(-1)
        shares = (
            scatter(ungroup_columns(dwqkv.reshape(GROUPS, CHUNK, CHUNK))),
            scatter(rest[4]),
            scatter(rest[:4].transpose(1, 0, 2).reshape(D, FF)),
            scatter(down_part.reshape(FF, D)),
        )
        news = [
            update(shares[i], states[i], states[4 + i], states[8 + i], tokens_all)
            for i in range(4)
        ]
        masters, moments, averages = zip(*news)
        gain_share = scatter(terms[:gains])
        bias_share = scatter(terms[gains : gains + bias_len * devices])
    gain_new = update_steps(gain_share, gain_master, gain_moment, gain_average, tokens_all)
    bias_new = update(bias_share, bias_master, bias_moment, bias_average, tokens_all)
    return (
        layer_output, input_grad, *shares, gain_share, bias_share,
        *masters, gain_new[0], bias_new[0],
        *moments, gain_new[1], bias_new[1],
        *averages, gain_new[2], bias_new[2],
    )


def solution(mesh):
    both = ("gx", "gy")
    two, one = P(both, None), P(both)
    weights = (two, two, two, two, one, one)
    in_specs = (two, two, one, two) + weights * 3
    out_specs = (two, two) + weights * 4
    return jax.shard_map(
        on_device, mesh=mesh, in_specs=in_specs, out_specs=out_specs, check_vma=False
    )
```

```python
from functools import partial

import jax
import jax.numpy as jnp
from jax import lax
from jax.experimental import pallas as pl
from jax.experimental.pallas import tpu as pltpu
from jax.sharding import PartitionSpec as P

D = 768
HEADS = 12
HEAD_DIM = 64
FF = 3072
SEQ = 512
BAND = 128
PACK = 4
GROUPS = HEADS // PACK
WIDE = PACK * HEAD_DIM
VMEM = 60 * 1024 * 1024

norm_eps = 1e-06
momentum_coef = 0.9
learn_rate = 4.0
average_keep = 0.9

G1, G2, BQ, BV, BO, C1, B1, B2, C2 = (0, 1, 2, 3, 4, 5, 6, 10, 11)
TABLE = 16
CHUNK = 768
CHUNKS = 12
HALF = CHUNK // 2
MESH = pl.DeviceIdType.MESH

f32 = jnp.float32
bf16 = jnp.bfloat16

LOG2E = 1.4426950408889634
SCORE = HEAD_DIM ** (-0.5) * LOG2E


def nn(a, b):
    return lax.dot_general(a, b, (((1,), (0,)), ((), ())), preferred_element_type=f32)


def nt(a, b):
    return lax.dot_general(a, b, (((1,), (1,)), ((), ())), preferred_element_type=f32)


def tn(a, b):
    return lax.dot_general(a, b, (((0,), (0,)), ((), ())), preferred_element_type=f32)


def normal_cdf(u):
    gauss = jnp.exp2(u * u * (-0.5 * LOG2E))
    return 0.5 + 0.5 * lax.erf(u * 0.7071067811865476), gauss


def windows():
    for b in range(SEQ // BAND):
        first = max(0, (b - 1) * BAND)
        last = min(SEQ, (b + 2) * BAND)
        yield b, first, last - first


def head_masks():
    lane = lax.broadcasted_iota(jnp.int32, (BAND, WIDE), 1) // HEAD_DIM
    return [jnp.where(lane == h, 1.0, 0.0).astype(bf16) for h in range(PACK)]


def spread_heads(block, masks):
    return jnp.concatenate([block * m for m in masks], axis=0)


def pick_heads(wide):
    return jnp.concatenate(
        [
            wide[h * HEAD_DIM : (h + 1) * HEAD_DIM, h * BAND : (h + 1) * BAND]
            for h in range(PACK)
        ],
        axis=0,
    )


def mask_bias(col, row, b, first, width):
    keys = col[first : first + width, :]
    queries = row[0:1, b * BAND : (b + 1) * BAND]
    bias = jnp.where(keys == queries, 0.0, -1e30)
    return jnp.concatenate([bias] * PACK, axis=1)


def norm_stats(y):
    centre = jnp.mean(y, axis=-1, keepdims=True)
    centred = y - centre
    spread = jnp.mean(centred * centred, axis=-1, keepdims=True)
    r = lax.rsqrt(spread + norm_eps)
    return centred * r, r


def norm_back(dz, z, r):
    return r * (
        dz
        - jnp.mean(dz, axis=-1, keepdims=True)
        - z * jnp.mean(dz * z, axis=-1, keepdims=True)
    )


def remote(src, dst, send, recv, device):
    return pltpu.make_async_remote_copy(
        src_ref=src, dst_ref=dst, send_sem=send, recv_sem=recv, device_id=device,
        device_id_type=MESH,
    )


class Place:
    def __init__(self, nz):
        gx = lax.axis_index("gx")
        gy = lax.axis_index("gy")
        self.nz = nz
        self.x, self.y = gx % 2, gx // 2
        self.z, self.c = gy // 2, gy % 2
        x, y, z, c = self.x, self.y, self.z, self.c
        self.other = (gx, z * 2 + 1 - c)
        ax, ay = x + (1 - c) * (1 - 2 * x), y + c * (1 - 2 * y)
        bx, by = x + c * (1 - 2 * x), y + (1 - c) * (1 - 2 * y)
        self.first = (ay * 2 + ax, gy)
        self.second = (by * 2 + bx, gy)
        self.far = ((1 - y) * 2 + 1 - x, gy)
        self.quarter = gx
        self.quarter_first = ay * 2 + ax
        self.quarter_second = by * 2 + bx
        self.quarter_far = (1 - y) * 2 + 1 - x

    def along_z(self, j):
        return (self.quarter, (self.z + j) % self.nz * 2 + self.c)

    def greet(self):
        sem = pltpu.get_barrier_semaphore()
        partners = [self.other, self.first, self.second, self.far]
        partners += [self.along_z(j) for j in range(1, self.nz)]
        for p in partners:
            pl.semaphore_signal(sem, inc=1, device_id=p, device_id_type=MESH)

    def meet(self):
        pl.semaphore_wait(pltpu.get_barrier_semaphore(), 4 + self.nz - 1)


def fold_rows(v):
    n = v.shape[0]
    return jnp.sum(v.reshape(n // 8, 8, v.shape[1]), axis=0)


class Gather:
    TURNS = (-2, 0, 2, 4, 5, 6)

    def __init__(self, nz, wa, wb, held, stage, z_sem, s_sem, own_sem, out_sem):
        self.at = Place(nz)
        self.nz, self.wa, self.wb, self.held, self.stage = nz, wa, wb, held, stage
        self.z_sem, self.s_sem, self.own_sem, self.out_sem = z_sem, s_sem, own_sem, out_sem

    def pump(self, s):
        for j in (5, 4, 3, 2, 1, 0):
            turn = s + 3 - self.TURNS[j]
            k = (2 * turn + 1) // 3
            due = (turn % 3 != 2) & (k >= (4, 2, 2, 2, 2, 2)[j]) & (k < CHUNKS - 2)
            pl.when(due)(partial(self.act, j, k))

        @pl.when(s <= 5)
        def _():
            for j, turn in ((2, 1), (3, 3), (4, 4), (5, 5)):
                pl.when(s == turn)(partial(self.act, j, 1))

        @pl.when(s >= 10)
        def _():
            for k in (CHUNKS - 2, CHUNKS - 1):
                for j in range(6):
                    turn = k + (0, 2, 3, 4, 5, 6)[j]
                    pl.when(s == turn)(partial(self.act, j, k))

    def rest(self):
        self.act(5, CHUNKS - 3)
        self.act(5, CHUNKS - 2)
        self.act(4, CHUNKS - 1)
        self.act(5, CHUNKS - 1)

    def act(self, j, k):
        at, nz = self.at, self.nz
        direct = isinstance(k, int) and k == 0
        mine = pl.ds(pl.multiple_of(at.c * HALF, HALF), HALF)
        others = pl.ds(pl.multiple_of((1 - at.c) * HALF, HALF), HALF)

        def spot(chip, lanes=mine):
            return self.held.at[k, chip, :, lanes]

        def quarter(q):
            return spot(pl.ds(q * nz, nz))

        def z_copy(i, chip):
            return remote(
                self.stage.at[k], spot(chip), self.z_sem.at[0, k, i - 1],
                self.z_sem.at[1, k, i - 1], at.along_z(i),
            )

        def s_copy(i, q, device):
            return remote(
                quarter(q), quarter(q), self.s_sem.at[0, k, i], self.s_sem.at[1, k, i], device
            )

        def far_copy(q):
            if direct:
                return s_copy(2, at.quarter if q is None else q, at.far)
            return s_copy(2, at.quarter_first if q is None else q, at.second)

        def c_copy(lanes):
            whole = spot(slice(None), lanes)
            return remote(
                whole, whole, self.s_sem.at[0, k, 3], self.s_sem.at[1, k, 3], at.other
            )

        def own():
            return pltpu.make_async_copy(self.stage.at[k], spot(chip), self.own_sem.at[k])

        chip = at.quarter * nz + at.z
        if j == 0:
            for i in range(1, nz):
                z_copy(i, chip).start()
            own().start()
        elif j == 1:
            for i in range(1, nz):
                z_copy(i, at.quarter * nz + (at.z - i + nz) % nz).wait_recv()
            own().wait()
            s_copy(0, at.quarter, at.first).start()
            s_copy(1, at.quarter, at.second).start()
            if direct:
                far_copy(None).start()
        elif j == 2:
            s_copy(0, at.quarter_first, at.first).wait_recv()
            if not direct:
                far_copy(None).start()
        elif j == 3:
            s_copy(1, at.quarter_second, at.second).wait_recv()
            far_copy(at.quarter_far).wait_recv()
            c_copy(mine).start()
        elif j == 4:
            c_copy(others).wait_recv()
            for i in range(1, nz):
                z_copy(i, chip).wait_send()
            s_copy(0, at.quarter, at.first).wait_send()
            s_copy(1, at.quarter, at.second).wait_send()
            far_copy(None).wait_send()
            c_copy(mine).wait_send()
            self.keep(k, lambda copy: copy.start())
        else:
            self.keep(k, lambda copy: copy.wait())

    def keep(self, k, fn):
        def early():
            fn(pltpu.make_async_copy(self.held.at[k], self.wa.at[k], self.out_sem.at[k]))

        def late():
            fn(pltpu.make_async_copy(self.held.at[k], self.wb.at[:, k - 8], self.out_sem.at[k]))

        if isinstance(k, int) and k < 8:
            early()
        elif isinstance(k, int):
            late()
        else:
            pl.when(k < 8)(early)
            pl.when(k >= 8)(late)


def share_start(nz, part_ref, masters, sibs, stage, table_ref, sums, got, x_sem, v_sem, gather):
    at = gather.at
    at.greet()
    at.meet()
    swaps = [
        remote(m, o, x_sem.at[0, i], x_sem.at[1, i], at.other)
        for i, (m, o) in enumerate(zip(masters, sibs))
    ]
    swaps.insert(1, remote(part_ref, got.at[0], x_sem.at[0, 4], x_sem.at[1, 4], at.other))
    for swap in swaps:
        swap.start()
    mq, mo, m1, m2 = masters
    sq, so, s1, s2 = sibs
    even = at.c == 0

    def halves(own, sib):
        own = jnp.where(even, own[:, :HALF], own[:, HALF:])
        sib = jnp.where(even, sib[:, :HALF], sib[:, HALF:])
        top, low = jnp.where(even, own, sib), jnp.where(even, sib, own)
        return jnp.concatenate([top, low], axis=0).astype(bf16)

    def group(ref, hg):
        cols = [ref[:, i * D + hg * WIDE : i * D + (hg + 1) * WIDE] for i in range(3)]
        return jnp.concatenate(cols, axis=1)

    def vec_copy(i, src, device):
        return remote(src, got.at[i], v_sem.at[0, i], v_sem.at[1, i], device)

    swaps[0].wait()
    for hg in range(GROUPS):
        stage[hg] = halves(group(mq, hg), group(sq, hg))
        if hg == 0:
            gather.act(0, hg)
    swaps[1].wait()
    sums[0] = part_ref[...] + got[0]
    z_copies = [vec_copy(i, sums.at[0], at.along_z(i)) for i in range(1, nz)]
    for copy in z_copies:
        copy.start()
    for swap in swaps[2:]:
        swap.wait()
    stage[3] = halves(mo[...], so[...])
    for f in range(4):
        cols = slice(f * CHUNK, (f + 1) * CHUNK)
        stage[4 + f] = halves(m1[:, cols], s1[:, cols])
    step = stage.shape[1]
    for i in range(4):
        rows = slice(i % 2 * step, (i % 2 + 1) * step)
        block = jnp.where(at.c == i // 2, m2[rows, :], s2[rows, :])
        stage[8 + i] = jnp.where(even, block[:, :HALF], block[:, HALF:]).astype(bf16)
    for copy in z_copies:
        copy.wait()
    total = sums[0]
    for i in range(1, nz):
        total = total + got[i]
    sums[1] = total
    near = [
        vec_copy(nz + i, sums.at[1], device)
        for i, device in enumerate((at.first, at.second, at.far))
    ]
    gather.act(1, 0)
    for copy in near:
        copy.start()
    gather.act(0, 1)
    gather.act(0, 2)
    gather.act(0, 3)
    gather.act(2, 0)
    gather.act(3, 0)
    for copy in near:
        copy.wait()
    table_ref[...] = (sums[1] + got[nz] + got[nz + 1] + got[nz + 2]).astype(f32)
    gather.act(1, 1)
    gather.act(4, 0)


def front_kernel(nz, *refs):
    refs = list(refs)
    x_ref, row_ref, col_ref, vec_ref = refs[:4]
    s = pl.program_id(0)
    att = GROUPS * 4
    if nz:
        masters, refs = refs[4:8], refs[8:]
    else:
        wa_ref, refs = refs[4], refs[5:]
    q_ref, k_ref, v_ref, lse_ref, c_ref, y1_ref, n1_ref, g_ref, gp_ref = refs[:9]
    refs = refs[9:]
    if nz:
        wa_ref, wb_ref, table_ref = refs[:3]
        c_all, held, stage, sq, so, s1, s2, sums, got = refs[3:12]
        z_sem, s_sem, own_sem, out_sem, x_sem, v_sem = refs[12:]
        gather = Gather(nz, wa_ref, wb_ref, held, stage, z_sem, s_sem, own_sem, out_sem)

        @pl.when(s == 0)
        def _():
            share_start(
                nz, vec_ref, masters, (sq, so, s1, s2), stage, table_ref, sums, got,
                x_sem, v_sem, gather,
            )

        pl.when(s == 2)(partial(gather.act, 5, 0))
        gather.pump(s)
    else:
        c_all, held, load_sem = refs
        table_ref = vec_ref

        @pl.when(s == 0)
        def _():
            copy = pltpu.make_async_copy(wa_ref, held, load_sem)
            copy.start()
            copy.wait()

    def weight(k):
        return held[k].reshape(CHUNK, CHUNK)

    @pl.when(s < att)
    def _():
        hg = s // 4
        r = s % 4
        rows = pl.multiple_of(r * SEQ, SEQ)
        lanes = pl.multiple_of(hg * WIDE, WIDE)
        xr = x_ref[pl.ds(rows, SEQ), :]
        wqkv = weight(hg)
        q = nn(xr, wqkv[:, 0:WIDE]) + table_ref[BQ : BQ + 1, pl.ds(lanes, WIDE)]
        q = q.astype(bf16)
        k = nn(xr, wqkv[:, WIDE : 2 * WIDE]).astype(bf16)
        v = nn(xr, wqkv[:, 2 * WIDE :]) + table_ref[BV : BV + 1, pl.ds(lanes, WIDE)]
        v = v.astype(bf16)
        q_ref[...] = q
        k_ref[...] = k
        v_ref[...] = v
        vt = v.T
        masks = head_masks()
        places = list(windows())

        def begin(b, first, width):
            qc = spread_heads(q[b * BAND : (b + 1) * BAND, :], masks)
            return nt(k[first : first + width, :], qc)

        ahead = begin(*places[0])
        for b, first, width in places:
            t = ahead
            if b + 1 < len(places):
                ahead = begin(*places[b + 1])
            t = t * SCORE + mask_bias(col_ref.at[0], row_ref.at[0], b, first, width)
            m = jnp.max(t, axis=0, keepdims=True)
            e = jnp.exp2(t - m)
            l = jnp.sum(e, axis=0, keepdims=True)
            p = (e * (1.0 / l)).astype(bf16)
            lse_ref[0, b : b + 1, :] = m + jnp.log2(l)
            ot = nn(vt[:, first : first + width], p)
            c = pick_heads(ot).T.astype(bf16)
            c_all[pl.ds(rows + b * BAND, BAND), pl.ds(lanes, WIDE)] = c

    @pl.when(s >= att)
    def _():
        r = s - att
        rows = pl.multiple_of(r * SEQ, SEQ)
        c = c_all[pl.ds(rows, SEQ), :]
        c_ref[...] = c
        y1 = x_ref[pl.ds(rows, SEQ), :].astype(f32) + (
            nn(c, weight(3)) + table_ref[BO : BO + 1, :]
        )
        y1_ref[...] = y1
        z1, _ = norm_stats(y1)
        n1 = (z1 * table_ref[G1 : G1 + 1, :] + table_ref[C1 : C1 + 1, :]).astype(bf16)
        n1_ref[...] = n1
        for f in range(4):
            cols = slice(f * CHUNK, (f + 1) * CHUNK)
            u = nn(n1, weight(4 + f)) + table_ref[B1 + f : B1 + f + 1, :]
            cdf, gauss = normal_cdf(u)
            g_ref[:, cols] = (u * cdf).astype(bf16)
            gp_ref[:, cols] = (cdf + u * (gauss * 0.3989422804014327)).astype(bf16)
        if nz:
            pl.when(s == att + 3)(gather.rest)


def constant(shape):
    return pl.BlockSpec(shape, lambda s: (0,) * len(shape), pipeline_mode=pl.Buffered(1))


def front(x, row_codes, col_codes, table, weights, chips=0):
    tokens = x.shape[0]
    rows = tokens // SEQ
    assert rows == 4
    att = GROUPS * rows
    nz = chips // 4

    def code_at(s):
        return (jnp.where(s < att, s % rows, rows - 1), 0, 0)

    def head_at(s):
        return (jnp.where(s < att, s % rows, rows - 1), jnp.minimum(s // rows, GROUPS - 1))

    def tile_at(s):
        return (jnp.maximum(s - att, 0), 0)

    anywhere = pl.BlockSpec(memory_space=pl.ANY)
    narrow = pl.BlockSpec((SEQ, D), tile_at)
    head = pl.BlockSpec((SEQ, WIDE), head_at)
    wide = pl.BlockSpec((SEQ, FF), tile_at)
    in_specs = [
        constant((tokens, D)),
        pl.BlockSpec((1, 8, SEQ), code_at),
        pl.BlockSpec((1, SEQ, BAND), code_at),
        constant((TABLE, CHUNK)),
    ]
    out_specs = [
        head, head, head,
        pl.BlockSpec((1, 8, PACK * BAND), lambda s: (jnp.minimum(s, att - 1), 0, 0)),
        narrow, narrow, narrow, wide, wide,
    ]
    low = jax.ShapeDtypeStruct((tokens, D), bf16)
    out_shape = [
        low, low, low,
        jax.ShapeDtypeStruct((att, 8, PACK * BAND), f32),
        low,
        jax.ShapeDtypeStruct((tokens, D), f32),
        low,
        jax.ShapeDtypeStruct((tokens, FF), bf16),
        jax.ShapeDtypeStruct((tokens, FF), bf16),
    ]
    if nz:
        step = CHUNK // chips
        in_specs += [constant(w.shape) for w in weights]
        out_specs += [anywhere, anywhere, pl.BlockSpec((TABLE, CHUNK), lambda s: (0, 0))]
        out_shape += [
            jax.ShapeDtypeStruct((8, chips, step, CHUNK), bf16),
            jax.ShapeDtypeStruct((chips, 4, step, CHUNK), bf16),
            jax.ShapeDtypeStruct((TABLE, CHUNK), f32),
        ]
        dma = pltpu.SemaphoreType.DMA
        scratch = [
            pltpu.VMEM((tokens, D), bf16),
            pltpu.VMEM((CHUNKS, chips, step, CHUNK), bf16),
            pltpu.VMEM((CHUNKS, step, HALF), bf16),
            *(pltpu.VMEM(w.shape, f32) for w in weights),
            pltpu.VMEM((2, TABLE, CHUNK), bf16),
            pltpu.VMEM((nz + 3, TABLE, CHUNK), bf16),
            dma((2, CHUNKS, nz - 1)), dma((2, CHUNKS, 4)), dma((CHUNKS,)), dma((CHUNKS,)),
            dma((2, 5)), dma((2, nz + 3)),
        ]
        params = pltpu.CompilerParams(
            vmem_limit_bytes=VMEM, collective_id=0, has_side_effects=True
        )
    else:
        in_specs.append(anywhere)
        scratch = [
            pltpu.VMEM((tokens, D), bf16),
            pltpu.VMEM(weights[0].shape, bf16),
            pltpu.SemaphoreType.DMA,
        ]
        params = pltpu.CompilerParams(vmem_limit_bytes=VMEM)
    return pl.pallas_call(
        partial(front_kernel, nz),
        grid=(att + rows,),
        in_specs=in_specs,
        out_specs=out_specs,
        out_shape=out_shape,
        scratch_shapes=scratch,
        compiler_params=params,
        name="front",
    )(x, row_codes, col_codes, table, *weights)


def middle_kernel(
    y1_ref, g_ref, gp_ref, cot_ref, vec_ref, wo_ref, w1_ref, w2_ref,
    out_ref, df_ref, du_ref, dy1_ref, da_ref, dc_ref, grads_ref, sums_ref, ups_ref,
):
    s = pl.program_id(0)

    @pl.when(s == 0)
    def _():
        sums_ref[...] = jnp.zeros_like(sums_ref)
        ups_ref[...] = jnp.zeros_like(ups_ref)

    gain1 = vec_ref[G1 : G1 + 1, :]
    gain2 = vec_ref[G2 : G2 + 1, :]
    part = y1_ref.shape[0] // 2
    kept = [{}, {}]

    def down(h):
        rows = slice(h * part, (h + 1) * part)
        kept[h]["f"] = nn(g_ref[rows, :], w2_ref[...])

    def norm_two(h):
        rows = slice(h * part, (h + 1) * part)
        z1, r1 = norm_stats(y1_ref[rows, :])
        n1 = z1 * gain1 + vec_ref[C1 : C1 + 1, :]
        y2 = n1 + (kept[h]["f"] + vec_ref[B2 : B2 + 1, :])
        z2, r2 = norm_stats(y2)
        out_ref[rows, :] = (z2 * gain2 + vec_ref[C2 : C2 + 1, :]).astype(bf16)
        e = cot_ref[rows, :].astype(f32)
        sums_ref[0] += fold_rows(e * z2)
        sums_ref[1] += fold_rows(e)
        dy2 = norm_back(e * gain2, z2, r2)
        df = dy2.astype(bf16)
        df_ref[rows, :] = df
        sums_ref[2] += fold_rows(df.astype(f32))
        kept[h].update(dy2=dy2, df=df)

    def up_grad(h):
        rows = slice(h * part, (h + 1) * part)
        for f in range(4):
            cols = slice(f * CHUNK, (f + 1) * CHUNK)
            dg = nt(kept[h]["df"], w2_ref[cols, :])
            du = (dg * gp_ref[rows, cols].astype(f32)).astype(bf16)
            du_ref[rows, cols] = du
            ups_ref[:, cols] += fold_rows(du.astype(f32))

    def up_back(h):
        rows = slice(h * part, (h + 1) * part)
        dn1 = kept[h]["dy2"]
        for f in range(4):
            dn1 = dn1 + nt(du_ref[rows, f * CHUNK : (f + 1) * CHUNK], w1_ref[f])
        kept[h]["dn1"] = dn1

    def norm_one(h):
        rows = slice(h * part, (h + 1) * part)
        z1, r1 = norm_stats(y1_ref[rows, :])
        dn1 = kept[h]["dn1"]
        sums_ref[3] += fold_rows(dn1 * z1)
        sums_ref[4] += fold_rows(dn1)
        dy1 = norm_back(dn1 * gain1, z1, r1)
        dy1_ref[rows, :] = dy1
        da = dy1.astype(bf16)
        da_ref[rows, :] = da
        sums_ref[5] += fold_rows(da.astype(f32))
        dc_ref[rows, :] = nt(da, wo_ref[0]).astype(bf16)

    for stage in (down, norm_two, up_grad, up_back, norm_one):
        for h in range(2):
            stage(h)

    @pl.when(s == pl.num_programs(0) - 1)
    def _():
        grads_ref[...] = jnp.zeros_like(grads_ref)
        for i, row in enumerate((G2, C2, B2, G1, C1, BO)):
            grads_ref[row : row + 1, :] = jnp.sum(sums_ref[i], axis=0, keepdims=True)
        for f in range(4):
            cols = slice(f * CHUNK, (f + 1) * CHUNK)
            grads_ref[B1 + f : B1 + f + 1, :] = jnp.sum(ups_ref[:, cols], axis=0, keepdims=True)


def chunks_at(count, index):
    return pl.BlockSpec(
        (count, CHUNK, CHUNK), lambda s: (index, 0, 0), pipeline_mode=pl.Buffered(1)
    )


def middle(y1, g, gp, cot, table, wa, w2):
    tokens = y1.shape[0]
    tile = SEQ

    narrow = pl.BlockSpec((tile, D), lambda s: (s, 0))
    wide = pl.BlockSpec((tile, FF), lambda s: (s, 0))
    wide_out = pl.BlockSpec((tile, FF), lambda s: (s, 0))
    return pl.pallas_call(
        middle_kernel,
        grid=(tokens // tile,),
        in_specs=[
            narrow, wide, wide, narrow, constant((TABLE, CHUNK)),
            chunks_at(1, 3), chunks_at(4, 1), constant((FF, D)),
        ],
        out_specs=[
            narrow, narrow, wide_out, narrow, narrow, narrow,
            pl.BlockSpec((TABLE, CHUNK), lambda s: (0, 0)),
        ],
        out_shape=[
            jax.ShapeDtypeStruct((tokens, D), bf16),
            jax.ShapeDtypeStruct((tokens, D), bf16),
            jax.ShapeDtypeStruct((tokens, FF), bf16),
            jax.ShapeDtypeStruct((tokens, D), f32),
            jax.ShapeDtypeStruct((tokens, D), bf16),
            jax.ShapeDtypeStruct((tokens, D), bf16),
            jax.ShapeDtypeStruct((TABLE, CHUNK), f32),
        ],
        scratch_shapes=[pltpu.VMEM((6, 8, D), f32), pltpu.VMEM((8, FF), f32)],
        compiler_params=pltpu.CompilerParams(vmem_limit_bytes=VMEM),
        name="middle",
    )(y1, g, gp, cot, table, wa, wa, w2)


UP, PROJ, DOWN, QKV = 0, 4, 5, 9
OUTERS = 9


class Reduce:
    def __init__(self, nz, grads, made, local, bufs, fin, outs, sems):
        self.at = Place(nz)
        self.nz, self.grads, self.made, self.local = nz, grads, made, local
        self.bufs, self.fin, self.outs = bufs, fin, outs
        self.c_sem, self.l_sem, self.q_sem, self.z_sem, self.f_sem = sems

    TURNS = (-1, 0, 2, 4, 6, 7)

    def pump(self, s):
        for j in (5, 4, 3, 2, 1, 0):
            turn = s - 4 - self.TURNS[j]
            r = (2 * turn + 1) // 3
            due = (turn >= 0) & (turn % 3 != 2) & (r < QKV)
            pl.when(due)(partial(self.act, j, r))

        @pl.when(s >= 16)
        def _():
            for hg, turns in ((0, (16, 17, 19, 21, 22, 23)), (1, (18, 19, 21, 22, 23, 24))):
                for j in (5, 4, 3, 2, 1, 0):
                    pl.when(s == turns[j])(partial(self.act, j, QKV + hg))

    def source(self, r, lanes, fn):
        g2, g19 = self.grads
        if isinstance(r, int):
            fn(self.made.at[r - QKV, :, :, :, lanes])
            return
        pl.when(r >= DOWN)(lambda: fn(g2.at[:, :, r - DOWN, :, lanes]))
        pl.when(r < DOWN)(lambda: fn(g19.at[r, :, :, :, lanes]))

    def act(self, j, r):
        at, nz = self.at, self.nz
        r0, r1, r2, r3 = self.bufs
        fin, got = self.fin
        c, x, y, z = at.c, at.x, at.y, at.z
        half = [pl.ds(pl.multiple_of(i * HALF, HALF), HALF) for i in (c, 1 - c)]

        def c_copy(src):
            return remote(src, r0.at[r], self.c_sem.at[0, r], self.c_sem.at[1, r], at.other)

        def l_copy(src):
            return pltpu.make_async_copy(src, self.local.at[r % 2], self.l_sem.at[r % 2])

        def a_copy(i):
            q = (1 - c) * (2 * i + 1 - x) + c * (2 * (1 - y) + i)
            return remote(
                r0.at[r, q], r1.at[r, i],
                self.q_sem.at[0, r, i], self.q_sem.at[1, r, i], at.first,
            )

        keep = (1 - c) * y + c * x

        def b_copy():
            return remote(
                r1.at[r, 1 - keep], r2.at[r],
                self.q_sem.at[0, r, 2], self.q_sem.at[1, r, 2], at.second,
            )

        def z_copy(i):
            return remote(
                r2.at[r, (z + i) % nz], r3.at[r, i - 1],
                self.z_sem.at[0, r, i - 1], self.z_sem.at[1, r, i - 1], at.along_z(i),
            )

        def f_copy():
            return remote(fin.at[r], got.at[r], self.f_sem.at[0, r], self.f_sem.at[1, r], at.other)

        rows = fin.shape[1] // 2
        if j == 0:
            self.source(r, half[1], lambda src: c_copy(src).start())
            if not isinstance(r, int):
                self.source(r, half[0], lambda src: l_copy(src).start())
        elif j == 1:
            if isinstance(r, int):
                c_copy(self.made.at[r - QKV, :, :, :, half[1]]).wait()
                own = self.made.at[r - QKV]
                mine = jnp.where(c == 0, own[:, :, :, :HALF], own[:, :, :, HALF:])
            else:
                self.source(r, half[1], lambda src: c_copy(src).wait())
                self.source(r, half[0], lambda src: l_copy(src).wait())
                mine = self.local[r % 2]
            r0[r] = r0[r] + mine
            a_copy(0).start()
            a_copy(1).start()
        elif j == 2:
            for i in (0, 1):
                a_copy(i).wait()
                q = (1 - c) * (2 * i + x) + c * (2 * y + i)
                r1[r, i] = r1[r, i] + r0[r, q]
            b_copy().start()
        elif j == 3:
            b_copy().wait()
            r2[r] = r2[r] + r1[r, keep]
            for i in range(1, nz):
                z_copy(i).start()
        elif j == 4:
            total = r2[r, z].astype(f32)
            for i in range(1, nz):
                z_copy(i).wait()
                total = total + r3[r, i - 1].astype(f32)
            fin[r] = total
            f_copy().start()
        else:
            f_copy().wait()
            self.finish(r, rows)

    def finish(self, r, rows):
        c = self.at.c
        fin, got = self.fin
        out, out_down = self.outs
        even = c == 0

        def sides(own, other):
            return jnp.concatenate(
                [jnp.where(even, own, other), jnp.where(even, other, own)], axis=1
            )

        def down():
            @pl.when(c == (r - DOWN) // 2)
            def _():
                out_down[(r - DOWN) % 2] = sides(fin[r], got[r])

        def rest():
            own = jnp.where(even, fin[r, :rows, :], fin[r, rows:, :])
            other = jnp.where(even, got[r, :rows, :], got[r, rows:, :])
            out[r if not isinstance(r, int) else r - QKV + DOWN] = sides(own, other)

        if isinstance(r, int):
            rest()
        else:
            pl.when(r >= DOWN)(down)
            pl.when(r < DOWN)(rest)


def back_kernel(comm, nz, *refs):
    (
        x_hbm, row_ref, col_ref, wa_hbm, q_ref, k_ref, v_ref, dc_ref, lse_ref, dy1_ref, table_ref,
        g_hbm, df_hbm, n1_hbm, du_hbm, c_hbm, da_hbm,
        g2_hbm, g19_hbm, out, out_down, total_ref, dx_ref,
        x_ref, wqkv_ref, work, res, made, dk_sum, dv_sum, qv_sum, in_sem, res_sem,
    ) = refs[:33]
    s = pl.program_id(0)
    att = GROUPS * 4
    end = OUTERS + att
    if comm:
        local, r0, r1, r2, r3, fin, got, mine, came = refs[33:42]
        sems, v_sem = refs[42:47], refs[47]
        reduce = Reduce(
            nz, (g2_hbm, g19_hbm), made, local, (r0, r1, r2, r3), (fin, got), (out, out_down), sems
        )
        at = reduce.at

        pl.when(s == 0)(at.greet)
        pl.when(s == 3)(at.meet)

    def bring(src, dst, i):
        return pltpu.make_async_copy(src, dst, in_sem.at[i])

    def stream(i, fn):
        cols = pl.ds(pl.multiple_of(i % 4 * CHUNK, CHUNK), CHUNK)
        down = pl.ds(pl.multiple_of((i + 3) % 4 * CHUNK, CHUNK), CHUNK)
        slot = i % 2
        pl.when(i < PROJ)(lambda: fn(bring(du_hbm.at[:, cols], work.at[slot], slot)))
        pl.when(i == PROJ)(lambda: fn(bring(c_hbm, work.at[slot], slot)))
        pl.when(i >= DOWN)(lambda: fn(bring(g_hbm.at[:, down], work.at[slot], slot)))

    def store(i, fn):
        slot = i % 2
        pl.when(i >= DOWN)(
            lambda: fn(pltpu.make_async_copy(res.at[slot], g2_hbm.at[i - DOWN], res_sem.at[slot]))
        )
        pl.when(i < DOWN)(
            lambda: fn(pltpu.make_async_copy(res.at[slot], g19_hbm.at[i], res_sem.at[slot]))
        )

    whole_da = bring(da_hbm, work.at[2], 2)
    whole_n1, whole_df = bring(n1_hbm, work.at[3], 3), bring(df_hbm, work.at[3], 3)
    whole_x = bring(x_hbm, x_ref, 4)
    whole_w = bring(wa_hbm.at[0:GROUPS], wqkv_ref, 5)

    @pl.when(s == 0)
    def _():
        stream(s, lambda copy: copy.start())
        whole_n1.start()
        stream(s + 1, lambda copy: copy.start())
        whole_da.start()
        whole_n1.wait()
        qv_sum[...] = jnp.zeros_like(qv_sum)

    pl.when((s >= 2) & (s < OUTERS + 2))(lambda: store(s - 2, lambda copy: copy.wait()))
    if comm:
        reduce.pump(s)

    @pl.when(s < OUTERS)
    def _():
        stream(s, lambda copy: copy.wait())
        pl.when(s == PROJ)(lambda: whole_da.wait())
        pl.when(s == DOWN)(lambda: whole_df.wait())
        def put(product):
            res[s % 2] = product.astype(bf16).reshape(res.shape[1:])

        @pl.when(s < PROJ)
        def _():
            put(tn(work[3], work[s % 2]))

        @pl.when(s == PROJ)
        def _():
            put(tn(work[s % 2], work[2]))

        @pl.when(s >= DOWN)
        def _():
            put(tn(work[s % 2], work[3]))

        store(s, lambda copy: copy.start())
        pl.when(s < OUTERS - 2)(lambda: stream(s + 2, lambda copy: copy.start()))
        pl.when(s == PROJ - 1)(lambda: whole_df.start())

        @pl.when(s == 2)
        def _():
            whole_x.start()
            whole_w.start()

        @pl.when(s == OUTERS - 1)
        def _():
            whole_x.wait()
            whole_w.wait()

    @pl.when((s >= OUTERS) & (s < end))
    def _():
        hg = (s - OUTERS) // 4
        r = (s - OUTERS) % 4
        rows = pl.multiple_of(r * SEQ, SEQ)
        lanes = pl.ds(pl.multiple_of(hg * WIDE, WIDE), WIDE)
        kt = k_ref[...].T
        dk_sum[...] = jnp.zeros_like(dk_sum)
        dv_sum[...] = jnp.zeros_like(dv_sum)
        masks = head_masks()
        places = list(windows())

        def begin(b, first, width):
            block, span = slice(b * BAND, (b + 1) * BAND), slice(first, first + width)
            qc = spread_heads(q_ref[block, :], masks)
            dcc = spread_heads(dc_ref[block, :], masks)
            return qc, dcc, nt(k_ref[span, :], qc), nt(v_ref[span, :], dcc)

        ahead = begin(*places[0])
        for b, first, width in places:
            span = slice(first, first + width)
            qc, dcc, t, dp = ahead
            if b + 1 < len(places):
                ahead = begin(*places[b + 1])
            t = t * SCORE + mask_bias(col_ref.at[0], row_ref.at[0], b, first, width)
            p = jnp.exp2(t - lse_ref[0, b : b + 1, :])
            pdp = p * dp
            weighted = jnp.sum(pdp, axis=0, keepdims=True)
            ds = (pdp - p * weighted).astype(bf16)
            dv_sum[span, :] += nn(p.astype(bf16), dcc)
            dk_sum[span, :] += nn(ds, qc)
            dqt = nn(kt[:, span], ds)
            dq = (pick_heads(dqt).T * HEAD_DIM ** (-0.5)).astype(bf16)
            work[hg, pl.ds(rows + b * BAND, BAND), 0:WIDE] = dq
            qv_sum[0, :, lanes] += fold_rows(dq.astype(f32))
        dk = (dk_sum[...] * HEAD_DIM ** (-0.5)).astype(bf16)
        dv = dv_sum[...].astype(bf16)
        work[hg, pl.ds(rows, SEQ), WIDE : 2 * WIDE] = dk
        work[hg, pl.ds(rows, SEQ), 2 * WIDE :] = dv
        qv_sum[1, :, lanes] += fold_rows(dv.astype(f32))

        @pl.when(r == 3)
        def _():
            made[hg] = tn(x_ref[...], work[hg]).astype(bf16).reshape(made.shape[1:])

    last = QKV + GROUPS - 1
    if comm:
        def vec_copy(i, src, device):
            return remote(src, came.at[i], v_sem.at[0, i], v_sem.at[1, i], device)

        c_copy = vec_copy(0, mine.at[0], at.other)
        z_copies = [vec_copy(i, mine.at[1], at.along_z(i)) for i in range(1, nz)]
        near = [
            vec_copy(nz + i, mine.at[2], device)
            for i, device in enumerate((at.first, at.second, at.far))
        ]

        @pl.when(s == end - 1)
        def _():
            reduce.act(0, last)
            mine[0] = table_ref[...]
            mine[0, BQ : BQ + 1, :] = jnp.sum(qv_sum[0], axis=0, keepdims=True)
            mine[0, BV : BV + 1, :] = jnp.sum(qv_sum[1], axis=0, keepdims=True)
            c_copy.start()

        @pl.when(s == end)
        def _():
            reduce.act(1, last)
            c_copy.wait()
            mine[1] = mine[0] + came[0]
            for copy in z_copies:
                copy.start()

        @pl.when(s == end + 1)
        def _():
            reduce.act(3, last)
            total = mine[1]
            for i in range(1, nz):
                z_copies[i - 1].wait()
                total = total + came[i]
            mine[2] = total
            for copy in near:
                copy.start()

    @pl.when(s >= end)
    def _():
        half = SEQ // 2
        for h in range(2):
            if h == 1 and comm:
                pl.when(s == end)(lambda: reduce.act(2, last))
                pl.when(s == end + 1)(lambda: reduce.act(4, last))
            rows = pl.ds(pl.multiple_of((s - end) * SEQ + h * half, half), half)
            total = dy1_ref[h * half : (h + 1) * half, :]
            for hg in range(GROUPS):
                total = total + nt(work[hg, rows, :], wqkv_ref[hg].reshape(CHUNK, CHUNK))
            dx_ref[h * half : (h + 1) * half, :] = total

    @pl.when(s == end + 3)
    def _():
        if comm:
            for copy in near:
                copy.wait()
            total_ref[...] = mine[2] + came[nz] + came[nz + 1] + came[nz + 2]
            reduce.act(5, last)
        else:
            total_ref[...] = table_ref[...]
            total_ref[BQ : BQ + 1, :] = jnp.sum(qv_sum[0], axis=0, keepdims=True)
            total_ref[BV : BV + 1, :] = jnp.sum(qv_sum[1], axis=0, keepdims=True)
            out[...] = jnp.zeros_like(out)
            out_down[...] = jnp.zeros_like(out_down)


def back(x, row_codes, col_codes, wa, q, k, v, dc, lse, dy1, table, pairs, chips, comm):
    tokens = x.shape[0]
    rows = tokens // SEQ
    att = GROUPS * rows
    end = OUTERS + att
    assert rows == 4
    nz = chips // 4
    step = CHUNK // chips

    def turn(s):
        return jnp.clip(s - OUTERS, 0, att - 1)

    def code_at(s):
        return (turn(s) % rows, 0, 0)

    def head_at(s):
        return (turn(s) % rows, turn(s) // rows)

    def tile_at(s):
        return (jnp.maximum(s - end, 0), 0)

    anywhere = pl.BlockSpec(memory_space=pl.ANY)
    whole_table = pl.BlockSpec((TABLE, CHUNK), lambda s: (0, 0))
    head = pl.BlockSpec((SEQ, WIDE), head_at)
    tile = pl.BlockSpec((SEQ, D), tile_at)
    made_shape = (GROUPS, 4, nz, step, CHUNK)
    dma = pltpu.SemaphoreType.DMA
    scratch = [
        pltpu.VMEM((tokens, D), bf16),
        pltpu.VMEM((GROUPS, *wa.shape[1:]), bf16),
        pltpu.VMEM((4, tokens, CHUNK), bf16),
        pltpu.VMEM((2, 4, nz, step, CHUNK), bf16),
    ]
    if comm:
        scratch.append(pltpu.VMEM(made_shape, bf16))
    scratch += [
        pltpu.VMEM((SEQ, WIDE), f32),
        pltpu.VMEM((SEQ, WIDE), f32),
        pltpu.VMEM((2, 8, D), f32),
        dma((6,)), dma((2,)),
    ]
    out_specs = [
        anywhere, anywhere,
        pl.BlockSpec((8, step // 2, CHUNK), lambda s: (0, 0, 0)),
        pl.BlockSpec((2, step, CHUNK), lambda s: (0, 0, 0)),
        whole_table, tile,
    ]
    out_shape = [
        jax.ShapeDtypeStruct((4, nz, 4, step, CHUNK), bf16),
        jax.ShapeDtypeStruct((5, 4, nz, step, CHUNK), bf16),
        jax.ShapeDtypeStruct((8, step // 2, CHUNK), f32),
        jax.ShapeDtypeStruct((2, step, CHUNK), f32),
        jax.ShapeDtypeStruct((TABLE, CHUNK), f32),
        jax.ShapeDtypeStruct((tokens, D), f32),
    ]
    kernel = partial(back_kernel, comm, nz)
    if comm:
        scratch += [
            pltpu.VMEM((2, 4, nz, step, HALF), bf16),
            pltpu.VMEM((CHUNKS, 4, nz, step, HALF), bf16),
            pltpu.VMEM((CHUNKS, 2, nz, step, HALF), bf16),
            pltpu.VMEM((CHUNKS, nz, step, HALF), bf16),
            pltpu.VMEM((CHUNKS, nz - 1, step, HALF), bf16),
            pltpu.VMEM((CHUNKS, step, HALF), f32),
            pltpu.VMEM((CHUNKS, step, HALF), f32),
            pltpu.VMEM((3, TABLE, CHUNK), f32),
            pltpu.VMEM((nz + 3, TABLE, CHUNK), f32),
            dma((2, CHUNKS)), dma((2,)), dma((2, CHUNKS, 3)), dma((2, CHUNKS, nz - 1)),
            dma((2, CHUNKS)), dma((2, nz + 3)),
        ]
        params = pltpu.CompilerParams(
            vmem_limit_bytes=VMEM, collective_id=1, has_side_effects=True
        )
    else:
        def kernel(*refs):
            refs = list(refs)
            made = refs.pop(23)
            refs.insert(27, made)
            back_kernel(comm, nz, *refs)

        out_specs.append(pl.BlockSpec(made_shape, lambda s: (0,) * 5, pipeline_mode=pl.Buffered(1)))
        out_shape.append(jax.ShapeDtypeStruct(made_shape, bf16))
        params = pltpu.CompilerParams(vmem_limit_bytes=VMEM)
    return pl.pallas_call(
        kernel,
        grid=(end + rows,),
        in_specs=[
            anywhere,
            pl.BlockSpec((1, 8, SEQ), code_at),
            pl.BlockSpec((1, SEQ, BAND), code_at),
            anywhere,
            head, head, head, head,
            pl.BlockSpec((1, 8, PACK * BAND), lambda s: (turn(s), 0, 0)),
            tile, whole_table,
            *(anywhere for _ in pairs),
        ],
        out_specs=out_specs,
        out_shape=out_shape,
        scratch_shapes=scratch,
        compiler_params=params,
        name="back",
    )(x, row_codes, col_codes, wa, q, k, v, dc, lse, dy1, table, *pairs)


def update(grad, master, moment, average, tokens_all):
    mean_grad = grad / tokens_all
    moment_new = momentum_coef * moment + mean_grad
    step_size = -learn_rate * (mean_grad + momentum_coef * moment_new)
    master_new = master + step_size
    average_new = average_keep * average + (1.0 - average_keep) * master_new
    return (master_new, moment_new, average_new)


def update_steps(grad, master, moment, average, tokens_all):
    mean_grad = grad / tokens_all
    moment_new = momentum_coef * moment + mean_grad
    step_size = -learn_rate * (mean_grad + momentum_coef * moment_new)
    average_step = (1.0 - average_keep) * (master + step_size - average)
    return (step_size, moment_new, average_step)


def update_kernel(tokens_all, *refs):
    grad_ref, down_ref, dx_ref = refs[:3]
    states, outs, dx_out, kept, sem = refs[3:15], refs[15:31], *refs[31:34]
    parts = kept.shape[0]
    spans = [pl.ds(i * kept.shape[1], kept.shape[1]) for i in range(parts)]
    loads = [
        pltpu.make_async_copy(dx_ref.at[span], kept.at[i], sem.at[0, i])
        for i, span in enumerate(spans)
    ]
    saves = [
        pltpu.make_async_copy(kept.at[i], dx_out.at[span], sem.at[1, i])
        for i, span in enumerate(spans)
    ]
    for load in loads:
        load.start()

    def one(i, index, grad):
        master, moment, average = (states[i + 4 * j][index] for j in range(3))
        outs[i][index] = grad
        new = update(grad, master, moment, average, tokens_all)
        for j in range(3):
            outs[i + 4 * (j + 1)][index] = new[j]

    rows = grad_ref.shape[1]
    for i in range(parts):
        loads[i].wait()
        saves[i].start()
    for hg in range(GROUPS):
        for i in range(3):
            cols = slice(i * D + hg * WIDE, i * D + (hg + 1) * WIDE)
            one(0, (slice(None), cols), grad_ref[5 + hg, :, i * WIDE : (i + 1) * WIDE])
    one(1, (slice(None), slice(None)), grad_ref[4])
    for f in range(4):
        one(2, (slice(None), slice(f * CHUNK, (f + 1) * CHUNK)), grad_ref[f])
    for i in range(2):
        one(3, (slice(2 * rows * i, 2 * rows * (i + 1)), slice(None)), down_ref[i])
    for save in saves:
        save.wait()


def update_weights(grads, grads_down, dx, states, tokens_all):
    whole = pl.BlockSpec(memory_space=pltpu.VMEM)
    anywhere = pl.BlockSpec(memory_space=pl.ANY)
    shapes = [jax.ShapeDtypeStruct(w.shape, f32) for w in states[:4]]
    return pl.pallas_call(
        partial(update_kernel, tokens_all),
        in_specs=[whole] * 2 + [anywhere] + [whole] * 12,
        out_specs=[whole] * 16 + [anywhere],
        out_shape=shapes * 4 + [jax.ShapeDtypeStruct(dx.shape, f32)],
        scratch_shapes=[
            pltpu.VMEM((8, dx.shape[0] // 8, D), f32), pltpu.SemaphoreType.DMA((2, 8)),
        ],
        compiler_params=pltpu.CompilerParams(vmem_limit_bytes=VMEM),
        name="update",
    )(grads, grads_down, dx, *states)


def group_columns(w):
    n = w.shape[0]
    return w.reshape(n, 3, GROUPS, WIDE).transpose(2, 0, 1, 3).reshape(GROUPS, n, 3 * WIDE)


def ungroup_columns(w):
    n = w.shape[1]
    return w.reshape(GROUPS, n, 3, WIDE).transpose(1, 2, 0, 3).reshape(n, 3 * D)


def table_of(gains, biases):
    flat = jnp.concatenate([gains, biases, jnp.zeros((TABLE * CHUNK - 9216,), gains.dtype)])
    return flat.reshape(TABLE, CHUNK)


def on_device(
    tokens, segment_ids, pad_counts, out_cotangent,
    qkv_master, proj_master, up_master, down_master, gain_master, bias_master,
    qkv_moment, proj_moment, up_moment, down_moment, gain_moment, bias_moment,
    qkv_average, proj_average, up_average, down_average, gain_average, bias_average,
):
    axes = ("gx", "gy")
    devices = lax.axis_size(axes)
    seq_len = segment_ids.shape[1]
    tokens_all = tokens.shape[0] * devices
    position = jnp.arange(seq_len, dtype=jnp.int32)
    is_pad = position[None, :] >= (seq_len - pad_counts)[:, None]
    codes = segment_ids * 2 + is_pad.astype(jnp.int32)
    row_codes = jnp.broadcast_to(codes[:, None, :], (codes.shape[0], 8, seq_len))
    col_codes = jnp.broadcast_to(codes[:, :, None], (codes.shape[0], seq_len, BAND))
    gain_len, bias_len = gain_master.shape[0], bias_master.shape[0]
    gains = gain_len * devices
    place = lax.axis_index(axes)

    fine = lax.axis_size("gx") == 4 and lax.axis_size("gy") == 8
    if fine:
        chips = devices // 2
        part = jnp.zeros((TABLE * CHUNK,), bf16)
        part = lax.dynamic_update_slice(part, gain_master.astype(bf16), (place * gain_len,))
        part = lax.dynamic_update_slice(
            part, bias_master.astype(bf16), (gains + place * bias_len,)
        ).reshape(TABLE, CHUNK)
        q, k, v, lse, c, y1, n1, g, gp, wa, w2, table = front(
            tokens, row_codes, col_codes, part,
            (qkv_master, proj_master, up_master, down_master), chips,
        )
        w2 = w2.reshape(FF, D)
    else:
        gather = partial(lax.all_gather, axis_name=axes, axis=0, tiled=True)
        w1 = gather(up_master.astype(bf16))
        wa = jnp.concatenate(
            [
                group_columns(gather(qkv_master.astype(bf16))),
                gather(proj_master.astype(bf16))[None],
                w1.reshape(D, 4, CHUNK).transpose(1, 0, 2),
            ]
        ).reshape(8, 16, CHUNK // 16, CHUNK)
        w2 = gather(down_master.astype(bf16))
        table = table_of(
            gather(gain_master.astype(bf16)), gather(bias_master.astype(bf16))
        ).astype(f32)
        q, k, v, lse, c, y1, n1, g, gp = front(
            tokens, row_codes, col_codes, table, (wa,)
        )
    layer_output, df, du, dy1, da, dc, terms = middle(
        y1, g, gp, out_cotangent, table, wa.reshape(8, CHUNK, CHUNK), w2
    )
    results = back(
        tokens, row_codes, col_codes, wa, q, k, v, dc, lse, dy1, terms,
        (g, df, n1, du, c, da), chips if fine else 16, fine,
    )
    input_grad = results[5]
    scatter = partial(lax.psum_scatter, axis_name=axes, scatter_dimension=0, tiled=True)
    states = (
        qkv_master, proj_master, up_master, down_master,
        qkv_moment, proj_moment, up_moment, down_moment,
        qkv_average, proj_average, up_average, down_average,
    )
    if fine:
        grads, grads_down, terms = results[2:5]
        new = update_weights(grads, grads_down, input_grad, states, tokens_all)
        shares, masters, moments, averages = new[:4], new[4:8], new[8:12], new[12:16]
        input_grad = new[16]
        terms = terms.reshape(-1)
        gain_share = lax.dynamic_slice(terms, (place * gain_len,), (gain_len,))
        bias_share = lax.dynamic_slice(terms, (gains + place * bias_len,), (bias_len,))
    else:
        down_part, rest, terms, dwqkv = (results[i].astype(f32) for i in (0, 1, 4, 6))
        rest = rest.reshape(5, CHUNK, CHUNK)
        terms = terms.reshape(-1)
        shares = (
            scatter(ungroup_columns(dwqkv.reshape(GROUPS, CHUNK, CHUNK))),
            scatter(rest[4]),
            scatter(rest[:4].transpose(1, 0, 2).reshape(D, FF)),
            scatter(down_part.reshape(FF, D)),
        )
        news = [
            update(shares[i], states[i], states[4 + i], states[8 + i], tokens_all)
            for i in range(4)
        ]
        masters, moments, averages = zip(*news)
        gain_share = scatter(terms[:gains])
        bias_share = scatter(terms[gains : gains + bias_len * devices])
    gain_new = update_steps(gain_share, gain_master, gain_moment, gain_average, tokens_all)
    bias_new = update(bias_share, bias_master, bias_moment, bias_average, tokens_all)
    return (
        layer_output, input_grad, *shares, gain_share, bias_share,
        *masters, gain_new[0], bias_new[0],
        *moments, gain_new[1], bias_new[1],
        *averages, gain_new[2], bias_new[2],
    )


def solution(mesh):
    both = ("gx", "gy")
    two, one = P(both, None), P(both)
    weights = (two, two, two, two, one, one)
    in_specs = (two, two, one, two) + weights * 3
    out_specs = (two, two) + weights * 4
    return jax.shard_map(
        on_device, mesh=mesh, in_specs=in_specs, out_specs=out_specs, check_vma=False
    )
```

```python
from functools import partial

import jax
import jax.numpy as jnp
from jax import lax
from jax.experimental import pallas as pl
from jax.experimental.pallas import tpu as pltpu
from jax.sharding import PartitionSpec as P

D = 768
HEADS = 12
HEAD_DIM = 64
FF = 3072
SEQ = 512
BAND = 128
PACK = 4
GROUPS = HEADS // PACK
WIDE = PACK * HEAD_DIM
VMEM = 60 * 1024 * 1024

norm_eps = 1e-06
momentum_coef = 0.9
learn_rate = 4.0
average_keep = 0.9

G1, G2, BQ, BV, BO, C1, B1, B2, C2 = (0, 1, 2, 3, 4, 5, 6, 10, 11)
TABLE = 16
CHUNK = 768
CHUNKS = 12
HALF = CHUNK // 2
MESH = pl.DeviceIdType.MESH

f32 = jnp.float32
bf16 = jnp.bfloat16

LOG2E = 1.4426950408889634
SCORE = HEAD_DIM ** (-0.5) * LOG2E


def nn(a, b):
    return lax.dot_general(a, b, (((1,), (0,)), ((), ())), preferred_element_type=f32)


def nt(a, b):
    return lax.dot_general(a, b, (((1,), (1,)), ((), ())), preferred_element_type=f32)


def tn(a, b):
    return lax.dot_general(a, b, (((0,), (0,)), ((), ())), preferred_element_type=f32)


def normal_cdf(u):
    gauss = jnp.exp2(u * u * (-0.5 * LOG2E))
    return 0.5 + 0.5 * lax.erf(u * 0.7071067811865476), gauss


def windows():
    for b in range(SEQ // BAND):
        first = max(0, (b - 1) * BAND)
        last = min(SEQ, (b + 2) * BAND)
        yield b, first, last - first


def head_masks():
    lane = lax.broadcasted_iota(jnp.int32, (BAND, WIDE), 1) // HEAD_DIM
    return [jnp.where(lane == h, 1.0, 0.0).astype(bf16) for h in range(PACK)]


def spread_heads(block, masks):
    return jnp.concatenate([block * m for m in masks], axis=0)


def pick_heads(wide):
    return jnp.concatenate(
        [
            wide[h * HEAD_DIM : (h + 1) * HEAD_DIM, h * BAND : (h + 1) * BAND]
            for h in range(PACK)
        ],
        axis=0,
    )


def mask_bias(col, row, b, first, width):
    keys = col[first : first + width, :]
    queries = row[0:1, b * BAND : (b + 1) * BAND]
    bias = jnp.where(keys == queries, 0.0, -1e30)
    return jnp.concatenate([bias] * PACK, axis=1)


def norm_stats(y):
    centre = jnp.mean(y, axis=-1, keepdims=True)
    centred = y - centre
    spread = jnp.mean(centred * centred, axis=-1, keepdims=True)
    r = lax.rsqrt(spread + norm_eps)
    return centred * r, r


def norm_back(dz, z, r):
    return r * (
        dz
        - jnp.mean(dz, axis=-1, keepdims=True)
        - z * jnp.mean(dz * z, axis=-1, keepdims=True)
    )


def remote(src, dst, send, recv, device):
    return pltpu.make_async_remote_copy(
        src_ref=src, dst_ref=dst, send_sem=send, recv_sem=recv, device_id=device,
        device_id_type=MESH,
    )


class Place:
    def __init__(self, nz):
        gx = lax.axis_index("gx")
        gy = lax.axis_index("gy")
        self.nz = nz
        self.x, self.y = gx % 2, gx // 2
        self.z, self.c = gy // 2, gy % 2
        x, y, z, c = self.x, self.y, self.z, self.c
        self.other = (gx, z * 2 + 1 - c)
        ax, ay = x + (1 - c) * (1 - 2 * x), y + c * (1 - 2 * y)
        bx, by = x + c * (1 - 2 * x), y + (1 - c) * (1 - 2 * y)
        self.first = (ay * 2 + ax, gy)
        self.second = (by * 2 + bx, gy)
        self.far = ((1 - y) * 2 + 1 - x, gy)
        self.quarter = gx
        self.quarter_first = ay * 2 + ax
        self.quarter_second = by * 2 + bx
        self.quarter_far = (1 - y) * 2 + 1 - x

    def along_z(self, j):
        return (self.quarter, (self.z + j) % self.nz * 2 + self.c)

    def greet(self):
        sem = pltpu.get_barrier_semaphore()
        partners = [self.other, self.first, self.second, self.far]
        partners += [self.along_z(j) for j in range(1, self.nz)]
        for p in partners:
            pl.semaphore_signal(sem, inc=1, device_id=p, device_id_type=MESH)

    def meet(self):
        pl.semaphore_wait(pltpu.get_barrier_semaphore(), 4 + self.nz - 1)


def fold_rows(v):
    n = v.shape[0]
    return jnp.sum(v.reshape(n // 8, 8, v.shape[1]), axis=0)


class Gather:
    TURNS = (-3, 0, 2, 4, 5, 6)

    def __init__(self, nz, wa, wb, held, stage, z_sem, s_sem, own_sem, out_sem):
        self.at = Place(nz)
        self.nz, self.wa, self.wb, self.held, self.stage = nz, wa, wb, held, stage
        self.z_sem, self.s_sem, self.own_sem, self.out_sem = z_sem, s_sem, own_sem, out_sem

    def pump(self, s):
        for j in (5, 4, 3, 2, 1, 0):
            turn = s + 3 - self.TURNS[j]
            k = (2 * turn + 1) // 3
            due = (turn % 3 != 2) & (k >= (4, 2, 2, 2, 2, 2)[j]) & (k < CHUNKS - 2)
            pl.when(due)(partial(self.act, j, k))

        @pl.when(s <= 5)
        def _():
            for j, turn in ((2, 1), (3, 3), (4, 4), (5, 5)):
                pl.when(s == turn)(partial(self.act, j, 1))

        @pl.when(s >= 9)
        def _():
            for k in (CHUNKS - 2, CHUNKS - 1):
                for j in range(6):
                    turn = k + (-1, 2, 3, 4, 5, 6)[j]
                    pl.when(s == turn)(partial(self.act, j, k))

    def rest(self):
        self.act(5, CHUNKS - 3)
        self.act(5, CHUNKS - 2)
        self.act(4, CHUNKS - 1)
        self.act(5, CHUNKS - 1)

    def act(self, j, k):
        at, nz = self.at, self.nz
        direct = isinstance(k, int) and k == 0
        mine = pl.ds(pl.multiple_of(at.c * HALF, HALF), HALF)
        others = pl.ds(pl.multiple_of((1 - at.c) * HALF, HALF), HALF)

        def spot(chip, lanes=mine):
            return self.held.at[k, chip, :, lanes]

        def quarter(q):
            return spot(pl.ds(q * nz, nz))

        def z_copy(i, chip):
            return remote(
                self.stage.at[k], spot(chip), self.z_sem.at[0, k, i - 1],
                self.z_sem.at[1, k, i - 1], at.along_z(i),
            )

        def s_copy(i, q, device):
            return remote(
                quarter(q), quarter(q), self.s_sem.at[0, k, i], self.s_sem.at[1, k, i], device
            )

        def far_copy(q):
            if direct:
                return s_copy(2, at.quarter if q is None else q, at.far)
            return s_copy(2, at.quarter_first if q is None else q, at.second)

        def c_copy(lanes):
            whole = spot(slice(None), lanes)
            return remote(
                whole, whole, self.s_sem.at[0, k, 3], self.s_sem.at[1, k, 3], at.other
            )

        def own():
            return pltpu.make_async_copy(self.stage.at[k], spot(chip), self.own_sem.at[k])

        chip = at.quarter * nz + at.z
        if j == 0:
            for i in range(1, nz):
                z_copy(i, chip).start()
            own().start()
        elif j == 1:
            for i in range(1, nz):
                z_copy(i, at.quarter * nz + (at.z - i + nz) % nz).wait_recv()
            own().wait()
            s_copy(0, at.quarter, at.first).start()
            s_copy(1, at.quarter, at.second).start()
            if direct:
                far_copy(None).start()
        elif j == 2:
            s_copy(0, at.quarter_first, at.first).wait_recv()
            if not direct:
                far_copy(None).start()
        elif j == 3:
            s_copy(1, at.quarter_second, at.second).wait_recv()
            far_copy(at.quarter_far).wait_recv()
            c_copy(mine).start()
        elif j == 4:
            c_copy(others).wait_recv()
            for i in range(1, nz):
                z_copy(i, chip).wait_send()
            s_copy(0, at.quarter, at.first).wait_send()
            s_copy(1, at.quarter, at.second).wait_send()
            far_copy(None).wait_send()
            c_copy(mine).wait_send()
            self.keep(k, lambda copy: copy.start())
        else:
            self.keep(k, lambda copy: copy.wait())

    def keep(self, k, fn):
        def early():
            fn(pltpu.make_async_copy(self.held.at[k], self.wa.at[k], self.out_sem.at[k]))

        def late():
            fn(pltpu.make_async_copy(self.held.at[k], self.wb.at[:, k - 8], self.out_sem.at[k]))

        if isinstance(k, int) and k < 8:
            early()
        elif isinstance(k, int):
            late()
        else:
            pl.when(k < 8)(early)
            pl.when(k >= 8)(late)


def share_start(nz, part_ref, masters, sibs, stage, table_ref, sums, got, x_sem, v_sem, gather):
    at = gather.at
    at.greet()
    at.meet()
    swaps = [
        remote(m, o, x_sem.at[0, i], x_sem.at[1, i], at.other)
        for i, (m, o) in enumerate(zip(masters, sibs))
    ]
    swaps.insert(1, remote(part_ref, got.at[0], x_sem.at[0, 4], x_sem.at[1, 4], at.other))
    for swap in swaps:
        swap.start()
    mq, mo, m1, m2 = masters
    sq, so, s1, s2 = sibs
    even = at.c == 0

    def halves(own, sib):
        own = jnp.where(even, own[:, :HALF], own[:, HALF:])
        sib = jnp.where(even, sib[:, :HALF], sib[:, HALF:])
        top, low = jnp.where(even, own, sib), jnp.where(even, sib, own)
        return jnp.concatenate([top, low], axis=0).astype(bf16)

    def group(ref, hg):
        cols = [ref[:, i * D + hg * WIDE : i * D + (hg + 1) * WIDE] for i in range(3)]
        return jnp.concatenate(cols, axis=1)

    def vec_copy(i, src, device):
        return remote(src, got.at[i], v_sem.at[0, i], v_sem.at[1, i], device)

    swaps[0].wait()
    for hg in range(GROUPS):
        stage[hg] = halves(group(mq, hg), group(sq, hg))
        if hg == 0:
            gather.act(0, hg)
    swaps[1].wait()
    sums[0] = part_ref[...] + got[0]
    z_copies = [vec_copy(i, sums.at[0], at.along_z(i)) for i in range(1, nz)]
    for copy in z_copies:
        copy.start()
    for swap in swaps[2:]:
        swap.wait()
    stage[3] = halves(mo[...], so[...])
    for f in range(4):
        cols = slice(f * CHUNK, (f + 1) * CHUNK)
        stage[4 + f] = halves(m1[:, cols], s1[:, cols])
    step = stage.shape[1]
    for i in range(4):
        rows = slice(i % 2 * step, (i % 2 + 1) * step)
        block = jnp.where(at.c == i // 2, m2[rows, :], s2[rows, :])
        stage[8 + i] = jnp.where(even, block[:, :HALF], block[:, HALF:]).astype(bf16)
    for copy in z_copies:
        copy.wait()
    total = sums[0]
    for i in range(1, nz):
        total = total + got[i]
    sums[1] = total
    near = [
        vec_copy(nz + i, sums.at[1], device)
        for i, device in enumerate((at.first, at.second, at.far))
    ]
    gather.act(1, 0)
    for copy in near:
        copy.start()
    gather.act(0, 1)
    gather.act(0, 2)
    gather.act(0, 3)
    gather.act(2, 0)
    gather.act(3, 0)
    for copy in near:
        copy.wait()
    table_ref[...] = (sums[1] + got[nz] + got[nz + 1] + got[nz + 2]).astype(f32)
    gather.act(1, 1)
    gather.act(4, 0)


def front_kernel(nz, *refs):
    refs = list(refs)
    x_ref, row_ref, col_ref, vec_ref = refs[:4]
    s = pl.program_id(0)
    att = GROUPS * 4
    if nz:
        masters, refs = refs[4:8], refs[8:]
    else:
        wa_ref, refs = refs[4], refs[5:]
    q_ref, k_ref, v_ref, lse_ref, c_ref, y1_ref, n1_ref, g_ref, gp_ref = refs[:9]
    refs = refs[9:]
    if nz:
        wa_ref, wb_ref, table_ref = refs[:3]
        c_all, held, stage, sq, so, s1, s2, sums, got = refs[3:12]
        z_sem, s_sem, own_sem, out_sem, x_sem, v_sem = refs[12:]
        gather = Gather(nz, wa_ref, wb_ref, held, stage, z_sem, s_sem, own_sem, out_sem)

        @pl.when(s == 0)
        def _():
            share_start(
                nz, vec_ref, masters, (sq, so, s1, s2), stage, table_ref, sums, got,
                x_sem, v_sem, gather,
            )

        pl.when(s == 2)(partial(gather.act, 5, 0))
        gather.pump(s)
    else:
        c_all, held, load_sem = refs
        table_ref = vec_ref

        @pl.when(s == 0)
        def _():
            copy = pltpu.make_async_copy(wa_ref, held, load_sem)
            copy.start()
            copy.wait()

    def weight(k):
        return held[k].reshape(CHUNK, CHUNK)

    @pl.when(s < att)
    def _():
        hg = s // 4
        r = s % 4
        rows = pl.multiple_of(r * SEQ, SEQ)
        lanes = pl.multiple_of(hg * WIDE, WIDE)
        xr = x_ref[pl.ds(rows, SEQ), :]
        wqkv = weight(hg)
        q = nn(xr, wqkv[:, 0:WIDE]) + table_ref[BQ : BQ + 1, pl.ds(lanes, WIDE)]
        q = q.astype(bf16)
        k = nn(xr, wqkv[:, WIDE : 2 * WIDE]).astype(bf16)
        v = nn(xr, wqkv[:, 2 * WIDE :]) + table_ref[BV : BV + 1, pl.ds(lanes, WIDE)]
        v = v.astype(bf16)
        q_ref[...] = q
        k_ref[...] = k
        v_ref[...] = v
        vt = v.T
        masks = head_masks()
        places = list(windows())

        def begin(b, first, width):
            qc = spread_heads(q[b * BAND : (b + 1) * BAND, :], masks)
            return nt(k[first : first + width, :], qc)

        ahead = begin(*places[0])
        for b, first, width in places:
            t = ahead
            if b + 1 < len(places):
                ahead = begin(*places[b + 1])
            t = t * SCORE + mask_bias(col_ref.at[0], row_ref.at[0], b, first, width)
            m = jnp.max(t, axis=0, keepdims=True)
            e = jnp.exp2(t - m)
            l = jnp.sum(e, axis=0, keepdims=True)
            p = (e * (1.0 / l)).astype(bf16)
            lse_ref[0, b : b + 1, :] = m + jnp.log2(l)
            ot = nn(vt[:, first : first + width], p)
            c = pick_heads(ot).T.astype(bf16)
            c_all[pl.ds(rows + b * BAND, BAND), pl.ds(lanes, WIDE)] = c

    @pl.when(s >= att)
    def _():
        r = s - att
        rows = pl.multiple_of(r * SEQ, SEQ)
        c = c_all[pl.ds(rows, SEQ), :]
        c_ref[...] = c
        y1 = x_ref[pl.ds(rows, SEQ), :].astype(f32) + (
            nn(c, weight(3)) + table_ref[BO : BO + 1, :]
        )
        y1_ref[...] = y1
        z1, _ = norm_stats(y1)
        n1 = (z1 * table_ref[G1 : G1 + 1, :] + table_ref[C1 : C1 + 1, :]).astype(bf16)
        n1_ref[...] = n1
        for f in range(4):
            cols = slice(f * CHUNK, (f + 1) * CHUNK)
            u = nn(n1, weight(4 + f)) + table_ref[B1 + f : B1 + f + 1, :]
            cdf, gauss = normal_cdf(u)
            g_ref[:, cols] = (u * cdf).astype(bf16)
            gp_ref[:, cols] = (cdf + u * (gauss * 0.3989422804014327)).astype(bf16)
        if nz:
            pl.when(s == att + 3)(gather.rest)


def constant(shape):
    return pl.BlockSpec(shape, lambda s: (0,) * len(shape), pipeline_mode=pl.Buffered(1))


def front(x, row_codes, col_codes, table, weights, chips=0):
    tokens = x.shape[0]
    rows = tokens // SEQ
    assert rows == 4
    att = GROUPS * rows
    nz = chips // 4

    def code_at(s):
        return (jnp.where(s < att, s % rows, rows - 1), 0, 0)

    def head_at(s):
        return (jnp.where(s < att, s % rows, rows - 1), jnp.minimum(s // rows, GROUPS - 1))

    def tile_at(s):
        return (jnp.maximum(s - att, 0), 0)

    anywhere = pl.BlockSpec(memory_space=pl.ANY)
    narrow = pl.BlockSpec((SEQ, D), tile_at)
    head = pl.BlockSpec((SEQ, WIDE), head_at)
    wide = pl.BlockSpec((SEQ, FF), tile_at)
    in_specs = [
        constant((tokens, D)),
        pl.BlockSpec((1, 8, SEQ), code_at),
        pl.BlockSpec((1, SEQ, BAND), code_at),
        constant((TABLE, CHUNK)),
    ]
    out_specs = [
        head, head, head,
        pl.BlockSpec((1, 8, PACK * BAND), lambda s: (jnp.minimum(s, att - 1), 0, 0)),
        narrow, narrow, narrow, wide, wide,
    ]
    low = jax.ShapeDtypeStruct((tokens, D), bf16)
    out_shape = [
        low, low, low,
        jax.ShapeDtypeStruct((att, 8, PACK * BAND), f32),
        low,
        jax.ShapeDtypeStruct((tokens, D), f32),
        low,
        jax.ShapeDtypeStruct((tokens, FF), bf16),
        jax.ShapeDtypeStruct((tokens, FF), bf16),
    ]
    if nz:
        step = CHUNK // chips
        in_specs += [constant(w.shape) for w in weights]
        out_specs += [anywhere, anywhere, pl.BlockSpec((TABLE, CHUNK), lambda s: (0, 0))]
        out_shape += [
            jax.ShapeDtypeStruct((8, chips, step, CHUNK), bf16),
            jax.ShapeDtypeStruct((chips, 4, step, CHUNK), bf16),
            jax.ShapeDtypeStruct((TABLE, CHUNK), f32),
        ]
        dma = pltpu.SemaphoreType.DMA
        scratch = [
            pltpu.VMEM((tokens, D), bf16),
            pltpu.VMEM((CHUNKS, chips, step, CHUNK), bf16),
            pltpu.VMEM((CHUNKS, step, HALF), bf16),
            *(pltpu.VMEM(w.shape, f32) for w in weights),
            pltpu.VMEM((2, TABLE, CHUNK), bf16),
            pltpu.VMEM((nz + 3, TABLE, CHUNK), bf16),
            dma((2, CHUNKS, nz - 1)), dma((2, CHUNKS, 4)), dma((CHUNKS,)), dma((CHUNKS,)),
            dma((2, 5)), dma((2, nz + 3)),
        ]
        params = pltpu.CompilerParams(
            vmem_limit_bytes=VMEM, collective_id=0, has_side_effects=True
        )
    else:
        in_specs.append(anywhere)
        scratch = [
            pltpu.VMEM((tokens, D), bf16),
            pltpu.VMEM(weights[0].shape, bf16),
            pltpu.SemaphoreType.DMA,
        ]
        params = pltpu.CompilerParams(vmem_limit_bytes=VMEM)
    return pl.pallas_call(
        partial(front_kernel, nz),
        grid=(att + rows,),
        in_specs=in_specs,
        out_specs=out_specs,
        out_shape=out_shape,
        scratch_shapes=scratch,
        compiler_params=params,
        name="front",
    )(x, row_codes, col_codes, table, *weights)


def middle_kernel(
    y1_ref, g_ref, gp_ref, cot_ref, vec_ref, wo_ref, w1_ref, w2_ref,
    out_ref, df_ref, du_ref, dy1_ref, da_ref, dc_ref, grads_ref, sums_ref, ups_ref,
):
    s = pl.program_id(0)

    @pl.when(s == 0)
    def _():
        sums_ref[...] = jnp.zeros_like(sums_ref)
        ups_ref[...] = jnp.zeros_like(ups_ref)

    gain1 = vec_ref[G1 : G1 + 1, :]
    gain2 = vec_ref[G2 : G2 + 1, :]
    part = y1_ref.shape[0] // 2
    kept = [{}, {}]

    def down(h):
        rows = slice(h * part, (h + 1) * part)
        kept[h]["f"] = nn(g_ref[rows, :], w2_ref[...])

    def norm_two(h):
        rows = slice(h * part, (h + 1) * part)
        z1, r1 = norm_stats(y1_ref[rows, :])
        n1 = z1 * gain1 + vec_ref[C1 : C1 + 1, :]
        y2 = n1 + (kept[h]["f"] + vec_ref[B2 : B2 + 1, :])
        z2, r2 = norm_stats(y2)
        out_ref[rows, :] = (z2 * gain2 + vec_ref[C2 : C2 + 1, :]).astype(bf16)
        e = cot_ref[rows, :].astype(f32)
        sums_ref[0] += fold_rows(e * z2)
        sums_ref[1] += fold_rows(e)
        dy2 = norm_back(e * gain2, z2, r2)
        df = dy2.astype(bf16)
        df_ref[rows, :] = df
        sums_ref[2] += fold_rows(df.astype(f32))
        kept[h].update(dy2=dy2, df=df)

    def up_grad(h):
        rows = slice(h * part, (h + 1) * part)
        for f in range(4):
            cols = slice(f * CHUNK, (f + 1) * CHUNK)
            dg = nt(kept[h]["df"], w2_ref[cols, :])
            du = (dg * gp_ref[rows, cols].astype(f32)).astype(bf16)
            du_ref[rows, cols] = du
            ups_ref[:, cols] += fold_rows(du.astype(f32))

    def up_back(h):
        rows = slice(h * part, (h + 1) * part)
        dn1 = kept[h]["dy2"]
        for f in range(4):
            dn1 = dn1 + nt(du_ref[rows, f * CHUNK : (f + 1) * CHUNK], w1_ref[f])
        kept[h]["dn1"] = dn1

    def norm_one(h):
        rows = slice(h * part, (h + 1) * part)
        z1, r1 = norm_stats(y1_ref[rows, :])
        dn1 = kept[h]["dn1"]
        sums_ref[3] += fold_rows(dn1 * z1)
        sums_ref[4] += fold_rows(dn1)
        dy1 = norm_back(dn1 * gain1, z1, r1)
        dy1_ref[rows, :] = dy1
        da = dy1.astype(bf16)
        da_ref[rows, :] = da
        sums_ref[5] += fold_rows(da.astype(f32))
        dc_ref[rows, :] = nt(da, wo_ref[0]).astype(bf16)

    for stage in (down, norm_two, up_grad, up_back, norm_one):
        for h in range(2):
            stage(h)

    @pl.when(s == pl.num_programs(0) - 1)
    def _():
        grads_ref[...] = jnp.zeros_like(grads_ref)
        for i, row in enumerate((G2, C2, B2, G1, C1, BO)):
            grads_ref[row : row + 1, :] = jnp.sum(sums_ref[i], axis=0, keepdims=True)
        for f in range(4):
            cols = slice(f * CHUNK, (f + 1) * CHUNK)
            grads_ref[B1 + f : B1 + f + 1, :] = jnp.sum(ups_ref[:, cols], axis=0, keepdims=True)


def chunks_at(count, index):
    return pl.BlockSpec(
        (count, CHUNK, CHUNK), lambda s: (index, 0, 0), pipeline_mode=pl.Buffered(1)
    )


def middle(y1, g, gp, cot, table, wa, w2):
    tokens = y1.shape[0]
    tile = SEQ

    narrow = pl.BlockSpec((tile, D), lambda s: (s, 0))
    wide = pl.BlockSpec((tile, FF), lambda s: (s, 0))
    wide_out = pl.BlockSpec((tile, FF), lambda s: (s, 0))
    return pl.pallas_call(
        middle_kernel,
        grid=(tokens // tile,),
        in_specs=[
            narrow, wide, wide, narrow, constant((TABLE, CHUNK)),
            chunks_at(1, 3), chunks_at(4, 1), constant((FF, D)),
        ],
        out_specs=[
            narrow, narrow, wide_out, narrow, narrow, narrow,
            pl.BlockSpec((TABLE, CHUNK), lambda s: (0, 0)),
        ],
        out_shape=[
            jax.ShapeDtypeStruct((tokens, D), bf16),
            jax.ShapeDtypeStruct((tokens, D), bf16),
            jax.ShapeDtypeStruct((tokens, FF), bf16),
            jax.ShapeDtypeStruct((tokens, D), f32),
            jax.ShapeDtypeStruct((tokens, D), bf16),
            jax.ShapeDtypeStruct((tokens, D), bf16),
            jax.ShapeDtypeStruct((TABLE, CHUNK), f32),
        ],
        scratch_shapes=[pltpu.VMEM((6, 8, D), f32), pltpu.VMEM((8, FF), f32)],
        compiler_params=pltpu.CompilerParams(vmem_limit_bytes=VMEM),
        name="middle",
    )(y1, g, gp, cot, table, wa, wa, w2)


UP, PROJ, DOWN, QKV = 0, 4, 5, 9
OUTERS = 9


class Reduce:
    def __init__(self, nz, grads, made, local, bufs, fin, outs, sems):
        self.at = Place(nz)
        self.nz, self.grads, self.made, self.local = nz, grads, made, local
        self.bufs, self.fin, self.outs = bufs, fin, outs
        self.c_sem, self.l_sem, self.q_sem, self.z_sem, self.f_sem = sems

    TURNS = (-1, 0, 3, 5, 7, 8)

    def pump(self, s):
        for j in (5, 4, 3, 2, 1, 0):
            turn = s - 4 - self.TURNS[j]
            r = (2 * turn + 1) // 3
            due = (turn >= 0) & (turn % 3 != 2) & (r < QKV)
            pl.when(due)(partial(self.act, j, r))

        @pl.when(s >= 15)
        def _():
            for hg, turns in ((0, (15, 16, 19, 21, 23, 24)), (1, (17, 18, 21, 22, 23, 24))):
                for j in (5, 4, 3, 2, 1, 0):
                    pl.when(s == turns[j])(partial(self.act, j, QKV + hg))

    def source(self, r, lanes, fn):
        g2, g19 = self.grads
        if isinstance(r, int):
            fn(self.made.at[r - QKV, :, :, :, lanes])
            return
        pl.when(r >= DOWN)(lambda: fn(g2.at[:, :, r - DOWN, :, lanes]))
        pl.when(r < DOWN)(lambda: fn(g19.at[r, :, :, :, lanes]))

    def act(self, j, r):
        at, nz = self.at, self.nz
        r0, r1, r2, r3 = self.bufs
        fin, got = self.fin
        c, x, y, z = at.c, at.x, at.y, at.z
        half = [pl.ds(pl.multiple_of(i * HALF, HALF), HALF) for i in (c, 1 - c)]

        def c_copy(src):
            return remote(src, r0.at[r], self.c_sem.at[0, r], self.c_sem.at[1, r], at.other)

        def l_copy(src):
            return pltpu.make_async_copy(src, self.local.at[r % 2], self.l_sem.at[r % 2])

        def a_copy(i):
            q = (1 - c) * (2 * i + 1 - x) + c * (2 * (1 - y) + i)
            return remote(
                r0.at[r, q], r1.at[r, i],
                self.q_sem.at[0, r, i], self.q_sem.at[1, r, i], at.first,
            )

        keep = (1 - c) * y + c * x

        def b_copy():
            return remote(
                r1.at[r, 1 - keep], r2.at[r],
                self.q_sem.at[0, r, 2], self.q_sem.at[1, r, 2], at.second,
            )

        def z_copy(i):
            return remote(
                r2.at[r, (z + i) % nz], r3.at[r, i - 1],
                self.z_sem.at[0, r, i - 1], self.z_sem.at[1, r, i - 1], at.along_z(i),
            )

        def f_copy():
            return remote(fin.at[r], got.at[r], self.f_sem.at[0, r], self.f_sem.at[1, r], at.other)

        rows = fin.shape[1] // 2
        if j == 0:
            self.source(r, half[1], lambda src: c_copy(src).start())
            if not isinstance(r, int):
                self.source(r, half[0], lambda src: l_copy(src).start())
        elif j == 1:
            if isinstance(r, int):
                c_copy(self.made.at[r - QKV, :, :, :, half[1]]).wait()
                own = self.made.at[r - QKV]
                mine = jnp.where(c == 0, own[:, :, :, :HALF], own[:, :, :, HALF:])
            else:
                self.source(r, half[1], lambda src: c_copy(src).wait())
                self.source(r, half[0], lambda src: l_copy(src).wait())
                mine = self.local[r % 2]
            r0[r] = r0[r] + mine
            a_copy(0).start()
            a_copy(1).start()
        elif j == 2:
            for i in (0, 1):
                a_copy(i).wait()
                q = (1 - c) * (2 * i + x) + c * (2 * y + i)
                r1[r, i] = r1[r, i] + r0[r, q]
            b_copy().start()
        elif j == 3:
            b_copy().wait()
            r2[r] = r2[r] + r1[r, keep]
            for i in range(1, nz):
                z_copy(i).start()
        elif j == 4:
            total = r2[r, z].astype(f32)
            for i in range(1, nz):
                z_copy(i).wait()
                total = total + r3[r, i - 1].astype(f32)
            fin[r] = total
            f_copy().start()
        else:
            f_copy().wait()
            self.finish(r, rows)

    def finish(self, r, rows):
        c = self.at.c
        fin, got = self.fin
        out, out_down = self.outs
        even = c == 0

        def sides(own, other):
            return jnp.concatenate(
                [jnp.where(even, own, other), jnp.where(even, other, own)], axis=1
            )

        def down():
            @pl.when(c == (r - DOWN) // 2)
            def _():
                out_down[(r - DOWN) % 2] = sides(fin[r], got[r])

        def rest():
            own = jnp.where(even, fin[r, :rows, :], fin[r, rows:, :])
            other = jnp.where(even, got[r, :rows, :], got[r, rows:, :])
            out[r if not isinstance(r, int) else r - QKV + DOWN] = sides(own, other)

        if isinstance(r, int):
            rest()
        else:
            pl.when(r >= DOWN)(down)
            pl.when(r < DOWN)(rest)


def back_kernel(comm, nz, *refs):
    (
        x_hbm, row_ref, col_ref, wa_hbm, q_ref, k_ref, v_ref, dc_ref, lse_ref, dy1_ref, table_ref,
        g_hbm, df_hbm, n1_hbm, du_hbm, c_hbm, da_hbm,
        g2_hbm, g19_hbm, out, out_down, total_ref, dx_ref,
        x_ref, wqkv_ref, work, res, made, dk_sum, dv_sum, qv_sum, in_sem, res_sem,
    ) = refs[:33]
    s = pl.program_id(0)
    att = GROUPS * 4
    end = OUTERS + att
    if comm:
        local, r0, r1, r2, r3, fin, got, mine, came = refs[33:42]
        sems, v_sem = refs[42:47], refs[47]
        reduce = Reduce(
            nz, (g2_hbm, g19_hbm), made, local, (r0, r1, r2, r3), (fin, got), (out, out_down), sems
        )
        at = reduce.at

        pl.when(s == 0)(at.greet)
        pl.when(s == 3)(at.meet)

    def bring(src, dst, i):
        return pltpu.make_async_copy(src, dst, in_sem.at[i])

    def stream(i, fn):
        cols = pl.ds(pl.multiple_of(i % 4 * CHUNK, CHUNK), CHUNK)
        down = pl.ds(pl.multiple_of((i + 3) % 4 * CHUNK, CHUNK), CHUNK)
        slot = i % 2
        pl.when(i < PROJ)(lambda: fn(bring(du_hbm.at[:, cols], work.at[slot], slot)))
        pl.when(i == PROJ)(lambda: fn(bring(c_hbm, work.at[slot], slot)))
        pl.when(i >= DOWN)(lambda: fn(bring(g_hbm.at[:, down], work.at[slot], slot)))

    def store(i, fn):
        slot = i % 2
        pl.when(i >= DOWN)(
            lambda: fn(pltpu.make_async_copy(res.at[slot], g2_hbm.at[i - DOWN], res_sem.at[slot]))
        )
        pl.when(i < DOWN)(
            lambda: fn(pltpu.make_async_copy(res.at[slot], g19_hbm.at[i], res_sem.at[slot]))
        )

    whole_da = bring(da_hbm, work.at[2], 2)
    whole_n1, whole_df = bring(n1_hbm, work.at[3], 3), bring(df_hbm, work.at[3], 3)
    whole_x = bring(x_hbm, x_ref, 4)
    whole_w = bring(wa_hbm.at[0:GROUPS], wqkv_ref, 5)

    @pl.when(s == 0)
    def _():
        stream(s, lambda copy: copy.start())
        whole_n1.start()
        stream(s + 1, lambda copy: copy.start())
        whole_da.start()
        whole_n1.wait()
        qv_sum[...] = jnp.zeros_like(qv_sum)

    pl.when((s >= 2) & (s < OUTERS + 2))(lambda: store(s - 2, lambda copy: copy.wait()))
    if comm:
        reduce.pump(s)

    @pl.when(s < OUTERS)
    def _():
        stream(s, lambda copy: copy.wait())
        pl.when(s == PROJ)(lambda: whole_da.wait())
        pl.when(s == DOWN)(lambda: whole_df.wait())
        def put(product):
            res[s % 2] = product.astype(bf16).reshape(res.shape[1:])

        @pl.when(s < PROJ)
        def _():
            put(tn(work[3], work[s % 2]))

        @pl.when(s == PROJ)
        def _():
            put(tn(work[s % 2], work[2]))

        @pl.when(s >= DOWN)
        def _():
            put(tn(work[s % 2], work[3]))

        store(s, lambda copy: copy.start())
        pl.when(s < OUTERS - 2)(lambda: stream(s + 2, lambda copy: copy.start()))
        pl.when(s == PROJ - 1)(lambda: whole_df.start())

        @pl.when(s == 2)
        def _():
            whole_x.start()
            whole_w.start()

        @pl.when(s == OUTERS - 1)
        def _():
            whole_x.wait()
            whole_w.wait()

    @pl.when((s >= OUTERS) & (s < end))
    def _():
        hg = (s - OUTERS) // 4
        r = (s - OUTERS) % 4
        rows = pl.multiple_of(r * SEQ, SEQ)
        lanes = pl.ds(pl.multiple_of(hg * WIDE, WIDE), WIDE)
        kt = k_ref[...].T
        dk_sum[...] = jnp.zeros_like(dk_sum)
        dv_sum[...] = jnp.zeros_like(dv_sum)
        masks = head_masks()
        places = list(windows())

        def begin(b, first, width):
            block, span = slice(b * BAND, (b + 1) * BAND), slice(first, first + width)
            qc = spread_heads(q_ref[block, :], masks)
            dcc = spread_heads(dc_ref[block, :], masks)
            return qc, dcc, nt(k_ref[span, :], qc), nt(v_ref[span, :], dcc)

        ahead = begin(*places[0])
        for b, first, width in places:
            span = slice(first, first + width)
            qc, dcc, t, dp = ahead
            if b + 1 < len(places):
                ahead = begin(*places[b + 1])
            t = t * SCORE + mask_bias(col_ref.at[0], row_ref.at[0], b, first, width)
            p = jnp.exp2(t - lse_ref[0, b : b + 1, :])
            pdp = p * dp
            weighted = jnp.sum(pdp, axis=0, keepdims=True)
            ds = (pdp - p * weighted).astype(bf16)
            dv_sum[span, :] += nn(p.astype(bf16), dcc)
            dk_sum[span, :] += nn(ds, qc)
            dqt = nn(kt[:, span], ds)
            dq = (pick_heads(dqt).T * HEAD_DIM ** (-0.5)).astype(bf16)
            work[hg, pl.ds(rows + b * BAND, BAND), 0:WIDE] = dq
            qv_sum[0, :, lanes] += fold_rows(dq.astype(f32))
        dk = (dk_sum[...] * HEAD_DIM ** (-0.5)).astype(bf16)
        dv = dv_sum[...].astype(bf16)
        work[hg, pl.ds(rows, SEQ), WIDE : 2 * WIDE] = dk
        work[hg, pl.ds(rows, SEQ), 2 * WIDE :] = dv
        qv_sum[1, :, lanes] += fold_rows(dv.astype(f32))

        @pl.when(r == 3)
        def _():
            made[hg] = tn(x_ref[...], work[hg]).astype(bf16).reshape(made.shape[1:])

    last = QKV + GROUPS - 1
    if comm:
        def vec_copy(i, src, device):
            return remote(src, came.at[i], v_sem.at[0, i], v_sem.at[1, i], device)

        c_copy = vec_copy(0, mine.at[0], at.other)
        z_copies = [vec_copy(i, mine.at[1], at.along_z(i)) for i in range(1, nz)]
        near = [
            vec_copy(nz + i, mine.at[2], device)
            for i, device in enumerate((at.first, at.second, at.far))
        ]

        @pl.when(s == end - 1)
        def _():
            reduce.act(0, last)
            mine[0] = table_ref[...]
            mine[0, BQ : BQ + 1, :] = jnp.sum(qv_sum[0], axis=0, keepdims=True)
            mine[0, BV : BV + 1, :] = jnp.sum(qv_sum[1], axis=0, keepdims=True)
            c_copy.start()

        @pl.when(s == end)
        def _():
            reduce.act(1, last)
            c_copy.wait()
            mine[1] = mine[0] + came[0]
            for copy in z_copies:
                copy.start()

        @pl.when(s == end + 1)
        def _():
            reduce.act(3, last)
            total = mine[1]
            for i in range(1, nz):
                z_copies[i - 1].wait()
                total = total + came[i]
            mine[2] = total
            for copy in near:
                copy.start()

    @pl.when(s >= end)
    def _():
        half = SEQ // 2
        for h in range(2):
            if h == 1 and comm:
                pl.when(s == end)(lambda: reduce.act(2, last))
                pl.when(s == end + 1)(lambda: reduce.act(4, last))
            rows = pl.ds(pl.multiple_of((s - end) * SEQ + h * half, half), half)
            total = dy1_ref[h * half : (h + 1) * half, :]
            for hg in range(GROUPS):
                total = total + nt(work[hg, rows, :], wqkv_ref[hg].reshape(CHUNK, CHUNK))
            dx_ref[h * half : (h + 1) * half, :] = total

    @pl.when(s == end + 3)
    def _():
        if comm:
            for copy in near:
                copy.wait()
            total_ref[...] = mine[2] + came[nz] + came[nz + 1] + came[nz + 2]
            reduce.act(5, last)
        else:
            total_ref[...] = table_ref[...]
            total_ref[BQ : BQ + 1, :] = jnp.sum(qv_sum[0], axis=0, keepdims=True)
            total_ref[BV : BV + 1, :] = jnp.sum(qv_sum[1], axis=0, keepdims=True)
            out[...] = jnp.zeros_like(out)
            out_down[...] = jnp.zeros_like(out_down)


def back(x, row_codes, col_codes, wa, q, k, v, dc, lse, dy1, table, pairs, chips, comm):
    tokens = x.shape[0]
    rows = tokens // SEQ
    att = GROUPS * rows
    end = OUTERS + att
    assert rows == 4
    nz = chips // 4
    step = CHUNK // chips

    def turn(s):
        return jnp.clip(s - OUTERS, 0, att - 1)

    def code_at(s):
        return (turn(s) % rows, 0, 0)

    def head_at(s):
        return (turn(s) % rows, turn(s) // rows)

    def tile_at(s):
        return (jnp.maximum(s - end, 0), 0)

    anywhere = pl.BlockSpec(memory_space=pl.ANY)
    whole_table = pl.BlockSpec((TABLE, CHUNK), lambda s: (0, 0))
    head = pl.BlockSpec((SEQ, WIDE), head_at)
    tile = pl.BlockSpec((SEQ, D), tile_at)
    made_shape = (GROUPS, 4, nz, step, CHUNK)
    dma = pltpu.SemaphoreType.DMA
    scratch = [
        pltpu.VMEM((tokens, D), bf16),
        pltpu.VMEM((GROUPS, *wa.shape[1:]), bf16),
        pltpu.VMEM((4, tokens, CHUNK), bf16),
        pltpu.VMEM((2, 4, nz, step, CHUNK), bf16),
    ]
    if comm:
        scratch.append(pltpu.VMEM(made_shape, bf16))
    scratch += [
        pltpu.VMEM((SEQ, WIDE), f32),
        pltpu.VMEM((SEQ, WIDE), f32),
        pltpu.VMEM((2, 8, D), f32),
        dma((6,)), dma((2,)),
    ]
    out_specs = [
        anywhere, anywhere,
        pl.BlockSpec((8, step // 2, CHUNK), lambda s: (0, 0, 0)),
        pl.BlockSpec((2, step, CHUNK), lambda s: (0, 0, 0)),
        whole_table, tile,
    ]
    out_shape = [
        jax.ShapeDtypeStruct((4, nz, 4, step, CHUNK), bf16),
        jax.ShapeDtypeStruct((5, 4, nz, step, CHUNK), bf16),
        jax.ShapeDtypeStruct((8, step // 2, CHUNK), f32),
        jax.ShapeDtypeStruct((2, step, CHUNK), f32),
        jax.ShapeDtypeStruct((TABLE, CHUNK), f32),
        jax.ShapeDtypeStruct((tokens, D), f32),
    ]
    kernel = partial(back_kernel, comm, nz)
    if comm:
        scratch += [
            pltpu.VMEM((2, 4, nz, step, HALF), bf16),
            pltpu.VMEM((CHUNKS, 4, nz, step, HALF), bf16),
            pltpu.VMEM((CHUNKS, 2, nz, step, HALF), bf16),
            pltpu.VMEM((CHUNKS, nz, step, HALF), bf16),
            pltpu.VMEM((CHUNKS, nz - 1, step, HALF), bf16),
            pltpu.VMEM((CHUNKS, step, HALF), f32),
            pltpu.VMEM((CHUNKS, step, HALF), f32),
            pltpu.VMEM((3, TABLE, CHUNK), f32),
            pltpu.VMEM((nz + 3, TABLE, CHUNK), f32),
            dma((2, CHUNKS)), dma((2,)), dma((2, CHUNKS, 3)), dma((2, CHUNKS, nz - 1)),
            dma((2, CHUNKS)), dma((2, nz + 3)),
        ]
        params = pltpu.CompilerParams(
            vmem_limit_bytes=VMEM, collective_id=1, has_side_effects=True
        )
    else:
        def kernel(*refs):
            refs = list(refs)
            made = refs.pop(23)
            refs.insert(27, made)
            back_kernel(comm, nz, *refs)

        out_specs.append(pl.BlockSpec(made_shape, lambda s: (0,) * 5, pipeline_mode=pl.Buffered(1)))
        out_shape.append(jax.ShapeDtypeStruct(made_shape, bf16))
        params = pltpu.CompilerParams(vmem_limit_bytes=VMEM)
    return pl.pallas_call(
        kernel,
        grid=(end + rows,),
        in_specs=[
            anywhere,
            pl.BlockSpec((1, 8, SEQ), code_at),
            pl.BlockSpec((1, SEQ, BAND), code_at),
            anywhere,
            head, head, head, head,
            pl.BlockSpec((1, 8, PACK * BAND), lambda s: (turn(s), 0, 0)),
            tile, whole_table,
            *(anywhere for _ in pairs),
        ],
        out_specs=out_specs,
        out_shape=out_shape,
        scratch_shapes=scratch,
        compiler_params=params,
        name="back",
    )(x, row_codes, col_codes, wa, q, k, v, dc, lse, dy1, table, *pairs)


def update(grad, master, moment, average, tokens_all):
    mean_grad = grad / tokens_all
    moment_new = momentum_coef * moment + mean_grad
    step_size = -learn_rate * (mean_grad + momentum_coef * moment_new)
    master_new = master + step_size
    average_new = average_keep * average + (1.0 - average_keep) * master_new
    return (master_new, moment_new, average_new)


def update_steps(grad, master, moment, average, tokens_all):
    mean_grad = grad / tokens_all
    moment_new = momentum_coef * moment + mean_grad
    step_size = -learn_rate * (mean_grad + momentum_coef * moment_new)
    average_step = (1.0 - average_keep) * (master + step_size - average)
    return (step_size, moment_new, average_step)


def update_kernel(tokens_all, *refs):
    grad_ref, down_ref, dx_ref = refs[:3]
    states, outs, dx_out, kept, sem = refs[3:15], refs[15:31], *refs[31:34]
    parts = kept.shape[0]
    spans = [pl.ds(i * kept.shape[1], kept.shape[1]) for i in range(parts)]
    loads = [
        pltpu.make_async_copy(dx_ref.at[span], kept.at[i], sem.at[0, i])
        for i, span in enumerate(spans)
    ]
    saves = [
        pltpu.make_async_copy(kept.at[i], dx_out.at[span], sem.at[1, i])
        for i, span in enumerate(spans)
    ]
    for load in loads:
        load.start()

    def one(i, index, grad):
        master, moment, average = (states[i + 4 * j][index] for j in range(3))
        outs[i][index] = grad
        new = update(grad, master, moment, average, tokens_all)
        for j in range(3):
            outs[i + 4 * (j + 1)][index] = new[j]

    rows = grad_ref.shape[1]
    for i in range(parts):
        loads[i].wait()
        saves[i].start()
    for hg in range(GROUPS):
        for i in range(3):
            cols = slice(i * D + hg * WIDE, i * D + (hg + 1) * WIDE)
            one(0, (slice(None), cols), grad_ref[5 + hg, :, i * WIDE : (i + 1) * WIDE])
    one(1, (slice(None), slice(None)), grad_ref[4])
    for f in range(4):
        one(2, (slice(None), slice(f * CHUNK, (f + 1) * CHUNK)), grad_ref[f])
    for i in range(2):
        one(3, (slice(2 * rows * i, 2 * rows * (i + 1)), slice(None)), down_ref[i])
    for save in saves:
        save.wait()


def update_weights(grads, grads_down, dx, states, tokens_all):
    whole = pl.BlockSpec(memory_space=pltpu.VMEM)
    anywhere = pl.BlockSpec(memory_space=pl.ANY)
    shapes = [jax.ShapeDtypeStruct(w.shape, f32) for w in states[:4]]
    return pl.pallas_call(
        partial(update_kernel, tokens_all),
        in_specs=[whole] * 2 + [anywhere] + [whole] * 12,
        out_specs=[whole] * 16 + [anywhere],
        out_shape=shapes * 4 + [jax.ShapeDtypeStruct(dx.shape, f32)],
        scratch_shapes=[
            pltpu.VMEM((8, dx.shape[0] // 8, D), f32), pltpu.SemaphoreType.DMA((2, 8)),
        ],
        compiler_params=pltpu.CompilerParams(vmem_limit_bytes=VMEM),
        name="update",
    )(grads, grads_down, dx, *states)


def group_columns(w):
    n = w.shape[0]
    return w.reshape(n, 3, GROUPS, WIDE).transpose(2, 0, 1, 3).reshape(GROUPS, n, 3 * WIDE)


def ungroup_columns(w):
    n = w.shape[1]
    return w.reshape(GROUPS, n, 3, WIDE).transpose(1, 2, 0, 3).reshape(n, 3 * D)


def table_of(gains, biases):
    flat = jnp.concatenate([gains, biases, jnp.zeros((TABLE * CHUNK - 9216,), gains.dtype)])
    return flat.reshape(TABLE, CHUNK)


def on_device(
    tokens, segment_ids, pad_counts, out_cotangent,
    qkv_master, proj_master, up_master, down_master, gain_master, bias_master,
    qkv_moment, proj_moment, up_moment, down_moment, gain_moment, bias_moment,
    qkv_average, proj_average, up_average, down_average, gain_average, bias_average,
):
    axes = ("gx", "gy")
    devices = lax.axis_size(axes)
    seq_len = segment_ids.shape[1]
    tokens_all = tokens.shape[0] * devices
    position = jnp.arange(seq_len, dtype=jnp.int32)
    is_pad = position[None, :] >= (seq_len - pad_counts)[:, None]
    codes = segment_ids * 2 + is_pad.astype(jnp.int32)
    row_codes = jnp.broadcast_to(codes[:, None, :], (codes.shape[0], 8, seq_len))
    col_codes = jnp.broadcast_to(codes[:, :, None], (codes.shape[0], seq_len, BAND))
    gain_len, bias_len = gain_master.shape[0], bias_master.shape[0]
    gains = gain_len * devices
    place = lax.axis_index(axes)

    fine = lax.axis_size("gx") == 4 and lax.axis_size("gy") == 8
    if fine:
        chips = devices // 2
        part = jnp.zeros((TABLE * CHUNK,), bf16)
        part = lax.dynamic_update_slice(part, gain_master.astype(bf16), (place * gain_len,))
        part = lax.dynamic_update_slice(
            part, bias_master.astype(bf16), (gains + place * bias_len,)
        ).reshape(TABLE, CHUNK)
        q, k, v, lse, c, y1, n1, g, gp, wa, w2, table = front(
            tokens, row_codes, col_codes, part,
            (qkv_master, proj_master, up_master, down_master), chips,
        )
        w2 = w2.reshape(FF, D)
    else:
        gather = partial(lax.all_gather, axis_name=axes, axis=0, tiled=True)
        w1 = gather(up_master.astype(bf16))
        wa = jnp.concatenate(
            [
                group_columns(gather(qkv_master.astype(bf16))),
                gather(proj_master.astype(bf16))[None],
                w1.reshape(D, 4, CHUNK).transpose(1, 0, 2),
            ]
        ).reshape(8, 16, CHUNK // 16, CHUNK)
        w2 = gather(down_master.astype(bf16))
        table = table_of(
            gather(gain_master.astype(bf16)), gather(bias_master.astype(bf16))
        ).astype(f32)
        q, k, v, lse, c, y1, n1, g, gp = front(
            tokens, row_codes, col_codes, table, (wa,)
        )
    layer_output, df, du, dy1, da, dc, terms = middle(
        y1, g, gp, out_cotangent, table, wa.reshape(8, CHUNK, CHUNK), w2
    )
    results = back(
        tokens, row_codes, col_codes, wa, q, k, v, dc, lse, dy1, terms,
        (g, df, n1, du, c, da), chips if fine else 16, fine,
    )
    input_grad = results[5]
    scatter = partial(lax.psum_scatter, axis_name=axes, scatter_dimension=0, tiled=True)
    states = (
        qkv_master, proj_master, up_master, down_master,
        qkv_moment, proj_moment, up_moment, down_moment,
        qkv_average, proj_average, up_average, down_average,
    )
    if fine:
        grads, grads_down, terms = results[2:5]
        new = update_weights(grads, grads_down, input_grad, states, tokens_all)
        shares, masters, moments, averages = new[:4], new[4:8], new[8:12], new[12:16]
        input_grad = new[16]
        terms = terms.reshape(-1)
        gain_share = lax.dynamic_slice(terms, (place * gain_len,), (gain_len,))
        bias_share = lax.dynamic_slice(terms, (gains + place * bias_len,), (bias_len,))
    else:
        down_part, rest, terms, dwqkv = (results[i].astype(f32) for i in (0, 1, 4, 6))
        rest = rest.reshape(5, CHUNK, CHUNK)
        terms = terms.reshape(-1)
        shares = (
            scatter(ungroup_columns(dwqkv.reshape(GROUPS, CHUNK, CHUNK))),
            scatter(rest[4]),
            scatter(rest[:4].transpose(1, 0, 2).reshape(D, FF)),
            scatter(down_part.reshape(FF, D)),
        )
        news = [
            update(shares[i], states[i], states[4 + i], states[8 + i], tokens_all)
            for i in range(4)
        ]
        masters, moments, averages = zip(*news)
        gain_share = scatter(terms[:gains])
        bias_share = scatter(terms[gains : gains + bias_len * devices])
    gain_new = update_steps(gain_share, gain_master, gain_moment, gain_average, tokens_all)
    bias_new = update(bias_share, bias_master, bias_moment, bias_average, tokens_all)
    return (
        layer_output, input_grad, *shares, gain_share, bias_share,
        *masters, gain_new[0], bias_new[0],
        *moments, gain_new[1], bias_new[1],
        *averages, gain_new[2], bias_new[2],
    )


def solution(mesh):
    both = ("gx", "gy")
    two, one = P(both, None), P(both)
    weights = (two, two, two, two, one, one)
    in_specs = (two, two, one, two) + weights * 3
    out_specs = (two, two) + weights * 4
    return jax.shard_map(
        on_device, mesh=mesh, in_specs=in_specs, out_specs=out_specs, check_vma=False
    )
```

```python
from functools import partial

import jax
import jax.numpy as jnp
from jax import lax
from jax.experimental import pallas as pl
from jax.experimental.pallas import tpu as pltpu
from jax.sharding import PartitionSpec as P

D = 768
HEADS = 12
HEAD_DIM = 64
FF = 3072
SEQ = 512
BAND = 128
PACK = 4
GROUPS = HEADS // PACK
WIDE = PACK * HEAD_DIM
VMEM = 60 * 1024 * 1024

norm_eps = 1e-06
momentum_coef = 0.9
learn_rate = 4.0
average_keep = 0.9

G1, G2, BQ, BV, BO, C1, B1, B2, C2 = (0, 1, 2, 3, 4, 5, 6, 10, 11)
TABLE = 16
CHUNK = 768
CHUNKS = 12
HALF = CHUNK // 2
MESH = pl.DeviceIdType.MESH

f32 = jnp.float32
bf16 = jnp.bfloat16

LOG2E = 1.4426950408889634
SCORE = HEAD_DIM ** (-0.5) * LOG2E


def nn(a, b):
    return lax.dot_general(a, b, (((1,), (0,)), ((), ())), preferred_element_type=f32)


def nt(a, b):
    return lax.dot_general(a, b, (((1,), (1,)), ((), ())), preferred_element_type=f32)


def tn(a, b):
    return lax.dot_general(a, b, (((0,), (0,)), ((), ())), preferred_element_type=f32)


def normal_cdf(u):
    gauss = jnp.exp2(u * u * (-0.5 * LOG2E))
    return 0.5 + 0.5 * lax.erf(u * 0.7071067811865476), gauss


def windows():
    for b in range(SEQ // BAND):
        first = max(0, (b - 1) * BAND)
        last = min(SEQ, (b + 2) * BAND)
        yield b, first, last - first


def head_masks():
    lane = lax.broadcasted_iota(jnp.int32, (BAND, WIDE), 1) // HEAD_DIM
    return [jnp.where(lane == h, 1.0, 0.0).astype(bf16) for h in range(PACK)]


def spread_heads(block, masks):
    return jnp.concatenate([block * m for m in masks], axis=0)


def pick_heads(wide):
    return jnp.concatenate(
        [
            wide[h * HEAD_DIM : (h + 1) * HEAD_DIM, h * BAND : (h + 1) * BAND]
            for h in range(PACK)
        ],
        axis=0,
    )


def mask_bias(col, row, b, first, width):
    keys = col[first : first + width, :]
    queries = row[0:1, b * BAND : (b + 1) * BAND]
    bias = jnp.where(keys == queries, 0.0, -1e30)
    return jnp.concatenate([bias] * PACK, axis=1)


def norm_stats(y):
    centre = jnp.mean(y, axis=-1, keepdims=True)
    centred = y - centre
    spread = jnp.mean(centred * centred, axis=-1, keepdims=True)
    r = lax.rsqrt(spread + norm_eps)
    return centred * r, r


def norm_back(dz, z, r):
    return r * (
        dz
        - jnp.mean(dz, axis=-1, keepdims=True)
        - z * jnp.mean(dz * z, axis=-1, keepdims=True)
    )


def remote(src, dst, send, recv, device):
    return pltpu.make_async_remote_copy(
        src_ref=src, dst_ref=dst, send_sem=send, recv_sem=recv, device_id=device,
        device_id_type=MESH,
    )


class Place:
    def __init__(self, nz):
        gx = lax.axis_index("gx")
        gy = lax.axis_index("gy")
        self.nz = nz
        self.x, self.y = gx % 2, gx // 2
        self.z, self.c = gy // 2, gy % 2
        x, y, z, c = self.x, self.y, self.z, self.c
        self.other = (gx, z * 2 + 1 - c)
        ax, ay = x + (1 - c) * (1 - 2 * x), y + c * (1 - 2 * y)
        bx, by = x + c * (1 - 2 * x), y + (1 - c) * (1 - 2 * y)
        self.first = (ay * 2 + ax, gy)
        self.second = (by * 2 + bx, gy)
        self.far = ((1 - y) * 2 + 1 - x, gy)
        self.quarter = gx
        self.quarter_first = ay * 2 + ax
        self.quarter_second = by * 2 + bx
        self.quarter_far = (1 - y) * 2 + 1 - x

    def along_z(self, j):
        return (self.quarter, (self.z + j) % self.nz * 2 + self.c)

    def greet(self):
        sem = pltpu.get_barrier_semaphore()
        partners = [self.other, self.first, self.second, self.far]
        partners += [self.along_z(j) for j in range(1, self.nz)]
        for p in partners:
            pl.semaphore_signal(sem, inc=1, device_id=p, device_id_type=MESH)

    def meet(self):
        pl.semaphore_wait(pltpu.get_barrier_semaphore(), 4 + self.nz - 1)


def fold_rows(v):
    n = v.shape[0]
    return jnp.sum(v.reshape(n // 8, 8, v.shape[1]), axis=0)


class Gather:
    TURNS = (-3, 0, 2, 4, 5, 6)

    def __init__(self, nz, wa, wb, held, stage, z_sem, s_sem, own_sem, out_sem):
        self.at = Place(nz)
        self.nz, self.wa, self.wb, self.held, self.stage = nz, wa, wb, held, stage
        self.z_sem, self.s_sem, self.own_sem, self.out_sem = z_sem, s_sem, own_sem, out_sem

    def pump(self, s):
        for j in (5, 4, 3, 2, 1, 0):
            turn = s + 3 - self.TURNS[j]
            k = (2 * turn + 1) // 3
            due = (turn % 3 != 2) & (k >= (4, 2, 2, 2, 2, 2)[j]) & (k < CHUNKS - 2)
            pl.when(due)(partial(self.act, j, k))

        @pl.when(s <= 5)
        def _():
            for j, turn in ((2, 1), (3, 3), (4, 4), (5, 5)):
                pl.when(s == turn)(partial(self.act, j, 1))

        @pl.when(s >= 9)
        def _():
            for k in (CHUNKS - 2, CHUNKS - 1):
                for j in range(6):
                    turn = k + (-1, 2, 3, 4, 5, 6)[j]
                    pl.when(s == turn)(partial(self.act, j, k))

    def rest(self):
        self.act(5, CHUNKS - 3)
        self.act(5, CHUNKS - 2)
        self.act(4, CHUNKS - 1)
        self.act(5, CHUNKS - 1)

    def act(self, j, k):
        at, nz = self.at, self.nz
        direct = isinstance(k, int) and k == 0
        mine = pl.ds(pl.multiple_of(at.c * HALF, HALF), HALF)
        others = pl.ds(pl.multiple_of((1 - at.c) * HALF, HALF), HALF)

        def spot(chip, lanes=mine):
            return self.held.at[k, chip, :, lanes]

        def quarter(q):
            return spot(pl.ds(q * nz, nz))

        def z_copy(i, chip):
            return remote(
                self.stage.at[k], spot(chip), self.z_sem.at[0, k, i - 1],
                self.z_sem.at[1, k, i - 1], at.along_z(i),
            )

        def s_copy(i, q, device):
            return remote(
                quarter(q), quarter(q), self.s_sem.at[0, k, i], self.s_sem.at[1, k, i], device
            )

        def far_copy(q):
            if direct:
                return s_copy(2, at.quarter if q is None else q, at.far)
            return s_copy(2, at.quarter_first if q is None else q, at.second)

        def c_copy(lanes):
            whole = spot(slice(None), lanes)
            return remote(
                whole, whole, self.s_sem.at[0, k, 3], self.s_sem.at[1, k, 3], at.other
            )

        def own():
            return pltpu.make_async_copy(self.stage.at[k], spot(chip), self.own_sem.at[k])

        chip = at.quarter * nz + at.z
        if j == 0:
            for i in range(1, nz):
                z_copy(i, chip).start()
            own().start()
        elif j == 1:
            for i in range(1, nz):
                z_copy(i, at.quarter * nz + (at.z - i + nz) % nz).wait_recv()
            own().wait()
            s_copy(0, at.quarter, at.first).start()
            s_copy(1, at.quarter, at.second).start()
            if direct:
                far_copy(None).start()
        elif j == 2:
            s_copy(0, at.quarter_first, at.first).wait_recv()
            if not direct:
                far_copy(None).start()
        elif j == 3:
            s_copy(1, at.quarter_second, at.second).wait_recv()
            far_copy(at.quarter_far).wait_recv()
            c_copy(mine).start()
        elif j == 4:
            c_copy(others).wait_recv()
            for i in range(1, nz):
                z_copy(i, chip).wait_send()
            s_copy(0, at.quarter, at.first).wait_send()
            s_copy(1, at.quarter, at.second).wait_send()
            far_copy(None).wait_send()
            c_copy(mine).wait_send()
            self.keep(k, lambda copy: copy.start())
        else:
            self.keep(k, lambda copy: copy.wait())

    def keep(self, k, fn):
        def early():
            fn(pltpu.make_async_copy(self.held.at[k], self.wa.at[k], self.out_sem.at[k]))

        def late():
            fn(pltpu.make_async_copy(self.held.at[k], self.wb.at[:, k - 8], self.out_sem.at[k]))

        if isinstance(k, int) and k < 8:
            early()
        elif isinstance(k, int):
            late()
        else:
            pl.when(k < 8)(early)
            pl.when(k >= 8)(late)


def share_start(nz, part_ref, masters, sibs, stage, table_ref, sums, got, x_sem, v_sem, gather):
    at = gather.at
    at.greet()
    at.meet()
    swaps = [
        remote(m, o, x_sem.at[0, i], x_sem.at[1, i], at.other)
        for i, (m, o) in enumerate(zip(masters, sibs))
    ]
    swaps.insert(1, remote(part_ref, got.at[0], x_sem.at[0, 4], x_sem.at[1, 4], at.other))
    for swap in swaps:
        swap.start()
    mq, mo, m1, m2 = masters
    sq, so, s1, s2 = sibs
    even = at.c == 0

    def halves(own, sib):
        own = jnp.where(even, own[:, :HALF], own[:, HALF:])
        sib = jnp.where(even, sib[:, :HALF], sib[:, HALF:])
        top, low = jnp.where(even, own, sib), jnp.where(even, sib, own)
        return jnp.concatenate([top, low], axis=0).astype(bf16)

    def group(ref, hg):
        cols = [ref[:, i * D + hg * WIDE : i * D + (hg + 1) * WIDE] for i in range(3)]
        return jnp.concatenate(cols, axis=1)

    def vec_copy(i, src, device):
        return remote(src, got.at[i], v_sem.at[0, i], v_sem.at[1, i], device)

    swaps[0].wait()
    for hg in range(GROUPS):
        stage[hg] = halves(group(mq, hg), group(sq, hg))
        if hg == 0:
            gather.act(0, hg)
    swaps[1].wait()
    sums[0] = part_ref[...] + got[0]
    z_copies = [vec_copy(i, sums.at[0], at.along_z(i)) for i in range(1, nz)]
    for copy in z_copies:
        copy.start()
    for swap in swaps[2:]:
        swap.wait()
    stage[3] = halves(mo[...], so[...])
    for f in range(4):
        cols = slice(f * CHUNK, (f + 1) * CHUNK)
        stage[4 + f] = halves(m1[:, cols], s1[:, cols])
    step = stage.shape[1]
    for i in range(4):
        rows = slice(i % 2 * step, (i % 2 + 1) * step)
        block = jnp.where(at.c == i // 2, m2[rows, :], s2[rows, :])
        stage[8 + i] = jnp.where(even, block[:, :HALF], block[:, HALF:]).astype(bf16)
    for copy in z_copies:
        copy.wait()
    total = sums[0]
    for i in range(1, nz):
        total = total + got[i]
    sums[1] = total
    near = [
        vec_copy(nz + i, sums.at[1], device)
        for i, device in enumerate((at.first, at.second, at.far))
    ]
    gather.act(1, 0)
    for copy in near:
        copy.start()
    gather.act(0, 1)
    gather.act(0, 2)
    gather.act(0, 3)
    gather.act(2, 0)
    gather.act(3, 0)
    for copy in near:
        copy.wait()
    table_ref[...] = (sums[1] + got[nz] + got[nz + 1] + got[nz + 2]).astype(f32)
    gather.act(1, 1)
    gather.act(4, 0)


def front_kernel(nz, *refs):
    refs = list(refs)
    x_ref, row_ref, col_ref, vec_ref = refs[:4]
    s = pl.program_id(0)
    att = GROUPS * 4
    if nz:
        masters, refs = refs[4:8], refs[8:]
    else:
        wa_ref, refs = refs[4], refs[5:]
    q_ref, k_ref, v_ref, lse_ref, c_ref, y1_ref, n1_ref, g_ref, gp_ref = refs[:9]
    refs = refs[9:]
    if nz:
        wa_ref, wb_ref, table_ref = refs[:3]
        c_all, held, stage, sq, so, s1, s2, sums, got = refs[3:12]
        z_sem, s_sem, own_sem, out_sem, x_sem, v_sem = refs[12:]
        gather = Gather(nz, wa_ref, wb_ref, held, stage, z_sem, s_sem, own_sem, out_sem)

        @pl.when(s == 0)
        def _():
            share_start(
                nz, vec_ref, masters, (sq, so, s1, s2), stage, table_ref, sums, got,
                x_sem, v_sem, gather,
            )

        pl.when(s == 2)(partial(gather.act, 5, 0))
        gather.pump(s)
    else:
        c_all, held, load_sem = refs
        table_ref = vec_ref

        @pl.when(s == 0)
        def _():
            copy = pltpu.make_async_copy(wa_ref, held, load_sem)
            copy.start()
            copy.wait()

    def weight(k):
        return held[k].reshape(CHUNK, CHUNK)

    @pl.when(s < att)
    def _():
        hg = s // 4
        r = s % 4
        rows = pl.multiple_of(r * SEQ, SEQ)
        lanes = pl.multiple_of(hg * WIDE, WIDE)
        xr = x_ref[pl.ds(rows, SEQ), :]
        wqkv = weight(hg)
        q = nn(xr, wqkv[:, 0:WIDE]) + table_ref[BQ : BQ + 1, pl.ds(lanes, WIDE)]
        q = q.astype(bf16)
        k = nn(xr, wqkv[:, WIDE : 2 * WIDE]).astype(bf16)
        v = nn(xr, wqkv[:, 2 * WIDE :]) + table_ref[BV : BV + 1, pl.ds(lanes, WIDE)]
        v = v.astype(bf16)
        q_ref[...] = q
        k_ref[...] = k
        v_ref[...] = v
        vt = v.T
        masks = head_masks()
        places = list(windows())

        def begin(b, first, width):
            qc = spread_heads(q[b * BAND : (b + 1) * BAND, :], masks)
            return nt(k[first : first + width, :], qc)

        ahead = begin(*places[0])
        for b, first, width in places:
            t = ahead
            if b + 1 < len(places):
                ahead = begin(*places[b + 1])
            t = t * SCORE + mask_bias(col_ref.at[0], row_ref.at[0], b, first, width)
            m = jnp.max(t, axis=0, keepdims=True)
            e = jnp.exp2(t - m)
            l = jnp.sum(e, axis=0, keepdims=True)
            p = (e * (1.0 / l)).astype(bf16)
            lse_ref[0, b : b + 1, :] = m + jnp.log2(l)
            ot = nn(vt[:, first : first + width], p)
            c = pick_heads(ot).T.astype(bf16)
            c_all[pl.ds(rows + b * BAND, BAND), pl.ds(lanes, WIDE)] = c

    @pl.when(s >= att)
    def _():
        r = s - att
        rows = pl.multiple_of(r * SEQ, SEQ)
        c = c_all[pl.ds(rows, SEQ), :]
        c_ref[...] = c
        y1 = x_ref[pl.ds(rows, SEQ), :].astype(f32) + (
            nn(c, weight(3)) + table_ref[BO : BO + 1, :]
        )
        y1_ref[...] = y1
        z1, _ = norm_stats(y1)
        n1 = (z1 * table_ref[G1 : G1 + 1, :] + table_ref[C1 : C1 + 1, :]).astype(bf16)
        n1_ref[...] = n1
        for f in range(4):
            cols = slice(f * CHUNK, (f + 1) * CHUNK)
            u = nn(n1, weight(4 + f)) + table_ref[B1 + f : B1 + f + 1, :]
            cdf, gauss = normal_cdf(u)
            g_ref[:, cols] = (u * cdf).astype(bf16)
            gp_ref[:, cols] = (cdf + u * (gauss * 0.3989422804014327)).astype(bf16)
        if nz:
            pl.when(s == att + 3)(gather.rest)


def constant(shape):
    return pl.BlockSpec(shape, lambda s: (0,) * len(shape), pipeline_mode=pl.Buffered(1))


def front(x, row_codes, col_codes, table, weights, chips=0):
    tokens = x.shape[0]
    rows = tokens // SEQ
    assert rows == 4
    att = GROUPS * rows
    nz = chips // 4

    def code_at(s):
        return (jnp.where(s < att, s % rows, rows - 1), 0, 0)

    def head_at(s):
        return (jnp.where(s < att, s % rows, rows - 1), jnp.minimum(s // rows, GROUPS - 1))

    def tile_at(s):
        return (jnp.maximum(s - att, 0), 0)

    anywhere = pl.BlockSpec(memory_space=pl.ANY)
    narrow = pl.BlockSpec((SEQ, D), tile_at)
    head = pl.BlockSpec((SEQ, WIDE), head_at)
    wide = pl.BlockSpec((SEQ, FF), tile_at)
    in_specs = [
        constant((tokens, D)),
        pl.BlockSpec((1, 8, SEQ), code_at),
        pl.BlockSpec((1, SEQ, BAND), code_at),
        constant((TABLE, CHUNK)),
    ]
    out_specs = [
        head, head, head,
        pl.BlockSpec((1, 8, PACK * BAND), lambda s: (jnp.minimum(s, att - 1), 0, 0)),
        narrow, narrow, narrow, wide, wide,
    ]
    low = jax.ShapeDtypeStruct((tokens, D), bf16)
    out_shape = [
        low, low, low,
        jax.ShapeDtypeStruct((att, 8, PACK * BAND), f32),
        low,
        jax.ShapeDtypeStruct((tokens, D), f32),
        low,
        jax.ShapeDtypeStruct((tokens, FF), bf16),
        jax.ShapeDtypeStruct((tokens, FF), bf16),
    ]
    if nz:
        step = CHUNK // chips
        in_specs += [constant(w.shape) for w in weights]
        out_specs += [anywhere, anywhere, pl.BlockSpec((TABLE, CHUNK), lambda s: (0, 0))]
        out_shape += [
            jax.ShapeDtypeStruct((8, chips, step, CHUNK), bf16),
            jax.ShapeDtypeStruct((chips, 4, step, CHUNK), bf16),
            jax.ShapeDtypeStruct((TABLE, CHUNK), f32),
        ]
        dma = pltpu.SemaphoreType.DMA
        scratch = [
            pltpu.VMEM((tokens, D), bf16),
            pltpu.VMEM((CHUNKS, chips, step, CHUNK), bf16),
            pltpu.VMEM((CHUNKS, step, HALF), bf16),
            *(pltpu.VMEM(w.shape, f32) for w in weights),
            pltpu.VMEM((2, TABLE, CHUNK), bf16),
            pltpu.VMEM((nz + 3, TABLE, CHUNK), bf16),
            dma((2, CHUNKS, nz - 1)), dma((2, CHUNKS, 4)), dma((CHUNKS,)), dma((CHUNKS,)),
            dma((2, 5)), dma((2, nz + 3)),
        ]
        params = pltpu.CompilerParams(
            vmem_limit_bytes=VMEM, collective_id=0, has_side_effects=True
        )
    else:
        in_specs.append(anywhere)
        scratch = [
            pltpu.VMEM((tokens, D), bf16),
            pltpu.VMEM(weights[0].shape, bf16),
            pltpu.SemaphoreType.DMA,
        ]
        params = pltpu.CompilerParams(vmem_limit_bytes=VMEM)
    return pl.pallas_call(
        partial(front_kernel, nz),
        grid=(att + rows,),
        in_specs=in_specs,
        out_specs=out_specs,
        out_shape=out_shape,
        scratch_shapes=scratch,
        compiler_params=params,
        name="front",
    )(x, row_codes, col_codes, table, *weights)


def middle_kernel(
    y1_ref, g_ref, gp_ref, cot_ref, vec_ref, wo_ref, w1_ref, w2_ref,
    out_ref, df_ref, du_ref, dy1_ref, da_ref, dc_ref, grads_ref, sums_ref, ups_ref,
):
    s = pl.program_id(0)

    @pl.when(s == 0)
    def _():
        sums_ref[...] = jnp.zeros_like(sums_ref)
        ups_ref[...] = jnp.zeros_like(ups_ref)

    gain1 = vec_ref[G1 : G1 + 1, :]
    gain2 = vec_ref[G2 : G2 + 1, :]
    part = y1_ref.shape[0] // 2
    kept = [{}, {}]

    def down(h):
        rows = slice(h * part, (h + 1) * part)
        kept[h]["f"] = nn(g_ref[rows, :], w2_ref[...])

    def norm_two(h):
        rows = slice(h * part, (h + 1) * part)
        z1, r1 = norm_stats(y1_ref[rows, :])
        n1 = z1 * gain1 + vec_ref[C1 : C1 + 1, :]
        y2 = n1 + (kept[h]["f"] + vec_ref[B2 : B2 + 1, :])
        z2, r2 = norm_stats(y2)
        out_ref[rows, :] = (z2 * gain2 + vec_ref[C2 : C2 + 1, :]).astype(bf16)
        e = cot_ref[rows, :].astype(f32)
        sums_ref[0] += fold_rows(e * z2)
        sums_ref[1] += fold_rows(e)
        dy2 = norm_back(e * gain2, z2, r2)
        df = dy2.astype(bf16)
        df_ref[rows, :] = df
        sums_ref[2] += fold_rows(df.astype(f32))
        kept[h].update(dy2=dy2, df=df)

    def up_grad(h):
        rows = slice(h * part, (h + 1) * part)
        for f in range(4):
            cols = slice(f * CHUNK, (f + 1) * CHUNK)
            dg = nt(kept[h]["df"], w2_ref[cols, :])
            du = (dg * gp_ref[rows, cols].astype(f32)).astype(bf16)
            du_ref[rows, cols] = du
            ups_ref[:, cols] += fold_rows(du.astype(f32))

    def up_back(h):
        rows = slice(h * part, (h + 1) * part)
        dn1 = kept[h]["dy2"]
        for f in range(4):
            dn1 = dn1 + nt(du_ref[rows, f * CHUNK : (f + 1) * CHUNK], w1_ref[f])
        kept[h]["dn1"] = dn1

    def norm_one(h):
        rows = slice(h * part, (h + 1) * part)
        z1, r1 = norm_stats(y1_ref[rows, :])
        dn1 = kept[h]["dn1"]
        sums_ref[3] += fold_rows(dn1 * z1)
        sums_ref[4] += fold_rows(dn1)
        dy1 = norm_back(dn1 * gain1, z1, r1)
        dy1_ref[rows, :] = dy1
        da = dy1.astype(bf16)
        da_ref[rows, :] = da
        sums_ref[5] += fold_rows(da.astype(f32))
        dc_ref[rows, :] = nt(da, wo_ref[0]).astype(bf16)

    for stage in (down, norm_two, up_grad, up_back, norm_one):
        for h in range(2):
            stage(h)

    @pl.when(s == pl.num_programs(0) - 1)
    def _():
        grads_ref[...] = jnp.zeros_like(grads_ref)
        for i, row in enumerate((G2, C2, B2, G1, C1, BO)):
            grads_ref[row : row + 1, :] = jnp.sum(sums_ref[i], axis=0, keepdims=True)
        for f in range(4):
            cols = slice(f * CHUNK, (f + 1) * CHUNK)
            grads_ref[B1 + f : B1 + f + 1, :] = jnp.sum(ups_ref[:, cols], axis=0, keepdims=True)


def chunks_at(count, index):
    return pl.BlockSpec(
        (count, CHUNK, CHUNK), lambda s: (index, 0, 0), pipeline_mode=pl.Buffered(1)
    )


def middle(y1, g, gp, cot, table, wa, w2):
    tokens = y1.shape[0]
    tile = SEQ

    narrow = pl.BlockSpec((tile, D), lambda s: (s, 0))
    wide = pl.BlockSpec((tile, FF), lambda s: (s, 0))
    wide_out = pl.BlockSpec((tile, FF), lambda s: (s, 0))
    return pl.pallas_call(
        middle_kernel,
        grid=(tokens // tile,),
        in_specs=[
            narrow, wide, wide, narrow, constant((TABLE, CHUNK)),
            chunks_at(1, 3), chunks_at(4, 1), constant((FF, D)),
        ],
        out_specs=[
            narrow, narrow, wide_out, narrow, narrow, narrow,
            pl.BlockSpec((TABLE, CHUNK), lambda s: (0, 0)),
        ],
        out_shape=[
            jax.ShapeDtypeStruct((tokens, D), bf16),
            jax.ShapeDtypeStruct((tokens, D), bf16),
            jax.ShapeDtypeStruct((tokens, FF), bf16),
            jax.ShapeDtypeStruct((tokens, D), f32),
            jax.ShapeDtypeStruct((tokens, D), bf16),
            jax.ShapeDtypeStruct((tokens, D), bf16),
            jax.ShapeDtypeStruct((TABLE, CHUNK), f32),
        ],
        scratch_shapes=[pltpu.VMEM((6, 8, D), f32), pltpu.VMEM((8, FF), f32)],
        compiler_params=pltpu.CompilerParams(vmem_limit_bytes=VMEM),
        name="middle",
    )(y1, g, gp, cot, table, wa, wa, w2)


UP, PROJ, DOWN, QKV = 0, 4, 5, 9
OUTERS = 9


class Reduce:
    def __init__(self, nz, grads, made, local, bufs, fin, outs, sems):
        self.at = Place(nz)
        self.nz, self.grads, self.made, self.local = nz, grads, made, local
        self.bufs, self.fin, self.outs = bufs, fin, outs
        self.c_sem, self.l_sem, self.q_sem, self.z_sem, self.f_sem = sems

    TURNS = (-1, 0, 3, 5, 7, 8)

    def pump(self, s):
        for j in (5, 4, 3, 2, 1, 0):
            turn = s - 4 - self.TURNS[j]
            r = (2 * turn + 1) // 3
            due = (turn >= 0) & (turn % 3 != 2) & (r < QKV)
            pl.when(due)(partial(self.act, j, r))

        @pl.when(s >= 15)
        def _():
            for hg, turns in ((0, (15, 16, 19, 21, 23, 24)), (1, (17, 18, 21, 22, 23, 24))):
                for j in (5, 4, 3, 2, 1, 0):
                    pl.when(s == turns[j])(partial(self.act, j, QKV + hg))

    def source(self, r, lanes, fn):
        g2, g19 = self.grads
        if isinstance(r, int):
            fn(self.made.at[r - QKV, :, :, :, lanes])
            return
        pl.when(r >= DOWN)(lambda: fn(g2.at[:, :, r - DOWN, :, lanes]))
        pl.when(r < DOWN)(lambda: fn(g19.at[r, :, :, :, lanes]))

    def act(self, j, r):
        at, nz = self.at, self.nz
        r0, r1, r2, r3 = self.bufs
        fin, got = self.fin
        c, x, y, z = at.c, at.x, at.y, at.z
        half = [pl.ds(pl.multiple_of(i * HALF, HALF), HALF) for i in (c, 1 - c)]

        def c_copy(src):
            return remote(src, r0.at[r], self.c_sem.at[0, r], self.c_sem.at[1, r], at.other)

        def l_copy(src):
            return pltpu.make_async_copy(src, self.local.at[r % 2], self.l_sem.at[r % 2])

        def a_copy(i):
            q = (1 - c) * (2 * i + 1 - x) + c * (2 * (1 - y) + i)
            return remote(
                r0.at[r, q], r1.at[r, i],
                self.q_sem.at[0, r, i], self.q_sem.at[1, r, i], at.first,
            )

        keep = (1 - c) * y + c * x

        def b_copy():
            return remote(
                r1.at[r, 1 - keep], r2.at[r],
                self.q_sem.at[0, r, 2], self.q_sem.at[1, r, 2], at.second,
            )

        def z_copy(i):
            return remote(
                r2.at[r, (z + i) % nz], r3.at[r, i - 1],
                self.z_sem.at[0, r, i - 1], self.z_sem.at[1, r, i - 1], at.along_z(i),
            )

        def f_copy():
            return remote(fin.at[r], got.at[r], self.f_sem.at[0, r], self.f_sem.at[1, r], at.other)

        rows = fin.shape[1] // 2
        if j == 0:
            self.source(r, half[1], lambda src: c_copy(src).start())
            if not isinstance(r, int):
                self.source(r, half[0], lambda src: l_copy(src).start())
        elif j == 1:
            if isinstance(r, int):
                c_copy(self.made.at[r - QKV, :, :, :, half[1]]).wait()
                own = self.made.at[r - QKV]
                mine = jnp.where(c == 0, own[:, :, :, :HALF], own[:, :, :, HALF:])
            else:
                self.source(r, half[1], lambda src: c_copy(src).wait())
                self.source(r, half[0], lambda src: l_copy(src).wait())
                mine = self.local[r % 2]
            r0[r] = r0[r] + mine
            a_copy(0).start()
            a_copy(1).start()
        elif j == 2:
            for i in (0, 1):
                a_copy(i).wait()
                q = (1 - c) * (2 * i + x) + c * (2 * y + i)
                r1[r, i] = r1[r, i] + r0[r, q]
            b_copy().start()
        elif j == 3:
            b_copy().wait()
            r2[r] = r2[r] + r1[r, keep]
            for i in range(1, nz):
                z_copy(i).start()
        elif j == 4:
            total = r2[r, z].astype(f32)
            for i in range(1, nz):
                z_copy(i).wait()
                total = total + r3[r, i - 1].astype(f32)
            fin[r] = total
            f_copy().start()
        else:
            f_copy().wait()
            self.finish(r, rows)

    def finish(self, r, rows):
        c = self.at.c
        fin, got = self.fin
        out, out_down = self.outs
        even = c == 0

        def sides(own, other):
            return jnp.concatenate(
                [jnp.where(even, own, other), jnp.where(even, other, own)], axis=1
            )

        def down():
            @pl.when(c == (r - DOWN) // 2)
            def _():
                out_down[(r - DOWN) % 2] = sides(fin[r], got[r])

        def rest():
            own = jnp.where(even, fin[r, :rows, :], fin[r, rows:, :])
            other = jnp.where(even, got[r, :rows, :], got[r, rows:, :])
            out[r if not isinstance(r, int) else r - QKV + DOWN] = sides(own, other)

        if isinstance(r, int):
            rest()
        else:
            pl.when(r >= DOWN)(down)
            pl.when(r < DOWN)(rest)


def back_kernel(comm, nz, *refs):
    (
        x_hbm, row_ref, col_ref, wa_hbm, q_ref, k_ref, v_ref, dc_ref, lse_ref, dy1_ref, table_ref,
        g_hbm, df_hbm, n1_hbm, du_hbm, c_hbm, da_hbm,
        g2_hbm, g19_hbm, out, out_down, total_ref, dx_ref,
        x_ref, wqkv_ref, work, res, made, dk_sum, dv_sum, qv_sum, in_sem, res_sem,
    ) = refs[:33]
    s = pl.program_id(0)
    att = GROUPS * 4
    end = OUTERS + att
    if comm:
        local, r0, r1, r2, r3, fin, got, mine, came = refs[33:42]
        sems, v_sem = refs[42:47], refs[47]
        reduce = Reduce(
            nz, (g2_hbm, g19_hbm), made, local, (r0, r1, r2, r3), (fin, got), (out, out_down), sems
        )
        at = reduce.at

        pl.when(s == 0)(at.greet)
        pl.when(s == 3)(at.meet)

    def bring(src, dst, i):
        return pltpu.make_async_copy(src, dst, in_sem.at[i])

    def stream(i, fn):
        cols = pl.ds(pl.multiple_of(i % 4 * CHUNK, CHUNK), CHUNK)
        down = pl.ds(pl.multiple_of((i + 3) % 4 * CHUNK, CHUNK), CHUNK)
        slot = i % 2
        pl.when(i < PROJ)(lambda: fn(bring(du_hbm.at[:, cols], work.at[slot], slot)))
        pl.when(i == PROJ)(lambda: fn(bring(c_hbm, work.at[slot], slot)))
        pl.when(i >= DOWN)(lambda: fn(bring(g_hbm.at[:, down], work.at[slot], slot)))

    def store(i, fn):
        slot = i % 2
        pl.when(i >= DOWN)(
            lambda: fn(pltpu.make_async_copy(res.at[slot], g2_hbm.at[i - DOWN], res_sem.at[slot]))
        )
        pl.when(i < DOWN)(
            lambda: fn(pltpu.make_async_copy(res.at[slot], g19_hbm.at[i], res_sem.at[slot]))
        )

    whole_da = bring(da_hbm, work.at[2], 2)
    whole_n1, whole_df = bring(n1_hbm, work.at[3], 3), bring(df_hbm, work.at[3], 3)
    whole_x = bring(x_hbm, x_ref, 4)
    whole_w = bring(wa_hbm.at[0:GROUPS], wqkv_ref, 5)

    @pl.when(s == 0)
    def _():
        stream(s, lambda copy: copy.start())
        whole_n1.start()
        stream(s + 1, lambda copy: copy.start())
        whole_da.start()
        whole_n1.wait()
        qv_sum[...] = jnp.zeros_like(qv_sum)

    pl.when((s >= 2) & (s < OUTERS + 2))(lambda: store(s - 2, lambda copy: copy.wait()))
    if comm:
        reduce.pump(s)

    @pl.when(s < OUTERS)
    def _():
        stream(s, lambda copy: copy.wait())
        pl.when(s == PROJ)(lambda: whole_da.wait())
        pl.when(s == DOWN)(lambda: whole_df.wait())
        def put(product):
            res[s % 2] = product.astype(bf16).reshape(res.shape[1:])

        @pl.when(s < PROJ)
        def _():
            put(tn(work[3], work[s % 2]))

        @pl.when(s == PROJ)
        def _():
            put(tn(work[s % 2], work[2]))

        @pl.when(s >= DOWN)
        def _():
            put(tn(work[s % 2], work[3]))

        store(s, lambda copy: copy.start())
        pl.when(s < OUTERS - 2)(lambda: stream(s + 2, lambda copy: copy.start()))
        pl.when(s == PROJ - 1)(lambda: whole_df.start())

        @pl.when(s == 2)
        def _():
            whole_x.start()
            whole_w.start()

        @pl.when(s == OUTERS - 1)
        def _():
            whole_x.wait()
            whole_w.wait()

    @pl.when((s >= OUTERS) & (s < end))
    def _():
        hg = (s - OUTERS) // 4
        r = (s - OUTERS) % 4
        rows = pl.multiple_of(r * SEQ, SEQ)
        lanes = pl.ds(pl.multiple_of(hg * WIDE, WIDE), WIDE)
        kt = k_ref[...].T
        dk_sum[...] = jnp.zeros_like(dk_sum)
        dv_sum[...] = jnp.zeros_like(dv_sum)
        masks = head_masks()
        places = list(windows())

        def begin(b, first, width):
            block, span = slice(b * BAND, (b + 1) * BAND), slice(first, first + width)
            qc = spread_heads(q_ref[block, :], masks)
            dcc = spread_heads(dc_ref[block, :], masks)
            return qc, dcc, nt(k_ref[span, :], qc), nt(v_ref[span, :], dcc)

        ahead = begin(*places[0])
        for b, first, width in places:
            span = slice(first, first + width)
            qc, dcc, t, dp = ahead
            if b + 1 < len(places):
                ahead = begin(*places[b + 1])
            t = t * SCORE + mask_bias(col_ref.at[r], row_ref.at[r], b, first, width)
            p = jnp.exp2(t - lse_ref[0, b : b + 1, :])
            pdp = p * dp
            weighted = jnp.sum(pdp, axis=0, keepdims=True)
            ds = (pdp - p * weighted).astype(bf16)
            dv_sum[span, :] += nn(p.astype(bf16), dcc)
            dk_sum[span, :] += nn(ds, qc)
            dqt = nn(kt[:, span], ds)
            dq = (pick_heads(dqt).T * HEAD_DIM ** (-0.5)).astype(bf16)
            work[hg, pl.ds(rows + b * BAND, BAND), 0:WIDE] = dq
            qv_sum[0, :, lanes] += fold_rows(dq.astype(f32))
        dk = (dk_sum[...] * HEAD_DIM ** (-0.5)).astype(bf16)
        dv = dv_sum[...].astype(bf16)
        work[hg, pl.ds(rows, SEQ), WIDE : 2 * WIDE] = dk
        work[hg, pl.ds(rows, SEQ), 2 * WIDE :] = dv
        qv_sum[1, :, lanes] += fold_rows(dv.astype(f32))

        @pl.when(r == 3)
        def _():
            made[hg] = tn(x_ref[...], work[hg]).astype(bf16).reshape(made.shape[1:])

    last = QKV + GROUPS - 1
    if comm:
        def vec_copy(i, src, device):
            return remote(src, came.at[i], v_sem.at[0, i], v_sem.at[1, i], device)

        c_copy = vec_copy(0, mine.at[0], at.other)
        z_copies = [vec_copy(i, mine.at[1], at.along_z(i)) for i in range(1, nz)]
        near = [
            vec_copy(nz + i, mine.at[2], device)
            for i, device in enumerate((at.first, at.second, at.far))
        ]

        @pl.when(s == end - 1)
        def _():
            reduce.act(0, last)
            mine[0] = table_ref[...]
            mine[0, BQ : BQ + 1, :] = jnp.sum(qv_sum[0], axis=0, keepdims=True)
            mine[0, BV : BV + 1, :] = jnp.sum(qv_sum[1], axis=0, keepdims=True)
            c_copy.start()

        @pl.when(s == end)
        def _():
            reduce.act(1, last)
            c_copy.wait()
            mine[1] = mine[0] + came[0]
            for copy in z_copies:
                copy.start()

        @pl.when(s == end + 1)
        def _():
            reduce.act(3, last)
            total = mine[1]
            for i in range(1, nz):
                z_copies[i - 1].wait()
                total = total + came[i]
            mine[2] = total
            for copy in near:
                copy.start()

    @pl.when(s >= end)
    def _():
        half = SEQ // 2
        for h in range(2):
            if h == 1 and comm:
                pl.when(s == end)(lambda: reduce.act(2, last))
                pl.when(s == end + 1)(lambda: reduce.act(4, last))
            rows = pl.ds(pl.multiple_of((s - end) * SEQ + h * half, half), half)
            total = dy1_ref[h * half : (h + 1) * half, :]
            for hg in range(GROUPS):
                total = total + nt(work[hg, rows, :], wqkv_ref[hg].reshape(CHUNK, CHUNK))
            dx_ref[h * half : (h + 1) * half, :] = total

    @pl.when(s == end + 3)
    def _():
        if comm:
            for copy in near:
                copy.wait()
            total_ref[...] = mine[2] + came[nz] + came[nz + 1] + came[nz + 2]
            reduce.act(5, last)
        else:
            total_ref[...] = table_ref[...]
            total_ref[BQ : BQ + 1, :] = jnp.sum(qv_sum[0], axis=0, keepdims=True)
            total_ref[BV : BV + 1, :] = jnp.sum(qv_sum[1], axis=0, keepdims=True)
            out[...] = jnp.zeros_like(out)
            out_down[...] = jnp.zeros_like(out_down)


def back(x, row_codes, col_codes, wa, q, k, v, dc, lse, dy1, table, pairs, chips, comm):
    tokens = x.shape[0]
    rows = tokens // SEQ
    att = GROUPS * rows
    end = OUTERS + att
    assert rows == 4
    nz = chips // 4
    step = CHUNK // chips

    def turn(s):
        return jnp.clip(s - OUTERS, 0, att - 1)

    def head_at(s):
        return (turn(s) % rows, turn(s) // rows)

    def tile_at(s):
        return (jnp.maximum(s - end, 0), 0)

    anywhere = pl.BlockSpec(memory_space=pl.ANY)
    whole_table = pl.BlockSpec((TABLE, CHUNK), lambda s: (0, 0))
    head = pl.BlockSpec((SEQ, WIDE), head_at)
    tile = pl.BlockSpec((SEQ, D), tile_at)
    made_shape = (GROUPS, 4, nz, step, CHUNK)
    dma = pltpu.SemaphoreType.DMA
    scratch = [
        pltpu.VMEM((tokens, D), bf16),
        pltpu.VMEM((GROUPS, *wa.shape[1:]), bf16),
        pltpu.VMEM((4, tokens, CHUNK), bf16),
        pltpu.VMEM((2, 4, nz, step, CHUNK), bf16),
    ]
    if comm:
        scratch.append(pltpu.VMEM(made_shape, bf16))
    scratch += [
        pltpu.VMEM((SEQ, WIDE), f32),
        pltpu.VMEM((SEQ, WIDE), f32),
        pltpu.VMEM((2, 8, D), f32),
        dma((6,)), dma((2,)),
    ]
    out_specs = [
        anywhere, anywhere,
        pl.BlockSpec((8, step // 2, CHUNK), lambda s: (0, 0, 0)),
        pl.BlockSpec((2, step, CHUNK), lambda s: (0, 0, 0)),
        whole_table, tile,
    ]
    out_shape = [
        jax.ShapeDtypeStruct((4, nz, 4, step, CHUNK), bf16),
        jax.ShapeDtypeStruct((5, 4, nz, step, CHUNK), bf16),
        jax.ShapeDtypeStruct((8, step // 2, CHUNK), f32),
        jax.ShapeDtypeStruct((2, step, CHUNK), f32),
        jax.ShapeDtypeStruct((TABLE, CHUNK), f32),
        jax.ShapeDtypeStruct((tokens, D), f32),
    ]
    kernel = partial(back_kernel, comm, nz)
    if comm:
        scratch += [
            pltpu.VMEM((2, 4, nz, step, HALF), bf16),
            pltpu.VMEM((CHUNKS, 4, nz, step, HALF), bf16),
            pltpu.VMEM((CHUNKS, 2, nz, step, HALF), bf16),
            pltpu.VMEM((CHUNKS, nz, step, HALF), bf16),
            pltpu.VMEM((CHUNKS, nz - 1, step, HALF), bf16),
            pltpu.VMEM((CHUNKS, step, HALF), f32),
            pltpu.VMEM((CHUNKS, step, HALF), f32),
            pltpu.VMEM((3, TABLE, CHUNK), f32),
            pltpu.VMEM((nz + 3, TABLE, CHUNK), f32),
            dma((2, CHUNKS)), dma((2,)), dma((2, CHUNKS, 3)), dma((2, CHUNKS, nz - 1)),
            dma((2, CHUNKS)), dma((2, nz + 3)),
        ]
        params = pltpu.CompilerParams(
            vmem_limit_bytes=VMEM, collective_id=1, has_side_effects=True
        )
    else:
        def kernel(*refs):
            refs = list(refs)
            made = refs.pop(23)
            refs.insert(27, made)
            back_kernel(comm, nz, *refs)

        out_specs.append(pl.BlockSpec(made_shape, lambda s: (0,) * 5, pipeline_mode=pl.Buffered(1)))
        out_shape.append(jax.ShapeDtypeStruct(made_shape, bf16))
        params = pltpu.CompilerParams(vmem_limit_bytes=VMEM)
    return pl.pallas_call(
        kernel,
        grid=(end + rows,),
        in_specs=[
            anywhere,
            constant((rows, 8, SEQ)),
            constant((rows, SEQ, BAND)),
            anywhere,
            head, head, head, head,
            pl.BlockSpec((1, 8, PACK * BAND), lambda s: (turn(s), 0, 0)),
            tile, whole_table,
            *(anywhere for _ in pairs),
        ],
        out_specs=out_specs,
        out_shape=out_shape,
        scratch_shapes=scratch,
        compiler_params=params,
        name="back",
    )(x, row_codes, col_codes, wa, q, k, v, dc, lse, dy1, table, *pairs)


def update(grad, master, moment, average, tokens_all):
    mean_grad = grad / tokens_all
    moment_new = momentum_coef * moment + mean_grad
    step_size = -learn_rate * (mean_grad + momentum_coef * moment_new)
    master_new = master + step_size
    average_new = average_keep * average + (1.0 - average_keep) * master_new
    return (master_new, moment_new, average_new)


def update_steps(grad, master, moment, average, tokens_all):
    mean_grad = grad / tokens_all
    moment_new = momentum_coef * moment + mean_grad
    step_size = -learn_rate * (mean_grad + momentum_coef * moment_new)
    average_step = (1.0 - average_keep) * (master + step_size - average)
    return (step_size, moment_new, average_step)


def update_kernel(tokens_all, *refs):
    grad_ref, down_ref, dx_ref = refs[:3]
    states, outs, dx_out, kept, sem = refs[3:15], refs[15:31], *refs[31:34]
    parts = kept.shape[0]
    spans = [pl.ds(i * kept.shape[1], kept.shape[1]) for i in range(parts)]
    loads = [
        pltpu.make_async_copy(dx_ref.at[span], kept.at[i], sem.at[0, i])
        for i, span in enumerate(spans)
    ]
    saves = [
        pltpu.make_async_copy(kept.at[i], dx_out.at[span], sem.at[1, i])
        for i, span in enumerate(spans)
    ]
    for load in loads:
        load.start()

    def one(i, index, grad):
        master, moment, average = (states[i + 4 * j][index] for j in range(3))
        outs[i][index] = grad
        new = update(grad, master, moment, average, tokens_all)
        for j in range(3):
            outs[i + 4 * (j + 1)][index] = new[j]

    rows = grad_ref.shape[1]
    for i in range(parts):
        loads[i].wait()
        saves[i].start()
    for hg in range(GROUPS):
        for i in range(3):
            cols = slice(i * D + hg * WIDE, i * D + (hg + 1) * WIDE)
            one(0, (slice(None), cols), grad_ref[5 + hg, :, i * WIDE : (i + 1) * WIDE])
    one(1, (slice(None), slice(None)), grad_ref[4])
    for f in range(4):
        one(2, (slice(None), slice(f * CHUNK, (f + 1) * CHUNK)), grad_ref[f])
    for i in range(2):
        one(3, (slice(2 * rows * i, 2 * rows * (i + 1)), slice(None)), down_ref[i])
    for save in saves:
        save.wait()


def update_weights(grads, grads_down, dx, states, tokens_all):
    whole = pl.BlockSpec(memory_space=pltpu.VMEM)
    anywhere = pl.BlockSpec(memory_space=pl.ANY)
    shapes = [jax.ShapeDtypeStruct(w.shape, f32) for w in states[:4]]
    return pl.pallas_call(
        partial(update_kernel, tokens_all),
        in_specs=[whole] * 2 + [anywhere] + [whole] * 12,
        out_specs=[whole] * 16 + [anywhere],
        out_shape=shapes * 4 + [jax.ShapeDtypeStruct(dx.shape, f32)],
        scratch_shapes=[
            pltpu.VMEM((8, dx.shape[0] // 8, D), f32), pltpu.SemaphoreType.DMA((2, 8)),
        ],
        compiler_params=pltpu.CompilerParams(vmem_limit_bytes=VMEM),
        name="update",
    )(grads, grads_down, dx, *states)


def group_columns(w):
    n = w.shape[0]
    return w.reshape(n, 3, GROUPS, WIDE).transpose(2, 0, 1, 3).reshape(GROUPS, n, 3 * WIDE)


def ungroup_columns(w):
    n = w.shape[1]
    return w.reshape(GROUPS, n, 3, WIDE).transpose(1, 2, 0, 3).reshape(n, 3 * D)


def table_of(gains, biases):
    flat = jnp.concatenate([gains, biases, jnp.zeros((TABLE * CHUNK - 9216,), gains.dtype)])
    return flat.reshape(TABLE, CHUNK)


def on_device(
    tokens, segment_ids, pad_counts, out_cotangent,
    qkv_master, proj_master, up_master, down_master, gain_master, bias_master,
    qkv_moment, proj_moment, up_moment, down_moment, gain_moment, bias_moment,
    qkv_average, proj_average, up_average, down_average, gain_average, bias_average,
):
    axes = ("gx", "gy")
    devices = lax.axis_size(axes)
    seq_len = segment_ids.shape[1]
    tokens_all = tokens.shape[0] * devices
    position = jnp.arange(seq_len, dtype=jnp.int32)
    is_pad = position[None, :] >= (seq_len - pad_counts)[:, None]
    codes = segment_ids * 2 + is_pad.astype(jnp.int32)
    row_codes = jnp.broadcast_to(codes[:, None, :], (codes.shape[0], 8, seq_len))
    col_codes = jnp.broadcast_to(codes[:, :, None], (codes.shape[0], seq_len, BAND))
    gain_len, bias_len = gain_master.shape[0], bias_master.shape[0]
    gains = gain_len * devices
    place = lax.axis_index(axes)

    fine = lax.axis_size("gx") == 4 and lax.axis_size("gy") == 8
    if fine:
        chips = devices // 2
        part = jnp.zeros((TABLE * CHUNK,), bf16)
        part = lax.dynamic_update_slice(part, gain_master.astype(bf16), (place * gain_len,))
        part = lax.dynamic_update_slice(
            part, bias_master.astype(bf16), (gains + place * bias_len,)
        ).reshape(TABLE, CHUNK)
        q, k, v, lse, c, y1, n1, g, gp, wa, w2, table = front(
            tokens, row_codes, col_codes, part,
            (qkv_master, proj_master, up_master, down_master), chips,
        )
        w2 = w2.reshape(FF, D)
    else:
        gather = partial(lax.all_gather, axis_name=axes, axis=0, tiled=True)
        w1 = gather(up_master.astype(bf16))
        wa = jnp.concatenate(
            [
                group_columns(gather(qkv_master.astype(bf16))),
                gather(proj_master.astype(bf16))[None],
                w1.reshape(D, 4, CHUNK).transpose(1, 0, 2),
            ]
        ).reshape(8, 16, CHUNK // 16, CHUNK)
        w2 = gather(down_master.astype(bf16))
        table = table_of(
            gather(gain_master.astype(bf16)), gather(bias_master.astype(bf16))
        ).astype(f32)
        q, k, v, lse, c, y1, n1, g, gp = front(
            tokens, row_codes, col_codes, table, (wa,)
        )
    layer_output, df, du, dy1, da, dc, terms = middle(
        y1, g, gp, out_cotangent, table, wa.reshape(8, CHUNK, CHUNK), w2
    )
    results = back(
        tokens, row_codes, col_codes, wa, q, k, v, dc, lse, dy1, terms,
        (g, df, n1, du, c, da), chips if fine else 16, fine,
    )
    input_grad = results[5]
    scatter = partial(lax.psum_scatter, axis_name=axes, scatter_dimension=0, tiled=True)
    states = (
        qkv_master, proj_master, up_master, down_master,
        qkv_moment, proj_moment, up_moment, down_moment,
        qkv_average, proj_average, up_average, down_average,
    )
    if fine:
        grads, grads_down, terms = results[2:5]
        new = update_weights(grads, grads_down, input_grad, states, tokens_all)
        shares, masters, moments, averages = new[:4], new[4:8], new[8:12], new[12:16]
        input_grad = new[16]
        terms = terms.reshape(-1)
        gain_share = lax.dynamic_slice(terms, (place * gain_len,), (gain_len,))
        bias_share = lax.dynamic_slice(terms, (gains + place * bias_len,), (bias_len,))
    else:
        down_part, rest, terms, dwqkv = (results[i].astype(f32) for i in (0, 1, 4, 6))
        rest = rest.reshape(5, CHUNK, CHUNK)
        terms = terms.reshape(-1)
        shares = (
            scatter(ungroup_columns(dwqkv.reshape(GROUPS, CHUNK, CHUNK))),
            scatter(rest[4]),
            scatter(rest[:4].transpose(1, 0, 2).reshape(D, FF)),
            scatter(down_part.reshape(FF, D)),
        )
        news = [
            update(shares[i], states[i], states[4 + i], states[8 + i], tokens_all)
            for i in range(4)
        ]
        masters, moments, averages = zip(*news)
        gain_share = scatter(terms[:gains])
        bias_share = scatter(terms[gains : gains + bias_len * devices])
    gain_new = update_steps(gain_share, gain_master, gain_moment, gain_average, tokens_all)
    bias_new = update(bias_share, bias_master, bias_moment, bias_average, tokens_all)
    return (
        layer_output, input_grad, *shares, gain_share, bias_share,
        *masters, gain_new[0], bias_new[0],
        *moments, gain_new[1], bias_new[1],
        *averages, gain_new[2], bias_new[2],
    )


def solution(mesh):
    both = ("gx", "gy")
    two, one = P(both, None), P(both)
    weights = (two, two, two, two, one, one)
    in_specs = (two, two, one, two) + weights * 3
    out_specs = (two, two) + weights * 4
    return jax.shard_map(
        on_device, mesh=mesh, in_specs=in_specs, out_specs=out_specs, check_vma=False
    )
```
